32 devices in a mesh: wide: 8 (over z, y), narrow: 4 (over x, core).
Axes of the slice: x: 2, y: 2, z: 4, core: 2. Of those that a mesh axis runs over, the one named last changes fastest.
Arguments:
- object_field: float32 [2, 2048, 4096], P(None, 'narrow', 'wide')
- probe: float32 [4, 2, 256, 256], replicated, may hold values from -3 to 3
- patterns: float32 [4, 8, 6, 256, 256], P('narrow', 'wide'), may hold values from 0.1 to 4
- offsets: int32 [4, 8, 6, 2], P('narrow', 'wide'), may hold values from -128 to 384
- counts: int32 [4, 8], P('narrow', 'wide'), may hold values from 1 to 6
Outputs:
- object_new: float32 [2, 2048, 4096], P(None, 'narrow', 'wide')
- probe_new: float32 [4, 2, 256, 256], replicated
The draws below stay inside these ranges and needn't reach their ends.
Inputs may be any that keep to these rules, and one draw needn't show every extreme that they name: A patch of 256 x 256 pixels at these offsets stays within the tile extended by 128 pixels on each side. `counts`: slots 0 to count - 1 of a tile are live, the others are ignored.
All inputs are finite; a program needn't handle non-finite values.
Results may differ from the reference program's by a relative error of at most 0.0003.
Values sent between devices are 32-bit elements; how exact they have to be, the bound alone decides.
No kernel may reach another device: no remote copies, remote signals or barrier semaphores. Data moves between devices by JAX's collectives and lax.ppermute only.
A program may use at most 128 MiB of HBM per device.

```python
import math
import jax
import jax.numpy as jnp
from jax import lax

R = 256
MODES = 4
TILE = 512
H = 128
BATCHES = 3
POS = 2
SLOTS = 6
NX = 2048
NY = 4096
N_WIDE = 8
N_NARROW = 4


def draw_object_field(key, part):
    columns = jnp.arange(NY, dtype=jnp.float32)
    ramp = 0.5 * (1.0 + 2.0 * columns / NY)
    values = jax.random.normal(key, (2, NX, NY), jnp.float32)
    return values * ramp[None, None, :]


def with_ends(entries, stream_key, smallest, high):
    extent = entries.shape
    index_at = [jax.random.randint(jax.random.fold_in(stream_key, axis), (), 0, extent[axis]) for axis in range(len(extent))]
    entries = entries.at[tuple(index_at)].set(smallest)
    longest = extent.index(max(extent))
    index_at[longest] = (index_at[longest] + 1) % extent[longest]
    return entries.at[tuple(index_at)].set(high)


def shard_levels(key, shape, pieces, smallest, high):
    gain, own = 1.0, jax.random.fold_in(key, 6)
    for dim, parts in pieces:
        draws = jnp.exp(jax.random.uniform(jax.random.fold_in(own, dim), (parts,), jnp.float32, smallest / len(pieces), high / len(pieces)))
        gain = gain * jnp.repeat(draws, shape[dim] // parts).reshape([-1 if axis == dim else 1 for axis in range(len(shape))])
    return gain


def bell_draw(stream_key, dims, width, reach, kind=jnp.bfloat16):
    array = width * jax.random.normal(stream_key, dims, jnp.float32)
    return jnp.clip(array, min=-reach, max=reach).astype(kind)


def setup_inputs(seed: int = 0) -> dict:
    seeds = jax.random.split(jax.random.key(seed), 6)
    object_field = draw_object_field(jax.random.fold_in(seeds[5], 71), 0)
    probe = bell_draw(seeds[1], (MODES, 2, R, R), 0.5, 3.0, jnp.float32)
    patterns = jnp.clip(jnp.exp(math.log(4.0) - 3.6888794 * jax.random.uniform(seeds[2], (N_NARROW, N_WIDE, SLOTS, R, R), jnp.float32) ** shard_levels(seeds[2], (N_NARROW, N_WIDE, SLOTS, R, R), ((0, 4), (1, 8)), -0.2, 0.2)), 0.1, 4.0)
    offsets = with_ends(jax.random.randint(seeds[3], (N_NARROW, N_WIDE, SLOTS, 2), 0 - H, TILE + H - R + 1), jax.random.fold_in(seeds[3], 1), 0 - H, TILE + H - R).astype(jnp.int32)
    counts = with_ends(jax.random.randint(seeds[4], (N_NARROW, N_WIDE), 1, SLOTS + 1), jax.random.fold_in(seeds[4], 1), 1, SLOTS).astype(jnp.int32)
    return dict(object_field=object_field, probe=probe, patterns=patterns, offsets=offsets, counts=counts)


def slot_terms(patch, probe, measured):
    probe_re = probe[:, 0]
    probe_im = probe[:, 1]
    obj_re = patch[0]
    obj_im = patch[1]
    psi = probe_re * obj_re - probe_im * obj_im + 1j * (probe_re * obj_im + probe_im * obj_re)
    far = jnp.fft.fft2(psi, norm='ortho')
    intensity = lax.optimization_barrier(jnp.sum(jnp.real(far) ** 2 + jnp.imag(far) ** 2, axis=0))
    ratio = jnp.sqrt(measured) / jnp.sqrt(intensity + 0.1)
    back = jnp.fft.ifft2(far * (1.0 - ratio), norm='ortho')
    back_re = jnp.real(back)
    back_im = jnp.imag(back)
    grad_re = lax.optimization_barrier(jnp.sum(probe_re * back_re + probe_im * back_im, axis=0))
    grad_im = lax.optimization_barrier(jnp.sum(probe_re * back_im - probe_im * back_re, axis=0))
    pgrad_re = obj_re * back_re + obj_im * back_im
    pgrad_im = obj_re * back_im - obj_im * back_re
    square = jnp.sum(obj_re * obj_re + obj_im * obj_im)
    return (jnp.stack([grad_re, grad_im]), jnp.stack([pgrad_re, pgrad_im], axis=1), square)

def reference(object_field, probe, patterns, offsets, counts):
    padded = jnp.pad(object_field, ((0, 0), (H, H), (H, H)))
    gradient = jnp.zeros_like(padded)
    flat_patterns = patterns.reshape(N_NARROW * N_WIDE, SLOTS, R, R)
    flat_offsets = offsets.reshape(N_NARROW * N_WIDE, SLOTS, 2)
    flat_counts = counts.reshape(N_NARROW * N_WIDE)
    devices_at = jnp.arange(N_NARROW * N_WIDE, dtype=jnp.int32)
    for minibatch in range(BATCHES):

        def visit(carry, inputs):
            gradient, probe_grad, coverage = carry
            measured_all, offs_all, count_here, device = inputs
            tile_row = device // N_WIDE * TILE
            tile_col = device % N_WIDE * TILE
            for position in range(POS):
                slot_at = minibatch * POS + position
                live = (slot_at < count_here).astype(jnp.float32)
                row_at = (tile_row + offs_all[slot_at, 0] + H).astype(jnp.int32)
                col_at = (tile_col + offs_all[slot_at, 1] + H).astype(jnp.int32)
                zero_at = jnp.zeros((), jnp.int32)
                patch = lax.dynamic_slice(padded, (zero_at, row_at, col_at), (2, R, R))
                obj_grad, pgrad, square = slot_terms(patch, probe, measured_all[slot_at])
                old = lax.dynamic_slice(gradient, (zero_at, row_at, col_at), (2, R, R))
                gradient = lax.dynamic_update_slice(gradient, old + live * obj_grad, (zero_at, row_at, col_at))
                probe_grad = probe_grad + live * pgrad
                coverage = coverage + live * square
            return ((gradient, probe_grad, coverage), None)
        start = (gradient, jnp.zeros_like(probe), jnp.zeros((), jnp.float32))
        (gradient, probe_grad, coverage), _ = lax.scan(visit, start, (flat_patterns, flat_offsets, flat_counts, devices_at))
        probe = probe - probe_grad / (coverage / (R * R))
    power = lax.optimization_barrier(jnp.sum(probe[:, 0] ** 2 + probe[:, 1] ** 2, axis=0))
    top = jnp.max(power)
    core = gradient[:, H:H + NX, H:H + NY]
    return (object_field - 0.5 * core / top, probe)
```

```python
import functools

import jax
import jax.numpy as jnp
import ml_dtypes
import numpy as np
from jax import lax
from jax.experimental import pallas as pl
from jax.experimental.pallas import tpu as pltpu
from jax.sharding import PartitionSpec as P

H = 128
BATCHES = 3
POS = 2
AXES = ("wide", "narrow")
F32 = jnp.float32
BF16 = jnp.bfloat16
VMEM_LIMIT = 48 * 1024 * 1024


def halves(table):
    high = table.astype(ml_dtypes.bfloat16)
    low = (table - high.astype(np.float64)).astype(ml_dtypes.bfloat16)
    return np.stack([high, low])


def dft_tables(size):
    half = size // 2
    k = np.arange(half)
    out = []
    for odd in range(2):
        phase = ((2 * k[:, None] + odd) * k[None, :]) % size
        angle = -2.0 * np.pi * phase / size
        re, im = np.cos(angle) / np.sqrt(size), np.sin(angle) / np.sqrt(size)
        out.append(np.block([[re, -im], [im, re]]))
    return np.stack([halves(t) for t in (out[0], out[1], out[0].T, out[1].T)])


def split(x):
    high = x.astype(BF16)
    return high, (x - high.astype(F32)).astype(BF16)


def dot(a, b):
    return jnp.dot(a, b, preferred_element_type=F32)


def left(tables, which, x):
    high, low = split(x)
    t_high, t_low = tables[which, 0], tables[which, 1]
    return dot(t_high, high) + dot(t_high, low) + dot(t_low, high)


def right(x, tables, which):
    high, low = split(x)
    t_high, t_low = tables[which, 0], tables[which, 1]
    return dot(high, t_high) + dot(low, t_high) + dot(high, t_low)


def forward(tables, re, im):
    h = re.shape[0] // 2
    u = jnp.concatenate([re[:h] + re[h:], im[:h] + im[h:]], 0)
    v = jnp.concatenate([re[:h] - re[h:], im[:h] - im[h:]], 0)
    even, odd = left(tables, 0, u), left(tables, 1, v)

    def columns(op):
        rows = [jnp.concatenate([op(y[:h, :h], y[:h, h:]), op(y[h:, :h], y[h:, h:])], 1) for y in (even, odd)]
        return jnp.concatenate(rows, 0)

    return (
        right(columns(lambda a, b: a + b), tables, 2),
        right(columns(lambda a, b: a - b), tables, 3),
    )


def inverse(tables, even, odd):
    h = even.shape[0] // 2
    a, b = right(even, tables, 0), right(odd, tables, 1)
    s, d = a + b, a - b

    def rows(lo):
        return jnp.concatenate(
            [
                jnp.concatenate([s[lo : lo + h, :h], d[lo : lo + h, :h]], 1),
                jnp.concatenate([s[lo : lo + h, h:], d[lo : lo + h, h:]], 1),
            ],
            0,
        )

    a, b = left(tables, 2, rows(0)), left(tables, 3, rows(h))
    s, d = a + b, a - b
    return jnp.concatenate([s[:h], d[:h]], 0), jnp.concatenate([s[h:], d[h:]], 0)


def spectrum_of(tables, patch, probe, mode):
    size = patch.shape[-1]
    base = mode * 2 * size
    p_re, p_im = probe[base : base + size], probe[base + size : base + 2 * size]
    o_re, o_im = patch[0, 0], patch[0, 1]
    return forward(tables, p_re * o_re - p_im * o_im, p_re * o_im + p_im * o_re)


def power_of(z):
    h = z.shape[-1] // 2
    return z[:, :h] * z[:, :h] + z[:, h:] * z[:, h:]


def gradients(tables, patch, probe, mode, even, odd, keep, pgrad, gpatch):
    size = patch.shape[-1]
    base = mode * 2 * size
    k_even, k_odd = keep[0, 0], keep[0, 1]
    b_re, b_im = inverse(
        tables,
        even * jnp.concatenate([k_even, k_even], 1),
        odd * jnp.concatenate([k_odd, k_odd], 1),
    )
    p_re, p_im = probe[base : base + size], probe[base + size : base + 2 * size]
    o_re, o_im = patch[0, 0], patch[0, 1]
    gpatch[0, 0] += p_re * b_re + p_im * b_im
    gpatch[0, 1] += p_re * b_im - p_im * b_re
    pgrad[base : base + size] += o_re * b_re + o_im * b_im
    pgrad[base + size : base + 2 * size] += o_re * b_im - o_im * b_re


def whole(*shape):
    return pl.BlockSpec(shape, lambda i, *_: (0,) * len(shape))


def per_slot(*shape):
    return pl.BlockSpec((1, *shape), lambda i, *_: (i,) + (0,) * len(shape))


def per_batch_slot(batch, *shape):
    return pl.BlockSpec((1, *shape), lambda i, *_: (batch * POS + i,) + (0,) * len(shape))


def call(body, scalars, operands, in_specs, out_shapes, out_specs, grid, scratch=(), aliases=None, flops=0, moved=0):
    return pl.pallas_call(
        body,
        out_shape=[jax.ShapeDtypeStruct(s, F32) for s in out_shapes],
        grid_spec=pltpu.PrefetchScalarGridSpec(
            num_scalar_prefetch=len(scalars),
            grid=(grid,),
            in_specs=in_specs,
            out_specs=out_specs,
            scratch_shapes=list(scratch),
        ),
        input_output_aliases=aliases or {},
        compiler_params=pltpu.CompilerParams(vmem_limit_bytes=VMEM_LIMIT),
        cost_estimate=pl.CostEstimate(flops=flops, bytes_accessed=moved, transcendentals=0),
    )(*scalars, *operands)


def cut_patches(offsets, tile, sides, size, slots):
    edge = tile.shape[1]
    full = edge + 2 * H

    def body(offs, tile_ref, left_ref, right_ref, top_ref, bottom_ref, out, ext):
        i = pl.program_id(0)

        @pl.when(i == 0)
        def _():
            ext[:, :H] = top_ref[...]
            ext[:, H + edge :] = bottom_ref[...]
            ext[:, H : H + edge, :H] = left_ref[...]
            ext[:, H : H + edge, H : H + edge] = tile_ref[...]
            ext[:, H : H + edge, H + edge :] = right_ref[...]

        row = offs[2 * i] + H
        col = offs[2 * i + 1] + H
        row_at = pl.multiple_of(jnp.minimum(row // 8 * 8, full - size - 8), 8)
        col_at = pl.multiple_of(jnp.minimum(col // 128 * 128, full - size - 128), 128)
        for part in range(2):
            block = ext[part, pl.ds(row_at, size + 8), pl.ds(col_at, size + 128)]
            block = pltpu.roll(block, size + 128 - (col - col_at), 1)[:, :size]
            block = pltpu.roll(block, size + 8 - (row - row_at), 0)[:size]
            out[0, part] = block

    return call(
        body,
        [offsets],
        [tile, *sides],
        [whole(2, edge, edge), whole(2, edge, H), whole(2, edge, H), whole(2, H, full), whole(2, H, full)],
        [(slots, 2, size, size)],
        [per_slot(2, size, size)],
        slots,
        scratch=[pltpu.VMEM((2, full, full), F32)],
        flops=10**6,
        moved=8 * 10**6,
    )[0]


def place_gradients(offsets, counts, patches, gradient, batch, full):
    size = patches.shape[-1]
    first = gradient is None

    def body(offs, counts_ref, patch_ref, *rest):
        out = rest[-1]
        i = pl.program_id(0)

        @pl.when(i == 0)
        def _():
            out[...] = jnp.zeros_like(out) if first else rest[0][...]

        slot = batch * POS + i

        @pl.when(slot < counts_ref[0])
        def _():
            row = offs[2 * slot] + H
            col = offs[2 * slot + 1] + H
            row_at = pl.multiple_of(jnp.minimum(row // 8 * 8, full - size - 8), 8)
            col_at = pl.multiple_of(jnp.minimum(col // 128 * 128, full - size - 128), 128)
            for part in range(2):
                block = patch_ref[0, part]
                block = jnp.concatenate([block, jnp.zeros((8, size), F32)], 0)
                block = pltpu.roll(block, row - row_at, 0)
                block = jnp.concatenate([block, jnp.zeros((size + 8, 128), F32)], 1)
                block = pltpu.roll(block, col - col_at, 1)
                out[part, pl.ds(row_at, size + 8), pl.ds(col_at, size + 128)] += block

    operands, specs = [patches], [per_slot(2, size, size)]
    if not first:
        operands, specs = [*operands, gradient], [*specs, whole(2, full, full)]
    return call(
        body,
        [offsets, counts],
        operands,
        specs,
        [(2, full, full)],
        [whole(2, full, full)],
        POS,
        flops=10**6,
        moved=10**7,
    )[0]


def merge_borders(gradient, from_right, from_left, from_below, from_above, edge):
    full = edge + 2 * H

    def body(g, fr, fl, fb, fa, out):
        out[...] = g[:, H : H + edge, H : H + edge]
        out[:, :, edge - H :] += fr[:, H : H + edge]
        out[:, :, :H] += fl[:, H : H + edge]
        out[:, edge - H :] += fb[...]
        out[:, :H] += fa[...]

    return call(
        body,
        [],
        [gradient, from_right, from_left, from_below, from_above],
        [whole(2, full, full), whole(2, full, H), whole(2, full, H), whole(2, H, edge), whole(2, H, edge)],
        [(2, edge, edge)],
        [whole(2, edge, edge)],
        1,
        flops=10**6,
        moved=10**7,
    )[0]


def forward_kernel(tables, counts, patches, probe, batch):
    size = patches.shape[-1]
    h = size // 2
    modes = probe.shape[0] // (2 * size)

    def body(counts_ref, t, patch, p, z, inten):
        @pl.when(batch * POS + pl.program_id(0) < counts_ref[0])
        def _():
            for m in range(modes):
                even, odd = spectrum_of(t, patch, p, m)
                z[0, m, 0] = even
                z[0, m, 1] = odd
                if m == 0:
                    inten[0, 0] = power_of(even)
                    inten[0, 1] = power_of(odd)
                else:
                    inten[0, 0] += power_of(even)
                    inten[0, 1] += power_of(odd)

    return call(
        body,
        [counts],
        [tables, patches, probe],
        [whole(*tables.shape), per_batch_slot(batch, 2, size, size), whole(*probe.shape)],
        [(POS, modes, 2, size, size), (POS, 2, size, h)],
        [per_slot(modes, 2, size, size), per_slot(2, size, h)],
        POS,
        flops=POS * modes * 24 * size**3,
        moved=4 * 10**6,
    )


def turn_kernel(tables, counts, patches, probe, roots, intensities, batch):
    size = patches.shape[-1]
    h = size // 2
    rows = probe.shape[0]
    modes = rows // (2 * size)
    n = len(intensities)

    def body(counts_ref, t, patch, p, root, *rest):
        parts, (sent, keep, gpatch, z) = rest[:n], rest[n:]
        i = pl.program_id(0)

        @pl.when(i == 0)
        def _():
            sent[...] = jnp.zeros_like(sent)

        gpatch[...] = jnp.zeros_like(gpatch)

        @pl.when(batch * POS + i < counts_ref[0])
        def _():
            for m in range(modes):
                even, odd = spectrum_of(t, patch, p, m)
                z[m, 0] = even
                z[m, 1] = odd
            for e in range(2):
                total = parts[0][0, e]
                for part in parts[1:]:
                    total = total + part[0, e]
                for m in range(modes):
                    total = total + power_of(z[m, e])
                keep[0, e] = 1.0 - root[0, e] * lax.rsqrt(total + 0.1)
            for m in range(modes):
                gradients(t, patch, p, m, z[m, 0], z[m, 1], keep, sent, gpatch)
            o_re, o_im = patch[0, 0], patch[0, 1]
            square = (o_re * o_re + o_im * o_im).reshape(size // 8, 8, size)
            sent[rows:] += jnp.sum(square, axis=0)

    return call(
        body,
        [counts],
        [tables, patches, probe, roots, *intensities],
        [
            whole(*tables.shape),
            per_batch_slot(batch, 2, size, size),
            whole(*probe.shape),
            per_batch_slot(batch, 2, size, h),
        ]
        + [per_slot(2, size, h)] * n,
        [(rows + 8, size), (POS, 2, size, h), (POS, 2, size, size)],
        [whole(rows + 8, size), per_slot(2, size, h), per_slot(2, size, size)],
        POS,
        scratch=[pltpu.VMEM((modes, 2, size, size), F32)],
        flops=POS * modes * 48 * size**3,
        moved=8 * 10**6,
    )


def gradient_kernel(tables, counts, patches, probe, spectra, keep, gpatch, batch):
    size = patches.shape[-1]
    h = size // 2
    modes = probe.shape[0] // (2 * size)

    def body(counts_ref, t, patch, p, z, k, g_in, pgrad, g_out):
        i = pl.program_id(0)

        @pl.when(i == 0)
        def _():
            pgrad[...] = jnp.zeros_like(pgrad)

        g_out[...] = g_in[...]

        @pl.when(batch * POS + i < counts_ref[0])
        def _():
            for m in range(modes):
                gradients(t, patch, p, m, z[0, m, 0], z[0, m, 1], k, pgrad, g_out)

    return call(
        body,
        [counts],
        [tables, patches, probe, spectra, keep, gpatch],
        [
            whole(*tables.shape),
            per_batch_slot(batch, 2, size, size),
            whole(*probe.shape),
            per_slot(modes, 2, size, size),
            per_slot(2, size, h),
            per_slot(2, size, size),
        ],
        [probe.shape, (POS, 2, size, size)],
        [whole(*probe.shape), per_slot(2, size, size)],
        POS,
        flops=POS * modes * 24 * size**3,
        moved=6 * 10**6,
    )


def flips(wide, narrow):
    bits = [(0, 2 << i) for i in range(1, narrow.bit_length() - 2)] + [
        (1 << i, 0) for i in range(1, wide.bit_length() - 1)
    ]

    def exchange(even, odd):
        pairs = []
        for w in range(wide):
            for n in range(narrow):
                dw, dn = odd if n & 1 else even
                pairs.append((w * narrow + n, (w ^ dw) * narrow + (n ^ dn)))
        return functools.partial(lax.ppermute, axis_name=AXES, perm=pairs)

    core = exchange((0, 1), (0, 1))
    first = exchange((0, 2), (1, 0))
    second = exchange((1, 0), (0, 2))
    return core, first, second, [exchange(a, b) for a, b in zip(bits, bits[::-1])]


def shifted(value, axis, steps):
    count = lax.axis_size(axis)
    leading, last = (max(0, -steps), min(count, count - steps))
    return lax.ppermute(value, axis, [(source, source + steps) for source in range(leading, last)])


def local(object_field, probe, patterns, offsets, counts):
    edge = object_field.shape[1]
    modes, _, size, _ = probe.shape
    slots = patterns.shape[2]
    h = size // 2
    full = edge + 2 * H
    wide, narrow = lax.axis_size("wide"), lax.axis_size("narrow")
    w, n = lax.axis_index("wide"), lax.axis_index("narrow")
    core, first, second, rest = flips(wide, narrow)
    offs = offsets.reshape(slots * 2)
    count = counts.reshape(1)

    left_side = shifted(object_field[:, :, edge - H :], "wide", 1)
    right_side = shifted(object_field[:, :, :H], "wide", -1)

    def strip(lo):
        return jnp.concatenate([x[:, lo : lo + H] for x in (left_side, object_field, right_side)], 2)

    top_side = shifted(strip(edge - H), "narrow", 1)
    bottom_side = shifted(strip(0), "narrow", -1)

    tables = jnp.asarray(dft_tables(size))
    order = np.concatenate([np.arange(0, size, 2), np.arange(1, size, 2)])
    pick = jnp.asarray(np.eye(size, dtype=np.float32)[order])
    roots = jnp.einsum("pj,sjk->spk", pick, jnp.sqrt(patterns[0, 0]), precision=lax.Precision.HIGHEST)
    roots = jnp.einsum("spk,qk->spq", roots, pick, precision=lax.Precision.HIGHEST)
    roots = roots.reshape(slots, size, 2, h).transpose(0, 2, 1, 3)

    c = n % 2
    bit_n, bit_w = (n // 2) % 2, w % 2
    b1 = jnp.where(c == 0, bit_n, bit_w)
    b2 = jnp.where(c == 0, bit_w, bit_n)
    ours, theirs = 2 * c, 2 * (1 - c)
    order_of = [ours + b1, ours + 1 - b1, theirs + b2, theirs + 1 - b2]
    rows = modes // 4 * 2 * size
    groups = probe.reshape(4, rows, size)
    p0, p1, p2, p3 = [lax.dynamic_index_in_dim(groups, m, 0, keepdims=False) for m in order_of]

    patches = cut_patches(offs, object_field, (left_side, right_side, top_side, bottom_side), size, slots)

    half, quarter = rows // 2, rows // 4
    gradient = None
    for batch in range(BATCHES):
        z0, i0 = forward_kernel(tables, count, patches, p0, batch)
        z1, i1 = forward_kernel(tables, count, patches, p1, batch)
        p23 = jnp.concatenate([p2, p3], 0)
        sent, keep, gpatch = turn_kernel(tables, count, patches, p23, roots, (i0, i1), batch)
        got = core(sent)
        cover = sent[2 * rows :] + got[2 * rows :]
        g1, gpatch = gradient_kernel(tables, count, patches, p1, z1, keep, gpatch, batch)
        g1 = g1 + got[rows : 2 * rows]
        got_a = first(jnp.concatenate([g1[:half], cover], 0))
        got_b = first(g1[half:])
        g0, gpatch = gradient_kernel(tables, count, patches, p0, z0, keep, gpatch, batch)
        g0 = g0 + got[:rows]
        cover = cover + got_a[half:]
        a = (g0[:half] + got_a[:half]).reshape(2, quarter, size)
        b = (g0[half:] + got_b).reshape(2, quarter, size)

        def part(x, at):
            return lax.dynamic_index_in_dim(x, at, 0, keepdims=False)

        got_a = second(jnp.concatenate([part(a, 1 - b2), cover], 0))
        got_b = second(part(b, 1 - b2))
        a = part(a, b2) + got_a[:quarter]
        b = part(b, b2) + got_b
        cover = cover + got_a[quarter:]
        for exchange in rest:
            got_a = exchange(jnp.concatenate([a, cover], 0))
            got_b = exchange(b)
            a = a + got_a[:quarter]
            cover = cover + got_a[quarter:]
            b = b + got_b
        scale = jnp.sum(cover) / (size * size)
        old_a = part(p0[:half].reshape(2, quarter, size), b2)
        old_b = part(p0[half:].reshape(2, quarter, size), b2)
        a = old_a - a / scale
        b = old_b - b / scale
        got_a = second(a)
        got_b = second(b)

        def join(mine, other):
            return jnp.where(b2 == 0, jnp.concatenate([mine, other], 0), jnp.concatenate([other, mine], 0))

        a, b = join(a, got_a), join(b, got_b)
        got_a, got_b = first(a), first(b)
        p0 = jnp.concatenate([a, b], 0)
        p2 = core(p0)
        p1 = jnp.concatenate([got_a, got_b], 0)
        p3 = core(p1)
        gradient = place_gradients(offs, count, gpatch, gradient, batch, full)

    from_right = shifted(gradient[:, :, :H], "wide", -1)
    from_left = shifted(gradient[:, :, H + edge :], "wide", 1)

    def border(lo):
        inner = gradient[:, lo : lo + H, H : H + edge]
        inner = inner + jnp.pad(from_right[:, lo : lo + H], ((0, 0), (0, 0), (edge - H, 0)))
        return inner + jnp.pad(from_left[:, lo : lo + H], ((0, 0), (0, 0), (0, edge - H)))

    from_below = shifted(border(0), "narrow", -1)
    from_above = shifted(border(H + edge), "narrow", 1)
    inner = merge_borders(gradient, from_right, from_left, from_below, from_above, edge)

    by_group = jnp.stack([p0, p1, p2, p3])
    where = jnp.stack([jnp.argmax(jnp.stack(order_of) == m) for m in range(4)])
    probe_new = jnp.take(by_group, where, axis=0).reshape(probe.shape)
    squares = by_group.reshape(modes, 2, size, size)
    top = jnp.max(jnp.sum(squares[:, 0] ** 2 + squares[:, 1] ** 2, axis=0))
    return (object_field - (0.5 / top) * inner, probe_new)


def solution(mesh):
    placed = (
        P(None, "narrow", "wide"),
        P(),
        P("narrow", "wide", None, None, None),
        P("narrow", "wide", None, None),
        P("narrow", "wide"),
    )
    return jax.shard_map(
        local,
        mesh=mesh,
        in_specs=placed,
        out_specs=(P(None, "narrow", "wide"), P()),
        check_vma=False,
    )
```

```python
import functools

import jax
import jax.numpy as jnp
import ml_dtypes
import numpy as np
from jax import lax
from jax.experimental import pallas as pl
from jax.experimental.pallas import tpu as pltpu
from jax.sharding import PartitionSpec as P

H = 128
BATCHES = 3
POS = 2
AXES = ("wide", "narrow")
F32 = jnp.float32
BF16 = jnp.bfloat16
VMEM_LIMIT = 48 * 1024 * 1024


def halves(table):
    high = table.astype(ml_dtypes.bfloat16)
    low = (table - high.astype(np.float64)).astype(ml_dtypes.bfloat16)
    return np.stack([high, low])


def dft_tables(size):
    half = size // 2
    k = np.arange(half)
    out = []
    for odd in range(2):
        phase = ((2 * k[:, None] + odd) * k[None, :]) % size
        angle = -2.0 * np.pi * phase / size
        re, im = np.cos(angle) / np.sqrt(size), np.sin(angle) / np.sqrt(size)
        out.append(np.block([[re, -im], [im, re]]))
    return np.stack([halves(t) for t in (out[0], out[1], out[0].T, out[1].T)])


def split(x):
    high = x.astype(BF16)
    return high, (x - high.astype(F32)).astype(BF16)


def dot(a, b):
    return jnp.dot(a, b, preferred_element_type=F32)


def left(tables, which, x):
    high, low = split(x)
    t_high, t_low = tables[which, 0], tables[which, 1]
    return dot(t_high, high) + dot(t_high, low) + dot(t_low, high)


def right(x, tables, which):
    high, low = split(x)
    t_high, t_low = tables[which, 0], tables[which, 1]
    return dot(high, t_high) + dot(low, t_high) + dot(high, t_low)


def forward(tables, re, im):
    h = re.shape[0] // 2
    u = jnp.concatenate([re[:h] + re[h:], im[:h] + im[h:]], 0)
    v = jnp.concatenate([re[:h] - re[h:], im[:h] - im[h:]], 0)
    even, odd = left(tables, 0, u), left(tables, 1, v)

    def columns(op):
        rows = [jnp.concatenate([op(y[:h, :h], y[:h, h:]), op(y[h:, :h], y[h:, h:])], 1) for y in (even, odd)]
        return jnp.concatenate(rows, 0)

    return (
        right(columns(lambda a, b: a + b), tables, 2),
        right(columns(lambda a, b: a - b), tables, 3),
    )


def inverse(tables, even, odd):
    h = even.shape[0] // 2
    a, b = right(even, tables, 0), right(odd, tables, 1)
    s, d = a + b, a - b

    def rows(lo):
        return jnp.concatenate(
            [
                jnp.concatenate([s[lo : lo + h, :h], d[lo : lo + h, :h]], 1),
                jnp.concatenate([s[lo : lo + h, h:], d[lo : lo + h, h:]], 1),
            ],
            0,
        )

    a, b = left(tables, 2, rows(0)), left(tables, 3, rows(h))
    s, d = a + b, a - b
    return jnp.concatenate([s[:h], d[:h]], 0), jnp.concatenate([s[h:], d[h:]], 0)


def power_of(z):
    h = z.shape[-1] // 2
    return z[:, :h] * z[:, :h] + z[:, h:] * z[:, h:]


def place_of(which, bit, h):
    return pl.multiple_of(jnp.where(bit == which, 0, h), h)


def rows_of(ref, bit):
    h = ref.shape[0] // 2
    return jnp.concatenate([ref[pl.ds(place_of(which, bit, h), h)] for which in range(2)], 0)


def add_rows(ref, base, bit, value):
    h = value.shape[0] // 2
    for which in range(2):
        ref[pl.ds(base + place_of(which, bit, h), h)] += value[which * h : (which + 1) * h]


def illuminated(tables, patch, probe):
    (p_re, p_im), (o_re, o_im) = probe, (patch[0, 0], patch[0, 1])
    return forward(tables, p_re * o_re - p_im * o_im, p_re * o_im + p_im * o_re)


def gradients(tables, patch, probe, spectrum, keep, pgrad, base, bit, gpatch):
    size = patch.shape[-1]
    k_even, k_odd = keep[0, 0], keep[0, 1]
    b_re, b_im = inverse(
        tables,
        spectrum[0] * jnp.concatenate([k_even, k_even], 1),
        spectrum[1] * jnp.concatenate([k_odd, k_odd], 1),
    )
    (p_re, p_im), (o_re, o_im) = probe, (patch[0, 0], patch[0, 1])
    gpatch[0, 0] += p_re * b_re + p_im * b_im
    gpatch[0, 1] += p_re * b_im - p_im * b_re
    add_rows(pgrad, base, bit, o_re * b_re + o_im * b_im)
    add_rows(pgrad, base + size, bit, o_re * b_im - o_im * b_re)


def whole(*shape):
    return pl.BlockSpec(shape, lambda i, *_: (0,) * len(shape))


def per_slot(*shape):
    return pl.BlockSpec((1, *shape), lambda i, *_: (i,) + (0,) * len(shape))


def per_batch_slot(batch, *shape):
    return pl.BlockSpec((1, *shape), lambda i, *_: (batch * POS + i,) + (0,) * len(shape))


def call(body, scalars, operands, in_specs, out_shapes, out_specs, grid, scratch=(), aliases=None, flops=0, moved=0):
    return pl.pallas_call(
        body,
        out_shape=[jax.ShapeDtypeStruct(s, F32) for s in out_shapes],
        grid_spec=pltpu.PrefetchScalarGridSpec(
            num_scalar_prefetch=len(scalars),
            grid=(grid,),
            in_specs=in_specs,
            out_specs=out_specs,
            scratch_shapes=list(scratch),
        ),
        input_output_aliases=aliases or {},
        compiler_params=pltpu.CompilerParams(vmem_limit_bytes=VMEM_LIMIT),
        cost_estimate=pl.CostEstimate(flops=flops, bytes_accessed=moved, transcendentals=0),
    )(*scalars, *operands)


def corner_of(offs, slot, full, size):
    row = offs[2 * slot] + H
    col = offs[2 * slot + 1] + H
    row_at = pl.multiple_of(jnp.minimum(row // 8 * 8, full - size - 8), 8)
    col_at = pl.multiple_of(jnp.minimum(col // 128 * 128, full - size - 128), 128)
    return row_at, col_at, row - row_at, col - col_at


def cut_patches(offsets, info, tile, sides, size, slots):
    edge = tile.shape[1]
    full = edge + 2 * H

    def body(offs, info_ref, tile_ref, left_ref, right_ref, top_ref, bottom_ref, out, cover, ext):
        i = pl.program_id(0)

        @pl.when(i == 0)
        def _():
            cover[...] = jnp.zeros_like(cover)
            ext[:, :H] = top_ref[...]
            ext[:, H + edge :] = bottom_ref[...]
            ext[:, H : H + edge, :H] = left_ref[...]
            ext[:, H : H + edge, H : H + edge] = tile_ref[...]
            ext[:, H : H + edge, H + edge :] = right_ref[...]

        @pl.when(i < info_ref[0])
        def _():
            row_at, col_at, row, col = corner_of(offs, i, full, size)
            total = jnp.zeros((1, size), F32)
            for part in range(2):
                block = ext[part, pl.ds(row_at, size + 8), pl.ds(col_at, size + 128)]
                block = pltpu.roll(block, size + 128 - col, 1)[:, :size]
                block = pltpu.roll(block, size + 8 - row, 0)[:size]
                out[0, part] = block
                total = total + jnp.sum(block * block, axis=0, keepdims=True)
            here = lax.broadcasted_iota(jnp.int32, cover.shape, 0) == i // POS
            cover[...] += jnp.where(here, total, 0.0)

    return call(
        body,
        [offsets, info],
        [tile, *sides],
        [whole(2, edge, edge), whole(2, edge, H), whole(2, edge, H), whole(2, H, full), whole(2, H, full)],
        [(slots, 2, size, size), (8, size)],
        [per_slot(2, size, size), whole(8, size)],
        slots,
        scratch=[pltpu.VMEM((2, full, full), F32)],
        flops=10**6,
        moved=8 * 10**6,
    )


def place_gradients(offsets, info, patches, after, edge):
    size = patches[0].shape[-1]
    full = edge + 2 * H
    n = len(patches)

    def body(offs, info_ref, *refs):
        patch_refs, (core, upper, lower, left_part, right_part, ext) = refs[:n], refs[n + len(after) :]
        i = pl.program_id(0)

        @pl.when(i == 0)
        def _():
            ext[...] = jnp.zeros_like(ext)

        for batch in range(n):

            @pl.when((i // POS == batch) & (i < info_ref[0]))
            def _():
                row_at, col_at, row, col = corner_of(offs, i, full, size)
                for part in range(2):
                    block = patch_refs[batch][0, part]
                    block = jnp.concatenate([block, jnp.zeros((8, size), F32)], 0)
                    block = pltpu.roll(block, row, 0)
                    block = jnp.concatenate([block, jnp.zeros((size + 8, 128), F32)], 1)
                    block = pltpu.roll(block, col, 1)
                    ext[part, pl.ds(row_at, size + 8), pl.ds(col_at, size + 128)] += block

        @pl.when(i == n * POS - 1)
        def _():
            core[...] = ext[:, H : H + edge, H : H + edge]
            upper[...] = ext[:, :H]
            lower[...] = ext[:, H + edge :]
            left_part[...] = ext[:, H : H + edge, :H]
            right_part[...] = ext[:, H : H + edge, H + edge :]

    def spec(batch):
        return pl.BlockSpec((1, 2, size, size), lambda i, *_: (jnp.clip(i - batch * POS, 0, POS - 1), 0, 0, 0))

    shapes = [(2, edge, edge), (2, H, full), (2, H, full), (2, edge, H), (2, edge, H)]
    return call(
        body,
        [offsets, info],
        [*patches, *after],
        [spec(batch) for batch in range(n)] + [pl.BlockSpec(memory_space=pl.ANY)] * len(after),
        shapes,
        [whole(*shape) for shape in shapes],
        n * POS,
        scratch=[pltpu.VMEM((2, full, full), F32)],
        flops=10**6,
        moved=10**7,
    )


def merge_borders(core, from_right, from_left, from_below, from_above):
    edge = core.shape[1]

    def body(g, fr, fl, fb, fa, out):
        out[...] = g[...]
        out[:, edge - H :] += fb[:, :, H : H + edge]
        out[:, :H] += fa[:, :, H : H + edge]
        out[:, :, edge - H :] += fr[...]
        out[:, :, :H] += fl[...]

    operands = [core, from_right, from_left, from_below, from_above]
    return call(
        body,
        [],
        operands,
        [whole(*x.shape) for x in operands],
        [core.shape],
        [whole(*core.shape)],
        1,
        flops=10**6,
        moved=10**7,
    )[0]


def turn_kernel(tables, info, patches, probes, roots, cover, batch):
    size = patches.shape[-1]
    h = size // 2
    rows = 4 * size
    extra = 0 if cover is None else cover.shape[0]

    def body(info_ref, t, patch, root, *rest):
        p, rest = rest[:8], rest[8:]
        if extra:
            cover_ref, rest = rest[0], rest[1:]
        sent, keep, gpatch, z, scratch = rest
        i = pl.program_id(0)

        @pl.when(i == 0)
        def _():
            sent[:rows] = jnp.zeros((rows, size), F32)
            if extra:
                sent[rows:] = cover_ref[...]

        gpatch[...] = jnp.zeros_like(gpatch)

        @pl.when(batch * POS + i < info_ref[0])
        def _():
            bits = [info_ref[2], info_ref[2], info_ref[1], info_ref[1]]
            totals = [0.0, 0.0]
            for m in range(4):
                pair = illuminated(t, patch, (rows_of(p[2 * m], bits[m]), rows_of(p[2 * m + 1], bits[m])))
                for e in range(2):
                    if m < 2:
                        z[0, m, e] = pair[e]
                    else:
                        scratch[m - 2, e] = pair[e]
                    totals[e] = totals[e] + power_of(pair[e])
            for e in range(2):
                keep[0, e] = 1.0 - root[0, e] * lax.rsqrt(totals[e] + 0.1)
            for m in range(2, 4):
                probe = (rows_of(p[2 * m], bits[m]), rows_of(p[2 * m + 1], bits[m]))
                spectrum = (scratch[m - 2, 0], scratch[m - 2, 1])
                gradients(t, patch, probe, spectrum, keep, sent, (m - 2) * 2 * size, bits[m], gpatch)

    operands = [tables, patches, roots, *probes]
    specs = [
        whole(*tables.shape),
        per_batch_slot(batch, 2, size, size),
        per_batch_slot(batch, 2, size, h),
    ] + [whole(size, size)] * 8
    if extra:
        operands, specs = [*operands, cover], [*specs, whole(*cover.shape)]
    return call(
        body,
        [info],
        operands,
        specs,
        [(rows + extra, size), (POS, 2, size, h), (POS, 2, size, size), (POS, 2, 2, size, size)],
        [whole(rows + extra, size), per_slot(2, size, h), per_slot(2, size, size), per_slot(2, 2, size, size)],
        POS,
        scratch=[pltpu.VMEM((2, 2, size, size), F32)],
        flops=POS * 6 * 24 * size**3,
        moved=8 * 10**6,
    )


def back_kernel(tables, info, patches, probes, spectra, keep, gpatch, batch):
    size = patches.shape[-1]
    h = size // 2

    def body(info_ref, t, patch, z, k, g_in, *rest):
        p, (g0, g1, g_out) = rest[:4], rest[4:]
        i = pl.program_id(0)

        @pl.when(i == 0)
        def _():
            g0[...] = jnp.zeros_like(g0)
            g1[...] = jnp.zeros_like(g1)

        g_out[...] = g_in[...]

        @pl.when(batch * POS + i < info_ref[0])
        def _():
            bit = info_ref[2]
            for m, out in ((1, g1), (0, g0)):
                probe = (rows_of(p[2 * m], bit), rows_of(p[2 * m + 1], bit))
                gradients(t, patch, probe, (z[0, m, 0], z[0, m, 1]), k, out, 0, bit, g_out)

    return call(
        body,
        [info],
        [tables, patches, spectra, keep, gpatch, *probes[:4]],
        [
            whole(*tables.shape),
            per_batch_slot(batch, 2, size, size),
            per_slot(2, 2, size, size),
            per_slot(2, size, h),
            per_slot(2, size, size),
        ]
        + [whole(size, size)] * 4,
        [(2 * size, size), (2 * size, size), (POS, 2, size, size)],
        [whole(2 * size, size), whole(2 * size, size), per_slot(2, size, size)],
        POS,
        flops=POS * 2 * 24 * size**3,
        moved=6 * 10**6,
    )


def finish_kernel(info, probes, field, inner):
    size = probes[0].shape[0]
    edge = field.shape[1]
    chunk = edge // 4

    def body(info_ref, *refs):
        p, (o, g, probe_out, object_out, power) = refs[:8], refs[8:]
        i = pl.program_id(0)
        for m in range(4):

            @pl.when(i == m)
            def _():
                bit = info_ref[2] if m < 2 else info_ref[1]
                re, im = rows_of(p[2 * m], bit), rows_of(p[2 * m + 1], bit)
                probe_out[0, 0], probe_out[0, 1] = re, im
                square = re * re + im * im
                power[...] = square if m == 0 else power[...] + square

        @pl.when(i >= 4)
        def _():
            top = jnp.max(power[...], keepdims=True)
            object_out[...] = o[...] - g[...] * (0.5 / top)[None]

    spec = pl.BlockSpec((2, chunk, edge), lambda i, *_: (0, jnp.maximum(i - 4, 0), 0))
    return call(
        body,
        [info],
        [*probes, field, inner],
        [whole(size, size)] * 8 + [spec, spec],
        [(4, 2, size, size), field.shape],
        [pl.BlockSpec((1, 2, size, size), lambda i, info_ref: (info_ref[3 + jnp.minimum(i, 3)], 0, 0, 0)), spec],
        8,
        scratch=[pltpu.VMEM((size, size), F32)],
        flops=10**6,
        moved=10**7,
    )


def flips(wide, narrow):
    bits = [(0, 2 << i) for i in range(1, narrow.bit_length() - 2)] + [
        (1 << i, 0) for i in range(1, wide.bit_length() - 1)
    ]

    def exchange(even, odd):
        pairs = []
        for w in range(wide):
            for n in range(narrow):
                dw, dn = odd if n & 1 else even
                pairs.append((w * narrow + n, (w ^ dw) * narrow + (n ^ dn)))
        return functools.partial(lax.ppermute, axis_name=AXES, perm=pairs)

    core = exchange((0, 1), (0, 1))
    first = exchange((0, 2), (1, 0))
    second = exchange((1, 0), (0, 2))
    return core, first, second, [exchange(a, b) for a, b in zip(bits, bits[::-1])]


def shifted(value, axis, steps):
    count = lax.axis_size(axis)
    leading, last = (max(0, -steps), min(count, count - steps))
    return lax.ppermute(value, axis, [(source, source + steps) for source in range(leading, last)])


def local(object_field, probe, patterns, offsets, counts):
    edge = object_field.shape[1]
    size = probe.shape[-1]
    slots = patterns.shape[2]
    h = size // 2
    wide, narrow = lax.axis_size("wide"), lax.axis_size("narrow")
    w, n = lax.axis_index("wide"), lax.axis_index("narrow")
    core, first, second, rest = flips(wide, narrow)
    offs = offsets.reshape(slots * 2)

    left_side = shifted(object_field[:, :, edge - H :], "wide", 1)
    right_side = shifted(object_field[:, :, :H], "wide", -1)

    def strip(lo):
        return jnp.concatenate([x[:, lo : lo + H] for x in (left_side, object_field, right_side)], 2)

    top_side = shifted(strip(edge - H), "narrow", 1)
    bottom_side = shifted(strip(0), "narrow", -1)

    tables = jnp.asarray(dft_tables(size))
    order = np.concatenate([np.arange(0, size, 2), np.arange(1, size, 2)])
    pick = jnp.asarray(np.eye(size, dtype=np.float32)[order])
    roots = jnp.einsum("pj,sjk->spk", pick, jnp.sqrt(patterns[0, 0]), precision=lax.Precision.HIGHEST)
    roots = jnp.einsum("spk,qk->spq", roots, pick, precision=lax.Precision.HIGHEST)
    roots = roots.reshape(slots, size, 2, h).transpose(0, 2, 1, 3)

    c = n % 2
    bit_n, bit_w = (n // 2) % 2, w % 2
    b1 = jnp.where(c == 0, bit_n, bit_w)
    b2 = jnp.where(c == 0, bit_w, bit_n)
    ours, theirs = 2 * c, 2 * (1 - c)
    order_of = [ours + b1, ours + 1 - b1, theirs + b2, theirs + 1 - b2]
    info = jnp.stack([counts[0, 0], b1, b2, *order_of]).astype(jnp.int32)
    split_rows = probe.reshape(4, 2, 2, h, size)
    probes = []
    for m, bit in zip(order_of, (b2, b2, b1, b1)):
        for part in range(2):
            mine = lax.dynamic_slice(split_rows, (m, part, bit, 0, 0), (1, 1, 1, h, size))
            other = lax.dynamic_slice(split_rows, (m, part, 1 - bit, 0, 0), (1, 1, 1, h, size))
            probes.append(jnp.concatenate([mine.reshape(h, size), other.reshape(h, size)], 0))

    sides = (left_side, right_side, top_side, bottom_side)
    patches, cover = cut_patches(offs, info, object_field, sides, size, slots)

    patch_gradients = []
    for batch in range(BATCHES):
        extra = cover if batch == 0 else None

        def ride(x):
            return x if extra is None else jnp.concatenate([x, extra], 0)

        sent, keep, gpatch, z = turn_kernel(tables, info, patches, probes, roots, extra, batch)
        got = core(sent)
        g0, g1, gpatch = back_kernel(tables, info, patches, probes, z, keep, gpatch, batch)
        patch_gradients.append(gpatch)
        if extra is not None:
            extra = extra + got[4 * size :]
        sent_a = g1[:size] + got[2 * size : 3 * size]
        sent_b = g1[size:] + got[3 * size : 4 * size]
        if batch == BATCHES - 1:
            placed = place_gradients(offs, info, patch_gradients, (sent_a, sent_b), edge)
        got_a = first(ride(sent_a))
        got_b = first(sent_b)
        sent_a = g0[h:size] + got[h:size] + got_a[h:size]
        sent_b = g0[size + h :] + got[size + h : 2 * size] + got_b[h:]
        a = g0[:h] + got[:h] + got_a[:h]
        b = g0[size : size + h] + got[size : size + h] + got_b[:h]
        if extra is not None:
            extra = extra + got_a[size:]
        got_a = second(ride(sent_a))
        got_b = second(sent_b)
        a = a + got_a[:h]
        b = b + got_b
        if extra is not None:
            extra = extra + got_a[h:]
        for exchange in rest:
            got_a = exchange(ride(a))
            got_b = exchange(b)
            a = a + got_a[:h]
            b = b + got_b
            if extra is not None:
                extra = extra + got_a[h:]
        if extra is not None:
            scales = jnp.sum(extra, axis=1) / (size * size)
        a = probes[0][:h] - a / scales[batch]
        b = probes[1][:h] - b / scales[batch]
        a = jnp.concatenate([a, second(a)], 0)
        b = jnp.concatenate([b, second(b)], 0)
        own = [a, b, first(a), first(b)]
        probes = own + [core(x) for x in own]

    inside, upper, lower, left_part, right_part = placed
    from_below = shifted(upper, "narrow", -1)
    from_above = shifted(lower, "narrow", 1)

    def border(part, lo):
        below = jnp.pad(from_below[:, :, lo : lo + H], ((0, 0), (edge - H, 0), (0, 0)))
        above = jnp.pad(from_above[:, :, lo : lo + H], ((0, 0), (0, edge - H), (0, 0)))
        return part + below + above

    from_right = shifted(border(left_part, 0), "wide", -1)
    from_left = shifted(border(right_part, H + edge), "wide", 1)
    inner = merge_borders(inside, from_right, from_left, from_below, from_above)
    probe_new, object_new = finish_kernel(info, probes, object_field, inner)
    return (object_new, probe_new)


def solution(mesh):
    placed = (
        P(None, "narrow", "wide"),
        P(),
        P("narrow", "wide", None, None, None),
        P("narrow", "wide", None, None),
        P("narrow", "wide"),
    )
    return jax.shard_map(
        local,
        mesh=mesh,
        in_specs=placed,
        out_specs=(P(None, "narrow", "wide"), P()),
        check_vma=False,
    )
```

```python
import functools

import jax
import jax.numpy as jnp
import ml_dtypes
import numpy as np
from jax import lax
from jax.experimental import pallas as pl
from jax.experimental.pallas import tpu as pltpu
from jax.sharding import PartitionSpec as P

H = 128
BATCHES = 3
POS = 2
AXES = ("wide", "narrow")
F32 = jnp.float32
BF16 = jnp.bfloat16
VMEM_LIMIT = 48 * 1024 * 1024


def halves(table):
    high = table.astype(ml_dtypes.bfloat16)
    low = (table - high.astype(np.float64)).astype(ml_dtypes.bfloat16)
    return np.stack([high, low])


def dft_tables(size):
    half = size // 2
    k = np.arange(half)
    out = []
    for odd in range(2):
        phase = ((2 * k[:, None] + odd) * k[None, :]) % size
        angle = -2.0 * np.pi * phase / size
        re, im = np.cos(angle) / np.sqrt(size), np.sin(angle) / np.sqrt(size)
        out.append(np.block([[re, -im], [im, re]]))
    return np.stack([halves(t) for t in (out[0], out[1], out[0].T, out[1].T)])


def split(x):
    high = x.astype(BF16)
    return high, (x - high.astype(F32)).astype(BF16)


def dot(a, b):
    return jnp.dot(a, b, preferred_element_type=F32)


def left(tables, which, x):
    high, low = split(x)
    t_high, t_low = tables[which, 0], tables[which, 1]
    return dot(t_high, high) + dot(t_high, low) + dot(t_low, high)


def right(x, tables, which):
    high, low = split(x)
    t_high, t_low = tables[which, 0], tables[which, 1]
    return dot(high, t_high) + dot(low, t_high) + dot(high, t_low)


def forward(tables, re, im):
    h = re.shape[0] // 2
    u = jnp.concatenate([re[:h] + re[h:], im[:h] + im[h:]], 0)
    v = jnp.concatenate([re[:h] - re[h:], im[:h] - im[h:]], 0)
    even, odd = left(tables, 0, u), left(tables, 1, v)

    def columns(op):
        rows = [jnp.concatenate([op(y[:h, :h], y[:h, h:]), op(y[h:, :h], y[h:, h:])], 1) for y in (even, odd)]
        return jnp.concatenate(rows, 0)

    return (
        right(columns(lambda a, b: a + b), tables, 2),
        right(columns(lambda a, b: a - b), tables, 3),
    )


def inverse(tables, even, odd):
    h = even.shape[0] // 2
    a, b = right(even, tables, 0), right(odd, tables, 1)
    s, d = a + b, a - b

    def rows(lo):
        return jnp.concatenate(
            [
                jnp.concatenate([s[lo : lo + h, :h], d[lo : lo + h, :h]], 1),
                jnp.concatenate([s[lo : lo + h, h:], d[lo : lo + h, h:]], 1),
            ],
            0,
        )

    a, b = left(tables, 2, rows(0)), left(tables, 3, rows(h))
    s, d = a + b, a - b
    return jnp.concatenate([s[:h], d[:h]], 0), jnp.concatenate([s[h:], d[h:]], 0)


def power_of(z):
    h = z.shape[-1] // 2
    return z[:, :h] * z[:, :h] + z[:, h:] * z[:, h:]


def place_of(which, bit, h):
    return pl.multiple_of(jnp.where(bit == which, 0, h), h)


def rows_of(ref, bit):
    h = ref.shape[0] // 2
    return jnp.concatenate([ref[pl.ds(place_of(which, bit, h), h)] for which in range(2)], 0)


def add_rows(ref, base, bit, value):
    h = value.shape[0] // 2
    for which in range(2):
        ref[pl.ds(base + place_of(which, bit, h), h)] += value[which * h : (which + 1) * h]


def illuminated(tables, patch, probe):
    (p_re, p_im), (o_re, o_im) = probe, (patch[0, 0], patch[0, 1])
    return forward(tables, p_re * o_re - p_im * o_im, p_re * o_im + p_im * o_re)


def gradients(tables, patch, probe, spectrum, keep, pgrad, base, bit, gpatch):
    size = patch.shape[-1]
    k_even, k_odd = keep[0, 0], keep[0, 1]
    b_re, b_im = inverse(
        tables,
        spectrum[0] * jnp.concatenate([k_even, k_even], 1),
        spectrum[1] * jnp.concatenate([k_odd, k_odd], 1),
    )
    (p_re, p_im), (o_re, o_im) = probe, (patch[0, 0], patch[0, 1])
    gpatch[0, 0] += p_re * b_re + p_im * b_im
    gpatch[0, 1] += p_re * b_im - p_im * b_re
    add_rows(pgrad, base, bit, o_re * b_re + o_im * b_im)
    add_rows(pgrad, base + size, bit, o_re * b_im - o_im * b_re)


def whole(*shape):
    return pl.BlockSpec(shape, lambda i, *_: (0,) * len(shape))


def per_slot(*shape):
    return pl.BlockSpec((1, *shape), lambda i, *_: (i,) + (0,) * len(shape))


def per_batch_slot(batch, *shape):
    return pl.BlockSpec((1, *shape), lambda i, *_: (batch * POS + i,) + (0,) * len(shape))


def call(body, scalars, operands, in_specs, out_shapes, out_specs, grid, scratch=(), aliases=None, flops=0, moved=0):
    return pl.pallas_call(
        body,
        out_shape=[jax.ShapeDtypeStruct(s, F32) for s in out_shapes],
        grid_spec=pltpu.PrefetchScalarGridSpec(
            num_scalar_prefetch=len(scalars),
            grid=(grid,),
            in_specs=in_specs,
            out_specs=out_specs,
            scratch_shapes=list(scratch),
        ),
        input_output_aliases=aliases or {},
        compiler_params=pltpu.CompilerParams(vmem_limit_bytes=VMEM_LIMIT),
        cost_estimate=pl.CostEstimate(flops=flops, bytes_accessed=moved, transcendentals=0),
    )(*scalars, *operands)


def corner_of(offs, slot, full, size):
    row = offs[2 * slot] + H
    col = offs[2 * slot + 1] + H
    row_at = pl.multiple_of(jnp.minimum(row // 8 * 8, full - size - 8), 8)
    col_at = pl.multiple_of(jnp.minimum(col // 128 * 128, full - size - 128), 128)
    return row_at, col_at, row - row_at, col - col_at


def shift_in(block, row, col):
    rows, columns = block.shape
    turn = lax.rem(128 - col, 128)
    tiles = [pltpu.roll(block[:, at : at + 128], turn, 1) for at in range(0, columns, 128)]
    here = lax.broadcasted_iota(jnp.int32, (rows, 128), 1) < 128 - col
    block = jnp.concatenate([jnp.where(here, a, b) for a, b in zip(tiles, tiles[1:])], 1)
    block = pltpu.roll(block.reshape(rows // 8, 8, columns - 128), lax.rem(8 - row, 8), 1)
    here = lax.broadcasted_iota(jnp.int32, (rows // 8 - 1, 8, columns - 128), 1) < 8 - row
    return jnp.where(here, block[:-1], block[1:]).reshape(rows - 8, columns - 128)


def shift_out(block, row, col):
    rows, columns = block.shape
    block = pltpu.roll(block.reshape(rows // 8, 8, columns), lax.rem(row, 8), 1)
    zero = jnp.zeros((1, 8, columns), F32)
    here = lax.broadcasted_iota(jnp.int32, (rows // 8 + 1, 8, columns), 1) >= row
    block = jnp.where(here, jnp.concatenate([block, zero], 0), jnp.concatenate([zero, block], 0))
    block = block.reshape(rows + 8, columns)
    zero = jnp.zeros((rows + 8, 128), F32)
    tiles = [zero] + [pltpu.roll(block[:, at : at + 128], lax.rem(col, 128), 1) for at in range(0, columns, 128)] + [zero]
    here = lax.broadcasted_iota(jnp.int32, (rows + 8, 128), 1) >= col
    return jnp.concatenate([jnp.where(here, b, a) for a, b in zip(tiles, tiles[1:])], 1)


def cut_corners(left_side, right_side, after):
    edge = left_side.shape[1]

    def body(left_ref, right_ref, *rest):
        leading, last = rest[-2:]
        for ref, rows in ((leading, slice(0, H)), (last, slice(edge - H, edge))):
            ref[:, :, :H] = left_ref[:, rows]
            ref[:, :, H:] = right_ref[:, rows]

    return call(
        body,
        [],
        [left_side, right_side, *after],
        [whole(2, edge, H)] * 2 + [pl.BlockSpec(memory_space=pl.ANY)] * len(after),
        [(2, H, 2 * H)] * 2,
        [whole(2, H, 2 * H)] * 2,
        1,
        flops=10**5,
        moved=2 * 10**6,
    )


def cut_patches(offsets, info, tile, sides, size, slots):
    edge = tile.shape[1]
    full = edge + 2 * H
    low, mid, high = slice(0, H), slice(H, H + edge), slice(H + edge, full)
    first_half, second_half, everything = slice(0, H), slice(H, 2 * H), slice(None)
    pieces = [
        (0, everything, mid, mid),
        (1, everything, mid, low),
        (2, everything, mid, high),
        (3, everything, low, mid),
        (4, everything, high, mid),
        (5, first_half, low, low),
        (5, second_half, low, high),
        (6, first_half, high, low),
        (6, second_half, high, high),
    ]

    def body(offs, info_ref, *refs):
        sources, (out, cover, ext, sems) = refs[:7], refs[7:]
        i = pl.program_id(0)

        @pl.when(i == 0)
        def _():
            copies = [
                pltpu.make_async_copy(sources[k].at[:, :, part], ext.at[:, rows, columns], sems.at[j])
                for j, (k, part, rows, columns) in enumerate(pieces)
            ]
            for copy in copies:
                copy.start()
            cover[...] = jnp.zeros_like(cover)
            for copy in copies:
                copy.wait()

        @pl.when(i < info_ref[0])
        def _():
            row_at, col_at, row, col = corner_of(offs, i, full, size)
            total = jnp.zeros((1, size), F32)
            for part in range(2):
                block = shift_in(ext[part, pl.ds(row_at, size + 8), pl.ds(col_at, size + 128)], row, col)
                out[0, part] = block
                total = total + jnp.sum(block * block, axis=0, keepdims=True)
            here = lax.broadcasted_iota(jnp.int32, cover.shape, 0) == i // POS
            cover[...] += jnp.where(here, total, 0.0)

    return call(
        body,
        [offsets, info],
        [tile, *sides],
        [pl.BlockSpec(memory_space=pl.ANY)] * 7,
        [(slots, 2, size, size), (8, size)],
        [per_slot(2, size, size), whole(8, size)],
        slots,
        scratch=[pltpu.VMEM((2, full, full), F32), pltpu.SemaphoreType.DMA((len(pieces),))],
        flops=10**6,
        moved=8 * 10**6,
    )


def place_gradients(offsets, info, patches, after, edge):
    size = patches[0].shape[-1]
    full = edge + 2 * H
    n = len(patches)

    def body(offs, info_ref, *refs):
        patch_refs, (core, upper, lower, left_part, right_part, ext) = refs[:n], refs[n + len(after) :]
        i = pl.program_id(0)

        @pl.when(i == 0)
        def _():
            ext[...] = jnp.zeros_like(ext)

        for batch in range(n):

            @pl.when((i // POS == batch) & (i < info_ref[0]))
            def _():
                row_at, col_at, row, col = corner_of(offs, i, full, size)
                for part in range(2):
                    block = shift_out(patch_refs[batch][0, part], row, col)
                    ext[part, pl.ds(row_at, size + 8), pl.ds(col_at, size + 128)] += block

        @pl.when(i == n * POS - 1)
        def _():
            core[...] = ext[:, H : H + edge, H : H + edge]
            upper[...] = ext[:, :H]
            lower[...] = ext[:, H + edge :]
            left_part[...] = ext[:, H : H + edge, :H]
            right_part[...] = ext[:, H : H + edge, H + edge :]

    def spec(batch):
        return pl.BlockSpec((1, 2, size, size), lambda i, *_: (jnp.clip(i - batch * POS, 0, POS - 1), 0, 0, 0))

    shapes = [(2, edge, edge), (2, H, full), (2, H, full), (2, edge, H), (2, edge, H)]
    return call(
        body,
        [offsets, info],
        [*patches, *after],
        [spec(batch) for batch in range(n)] + [pl.BlockSpec(memory_space=pl.ANY)] * len(after),
        shapes,
        [whole(*shape) for shape in shapes],
        n * POS,
        scratch=[pltpu.VMEM((2, full, full), F32)],
        flops=10**6,
        moved=10**7,
    )


def side_borders(left_part, right_part, from_below, from_above, after):
    edge = left_part.shape[1]
    full = from_below.shape[2]

    def body(left_ref, right_ref, below, above, *rest):
        for ref, out, at in ((left_ref, rest[-2], 0), (right_ref, rest[-1], H + edge)):
            out[...] = ref[...]
            out[:, edge - H :] += below[:, :, at : at + H]
            out[:, :H] += above[:, :, at : at + H]

    return call(
        body,
        [],
        [left_part, right_part, from_below, from_above, *after],
        [whole(2, edge, H)] * 2 + [whole(2, H, full)] * 2 + [pl.BlockSpec(memory_space=pl.ANY)] * len(after),
        [(2, edge, H)] * 2,
        [whole(2, edge, H)] * 2,
        1,
        flops=10**5,
        moved=4 * 10**6,
    )


def turn_kernel(tables, info, patches, probes, roots, cover, batch):
    size = patches.shape[-1]
    h = size // 2
    rows = 4 * size
    extra = 0 if cover is None else cover.shape[0]

    def body(info_ref, t, patch, root, *rest):
        p, rest = rest[:8], rest[8:]
        if extra:
            cover_ref, rest = rest[0], rest[1:]
        sent, keep, gpatch, z, scratch = rest
        i = pl.program_id(0)

        @pl.when(i == 0)
        def _():
            sent[:rows] = jnp.zeros((rows, size), F32)
            if extra:
                sent[rows:] = cover_ref[...]

        gpatch[...] = jnp.zeros_like(gpatch)

        @pl.when(batch * POS + i < info_ref[0])
        def _():
            bits = [info_ref[2], info_ref[2], info_ref[1], info_ref[1]]
            totals = [0.0, 0.0]
            for m in range(4):
                pair = illuminated(t, patch, (rows_of(p[2 * m], bits[m]), rows_of(p[2 * m + 1], bits[m])))
                for e in range(2):
                    if m < 2:
                        z[0, m, e] = pair[e]
                    else:
                        scratch[m - 2, e] = pair[e]
                    totals[e] = totals[e] + power_of(pair[e])
            for e in range(2):
                keep[0, e] = 1.0 - root[0, e] * lax.rsqrt(totals[e] + 0.1)
            for m in range(2, 4):
                probe = (rows_of(p[2 * m], bits[m]), rows_of(p[2 * m + 1], bits[m]))
                spectrum = (scratch[m - 2, 0], scratch[m - 2, 1])
                gradients(t, patch, probe, spectrum, keep, sent, (m - 2) * 2 * size, bits[m], gpatch)

    operands = [tables, patches, roots, *probes]
    specs = [
        whole(*tables.shape),
        per_batch_slot(batch, 2, size, size),
        per_batch_slot(batch, 2, size, h),
    ] + [whole(size, size)] * 8
    if extra:
        operands, specs = [*operands, cover], [*specs, whole(*cover.shape)]
    return call(
        body,
        [info],
        operands,
        specs,
        [(rows + extra, size), (POS, 2, size, h), (POS, 2, size, size), (POS, 2, 2, size, size)],
        [whole(rows + extra, size), per_slot(2, size, h), per_slot(2, size, size), per_slot(2, 2, size, size)],
        POS,
        scratch=[pltpu.VMEM((2, 2, size, size), F32)],
        flops=POS * 6 * 24 * size**3,
        moved=8 * 10**6,
    )


def back_kernel(tables, info, patches, probe, spectra, keep, gpatch, batch, mode, after):
    size = patches.shape[-1]
    h = size // 2

    def body(info_ref, t, patch, z, k, g_in, p_re, p_im, *rest):
        pgrad, g_out = rest[len(after) :]
        i = pl.program_id(0)

        @pl.when(i == 0)
        def _():
            pgrad[...] = jnp.zeros_like(pgrad)

        g_out[...] = g_in[...]

        @pl.when(batch * POS + i < info_ref[0])
        def _():
            bit = info_ref[2]
            pair = (rows_of(p_re, bit), rows_of(p_im, bit))
            gradients(t, patch, pair, (z[0, 0, 0], z[0, 0, 1]), k, pgrad, 0, bit, g_out)

    return call(
        body,
        [info],
        [tables, patches, spectra, keep, gpatch, *probe, *after],
        [
            whole(*tables.shape),
            per_batch_slot(batch, 2, size, size),
            pl.BlockSpec((1, 1, 2, size, size), lambda i, *_: (i, mode, 0, 0, 0)),
            per_slot(2, size, h),
            per_slot(2, size, size),
        ]
        + [whole(size, size)] * 2
        + [pl.BlockSpec(memory_space=pl.ANY)] * len(after),
        [(2 * size, size), (POS, 2, size, size)],
        [whole(2 * size, size), per_slot(2, size, size)],
        POS,
        flops=POS * 24 * size**3,
        moved=4 * 10**6,
    )


def probe_kernel(info, probes):
    size = probes[0].shape[0]

    def body(info_ref, *refs):
        p, (probe_out, top, power) = refs[:8], refs[8:]
        i = pl.program_id(0)
        for m in range(4):

            @pl.when(i == m)
            def _():
                bit = info_ref[2] if m < 2 else info_ref[1]
                re, im = rows_of(p[2 * m], bit), rows_of(p[2 * m + 1], bit)
                probe_out[0, 0], probe_out[0, 1] = re, im
                square = re * re + im * im
                power[...] = square if m == 0 else power[...] + square

        @pl.when(i == 3)
        def _():
            top[...] = jnp.broadcast_to(jnp.max(power[...], keepdims=True), top.shape)

    return call(
        body,
        [info],
        probes,
        [whole(size, size)] * 8,
        [(4, 2, size, size), (8, 128)],
        [pl.BlockSpec((1, 2, size, size), lambda i, info_ref: (info_ref[3 + i], 0, 0, 0)), whole(8, 128)],
        4,
        scratch=[pltpu.VMEM((size, size), F32)],
        flops=10**6,
        moved=4 * 10**6,
    )


def object_kernel(top, field, core, from_right, from_left, from_below, from_above):
    edge = field.shape[1]
    full = from_below.shape[2]
    steps = edge // H

    def body(top_ref, o, g, fr, fl, fb, fa, out):
        i = pl.program_id(0)
        step = (0.5 / top_ref[:1, :1])[None]
        out[...] = o[...] - step * g[...]
        out[:, :, edge - H :] -= step * fr[...]
        out[:, :, :H] -= step * fl[...]

        @pl.when(i == steps - 1)
        def _():
            out[...] -= step * fb[:, :, H : H + edge]

        @pl.when(i == 0)
        def _():
            out[...] -= step * fa[:, :, H : H + edge]

    band = pl.BlockSpec((2, H, edge), lambda i: (0, i, 0))
    side = pl.BlockSpec((2, H, H), lambda i: (0, i, 0))
    return call(
        body,
        [],
        [top, field, core, from_right, from_left, from_below, from_above],
        [whole(8, 128), band, band, side, side, whole(2, H, full), whole(2, H, full)],
        [field.shape],
        [band],
        steps,
        flops=10**6,
        moved=8 * 10**6,
    )[0]


def flips(wide, narrow):
    bits = [(0, 2 << i) for i in range(1, narrow.bit_length() - 2)] + [
        (1 << i, 0) for i in range(1, wide.bit_length() - 1)
    ]

    def exchange(even, odd):
        pairs = []
        for w in range(wide):
            for n in range(narrow):
                dw, dn = odd if n & 1 else even
                pairs.append((w * narrow + n, (w ^ dw) * narrow + (n ^ dn)))
        return functools.partial(lax.ppermute, axis_name=AXES, perm=pairs)

    core = exchange((0, 1), (0, 1))
    first = exchange((0, 2), (1, 0))
    second = exchange((1, 0), (0, 2))
    return core, first, second, [exchange(a, b) for a, b in zip(bits, bits[::-1])]


def shifted(value, axis, steps):
    count = lax.axis_size(axis)
    leading, last = (max(0, -steps), min(count, count - steps))
    return lax.ppermute(value, axis, [(source, source + steps) for source in range(leading, last)])


def local(object_field, probe, patterns, offsets, counts):
    edge = object_field.shape[1]
    size = probe.shape[-1]
    slots = patterns.shape[2]
    h = size // 2
    wide, narrow = lax.axis_size("wide"), lax.axis_size("narrow")
    w, n = lax.axis_index("wide"), lax.axis_index("narrow")
    core, first, second, rest = flips(wide, narrow)
    offs = offsets.reshape(slots * 2)

    left_side = shifted(object_field[:, :, edge - H :], "wide", 1)
    right_side = shifted(object_field[:, :, :H], "wide", -1)
    top_side = shifted(object_field[:, edge - H :], "narrow", 1)
    bottom_side = shifted(object_field[:, :H], "narrow", -1)

    tables = jnp.asarray(dft_tables(size))
    order = np.concatenate([np.arange(0, size, 2), np.arange(1, size, 2)])
    pick = jnp.asarray(np.eye(size, dtype=np.float32)[order])
    roots = jnp.einsum("pj,sjk->spk", pick, jnp.sqrt(patterns[0, 0]), precision=lax.Precision.HIGHEST)
    roots = jnp.einsum("spk,qk->spq", roots, pick, precision=lax.Precision.HIGHEST)
    roots = roots.reshape(slots, size, 2, h).transpose(0, 2, 1, 3)

    c = n % 2
    bit_n, bit_w = (n // 2) % 2, w % 2
    b1 = jnp.where(c == 0, bit_n, bit_w)
    b2 = jnp.where(c == 0, bit_w, bit_n)
    ours, theirs = 2 * c, 2 * (1 - c)
    order_of = [ours + b1, ours + 1 - b1, theirs + b2, theirs + 1 - b2]
    info = jnp.stack([counts[0, 0], b1, b2, *order_of]).astype(jnp.int32)
    split_rows = probe.reshape(4, 2, 2, h, size)
    probes = []
    for m, bit in zip(order_of, (b2, b2, b1, b1)):
        for part in range(2):
            mine = lax.dynamic_slice(split_rows, (m, part, bit, 0, 0), (1, 1, 1, h, size))
            other = lax.dynamic_slice(split_rows, (m, part, 1 - bit, 0, 0), (1, 1, 1, h, size))
            probes.append(jnp.concatenate([mine.reshape(h, size), other.reshape(h, size)], 0))

    leading, last = cut_corners(left_side, right_side, (roots, *probes))
    top_corners = shifted(last, "narrow", 1)
    bottom_corners = shifted(leading, "narrow", -1)
    sides = (left_side, right_side, top_side, bottom_side, top_corners, bottom_corners)
    patches, cover = cut_patches(offs, info, object_field, sides, size, slots)

    patch_gradients = []
    for batch in range(BATCHES):
        extra = cover if batch == 0 else None

        def ride(x):
            return x if extra is None else jnp.concatenate([x, extra], 0)

        sent, keep, gpatch, z = turn_kernel(tables, info, patches, probes, roots, extra, batch)
        got = core(sent)
        g1, gpatch = back_kernel(tables, info, patches, probes[2:4], z, keep, gpatch, batch, 1, ())
        if extra is not None:
            extra = extra + got[4 * size :]
        sent_a = g1[:size] + got[2 * size : 3 * size]
        sent_b = g1[size:] + got[3 * size : 4 * size]
        got_a = first(ride(sent_a))
        got_b = first(sent_b)
        g0, gpatch = back_kernel(tables, info, patches, probes[:2], z, keep, gpatch, batch, 0, (sent_a, sent_b))
        patch_gradients.append(gpatch)
        sent_a = g0[h:size] + got[h:size] + got_a[h:size]
        sent_b = g0[size + h :] + got[size + h : 2 * size] + got_b[h:]
        a = g0[:h] + got[:h] + got_a[:h]
        b = g0[size : size + h] + got[size : size + h] + got_b[:h]
        if extra is not None:
            extra = extra + got_a[size:]
        got_a = second(ride(sent_a))
        got_b = second(sent_b)
        a = a + got_a[:h]
        b = b + got_b
        if extra is not None:
            extra = extra + got_a[h:]
        if batch == BATCHES - 1:
            inside, upper, lower, left_part, right_part = place_gradients(offs, info, patch_gradients, (a, b), edge)
            from_below = shifted(upper, "narrow", -1)
            from_above = shifted(lower, "narrow", 1)
        for exchange in rest:
            got_a = exchange(ride(a))
            got_b = exchange(b)
            a = a + got_a[:h]
            b = b + got_b
            if extra is not None:
                extra = extra + got_a[h:]
        if extra is not None:
            scales = jnp.sum(extra, axis=1) / (size * size)
        a = probes[0][:h] - a / scales[batch]
        b = probes[1][:h] - b / scales[batch]
        a = jnp.concatenate([a, second(a)], 0)
        b = jnp.concatenate([b, second(b)], 0)
        own = [a, b, first(a), first(b)]
        probes = own + [core(x) for x in own]

    to_left, to_right = side_borders(left_part, right_part, from_below, from_above, own[2:])
    from_right = shifted(to_left, "wide", -1)
    from_left = shifted(to_right, "wide", 1)
    probe_new, top = probe_kernel(info, probes)
    object_new = object_kernel(top, object_field, inside, from_right, from_left, from_below, from_above)
    return (object_new, probe_new)


def solution(mesh):
    placed = (
        P(None, "narrow", "wide"),
        P(),
        P("narrow", "wide", None, None, None),
        P("narrow", "wide", None, None),
        P("narrow", "wide"),
    )
    return jax.shard_map(
        local,
        mesh=mesh,
        in_specs=placed,
        out_specs=(P(None, "narrow", "wide"), P()),
        check_vma=False,
    )
```

```python
import functools

import jax
import jax.numpy as jnp
import ml_dtypes
import numpy as np
from jax import lax
from jax.experimental import pallas as pl
from jax.experimental.pallas import tpu as pltpu
from jax.sharding import PartitionSpec as P

H = 128
BATCHES = 3
POS = 2
AXES = ("wide", "narrow")
F32 = jnp.float32
BF16 = jnp.bfloat16
VMEM_LIMIT = 32 * 1024 * 1024
VMEM_KERNEL = 24 * 1024 * 1024


def halves(table):
    high = table.astype(ml_dtypes.bfloat16)
    low = (table - high.astype(np.float64)).astype(ml_dtypes.bfloat16)
    return np.stack([high, low])


def dft_tables(size):
    half = size // 2
    k = np.arange(half)
    out = []
    for odd in range(2):
        phase = ((2 * k[:, None] + odd) * k[None, :]) % size
        angle = -2.0 * np.pi * phase / size
        re, im = np.cos(angle) / np.sqrt(size), np.sin(angle) / np.sqrt(size)
        out.append(np.block([[re, -im], [im, re]]))
    return np.stack([halves(t) for t in (out[0], out[1], out[0].T, out[1].T)])


def split(x):
    high = x.astype(BF16)
    return high, (x - high.astype(F32)).astype(BF16)


def dot(a, b):
    return jnp.dot(a, b, preferred_element_type=F32)


def left(tables, which, x):
    high, low = split(x)
    t_high, t_low = tables[which, 0], tables[which, 1]
    return dot(t_high, high) + dot(t_high, low) + dot(t_low, high)


def right(x, tables, which):
    high, low = split(x)
    t_high, t_low = tables[which, 0], tables[which, 1]
    return dot(high, t_high) + dot(low, t_high) + dot(high, t_low)


def forward(tables, re, im):
    h = re.shape[0] // 2
    u = jnp.concatenate([re[:h] + re[h:], im[:h] + im[h:]], 0)
    v = jnp.concatenate([re[:h] - re[h:], im[:h] - im[h:]], 0)
    even, odd = left(tables, 0, u), left(tables, 1, v)

    def columns(op):
        rows = [jnp.concatenate([op(y[:h, :h], y[:h, h:]), op(y[h:, :h], y[h:, h:])], 1) for y in (even, odd)]
        return jnp.concatenate(rows, 0)

    return (
        right(columns(lambda a, b: a + b), tables, 2),
        right(columns(lambda a, b: a - b), tables, 3),
    )


def inverse(tables, even, odd):
    h = even.shape[0] // 2
    a, b = right(even, tables, 0), right(odd, tables, 1)
    s, d = a + b, a - b

    def rows(lo):
        return jnp.concatenate(
            [
                jnp.concatenate([s[lo : lo + h, :h], d[lo : lo + h, :h]], 1),
                jnp.concatenate([s[lo : lo + h, h:], d[lo : lo + h, h:]], 1),
            ],
            0,
        )

    a, b = left(tables, 2, rows(0)), left(tables, 3, rows(h))
    s, d = a + b, a - b
    return jnp.concatenate([s[:h], d[:h]], 0), jnp.concatenate([s[h:], d[h:]], 0)


def power_of(z):
    h = z.shape[-1] // 2
    return z[:, :h] * z[:, :h] + z[:, h:] * z[:, h:]


def place_of(which, bit, h):
    return pl.multiple_of(jnp.where(bit == which, 0, h), h)


def rows_of(ref, bit):
    h = ref.shape[0] // 2
    return jnp.concatenate([ref[pl.ds(place_of(which, bit, h), h)] for which in range(2)], 0)


def add_rows(ref, base, bit, value):
    h = value.shape[0] // 2
    for which in range(2):
        ref[pl.ds(base + place_of(which, bit, h), h)] += value[which * h : (which + 1) * h]


def illuminated(tables, patch, probe):
    (p_re, p_im), (o_re, o_im) = probe, (patch[0, 0], patch[0, 1])
    return forward(tables, p_re * o_re - p_im * o_im, p_re * o_im + p_im * o_re)


def gradients(tables, patch, probe, spectrum, keep, pgrad, base, bit, gpatch):
    size = patch.shape[-1]
    k_even, k_odd = keep[0, 0], keep[0, 1]
    b_re, b_im = inverse(
        tables,
        spectrum[0] * jnp.concatenate([k_even, k_even], 1),
        spectrum[1] * jnp.concatenate([k_odd, k_odd], 1),
    )
    (p_re, p_im), (o_re, o_im) = probe, (patch[0, 0], patch[0, 1])
    gpatch[0, 0] += p_re * b_re + p_im * b_im
    gpatch[0, 1] += p_re * b_im - p_im * b_re
    add_rows(pgrad, base, bit, o_re * b_re + o_im * b_im)
    add_rows(pgrad, base + size, bit, o_re * b_im - o_im * b_re)


def whole(*shape):
    return pl.BlockSpec(shape, lambda i, *_: (0,) * len(shape))


def per_slot(*shape):
    return pl.BlockSpec((1, *shape), lambda i, *_: (i,) + (0,) * len(shape))


def per_batch_slot(batch, *shape):
    return pl.BlockSpec((1, *shape), lambda i, *_: (batch * POS + i,) + (0,) * len(shape))


def call(body, scalars, operands, in_specs, out_shapes, out_specs, grid, scratch=(), aliases=None, flops=0, moved=0):
    return pl.pallas_call(
        body,
        out_shape=[jax.ShapeDtypeStruct(s, F32) for s in out_shapes],
        grid_spec=pltpu.PrefetchScalarGridSpec(
            num_scalar_prefetch=len(scalars),
            grid=(grid,),
            in_specs=in_specs,
            out_specs=out_specs,
            scratch_shapes=list(scratch),
        ),
        input_output_aliases=aliases or {},
        compiler_params=pltpu.CompilerParams(vmem_limit_bytes=VMEM_LIMIT),
        cost_estimate=pl.CostEstimate(flops=flops, bytes_accessed=moved, transcendentals=0),
    )(*scalars, *operands)


def corner_of(offs, slot, full, size):
    row = offs[2 * slot] + H
    col = offs[2 * slot + 1] + H
    row_at = pl.multiple_of(jnp.minimum(row // 8 * 8, full - size - 8), 8)
    col_at = pl.multiple_of(jnp.minimum(col // 128 * 128, full - size - 128), 128)
    return row_at, col_at, row - row_at, col - col_at


def shift_in(block, row, col):
    rows, columns = block.shape
    turn = lax.rem(128 - col, 128)
    tiles = [pltpu.roll(block[:, at : at + 128], turn, 1) for at in range(0, columns, 128)]
    here = lax.broadcasted_iota(jnp.int32, (rows, 128), 1) < 128 - col
    block = jnp.concatenate([jnp.where(here, a, b) for a, b in zip(tiles, tiles[1:])], 1)
    block = pltpu.roll(block.reshape(rows // 8, 8, columns - 128), lax.rem(8 - row, 8), 1)
    here = lax.broadcasted_iota(jnp.int32, (rows // 8 - 1, 8, columns - 128), 1) < 8 - row
    return jnp.where(here, block[:-1], block[1:]).reshape(rows - 8, columns - 128)


def shift_out(block, row, col):
    rows, columns = block.shape
    block = pltpu.roll(block.reshape(rows // 8, 8, columns), lax.rem(row, 8), 1)
    zero = jnp.zeros((1, 8, columns), F32)
    here = lax.broadcasted_iota(jnp.int32, (rows // 8 + 1, 8, columns), 1) >= row
    block = jnp.where(here, jnp.concatenate([block, zero], 0), jnp.concatenate([zero, block], 0))
    block = block.reshape(rows + 8, columns)
    zero = jnp.zeros((rows + 8, 128), F32)
    tiles = [zero] + [pltpu.roll(block[:, at : at + 128], lax.rem(col, 128), 1) for at in range(0, columns, 128)] + [zero]
    here = lax.broadcasted_iota(jnp.int32, (rows + 8, 128), 1) >= col
    return jnp.concatenate([jnp.where(here, b, a) for a, b in zip(tiles, tiles[1:])], 1)


def cut_corners(left_side, right_side, after):
    edge = left_side.shape[1]

    def body(left_ref, right_ref, *rest):
        leading, last = rest[-2:]
        for ref, rows in ((leading, slice(0, H)), (last, slice(edge - H, edge))):
            ref[:, :, :H] = left_ref[:, rows]
            ref[:, :, H:] = right_ref[:, rows]

    return call(
        body,
        [],
        [left_side, right_side, *after],
        [whole(2, edge, H)] * 2 + [pl.BlockSpec(memory_space=pl.ANY)] * len(after),
        [(2, H, 2 * H)] * 2,
        [whole(2, H, 2 * H)] * 2,
        1,
        flops=10**5,
        moved=2 * 10**6,
    )


def cut_patches(offsets, info, tile, sides, size, slots):
    edge = tile.shape[1]
    full = edge + 2 * H
    low, mid, high = slice(0, H), slice(H, H + edge), slice(H + edge, full)
    first_half, second_half, everything = slice(0, H), slice(H, 2 * H), slice(None)
    pieces = [
        (0, everything, mid, mid),
        (1, everything, mid, low),
        (2, everything, mid, high),
        (3, everything, low, mid),
        (4, everything, high, mid),
        (5, first_half, low, low),
        (5, second_half, low, high),
        (6, first_half, high, low),
        (6, second_half, high, high),
    ]

    def body(offs, info_ref, *refs):
        sources, (out, cover, ext, sems) = refs[:7], refs[7:]
        i = pl.program_id(0)

        @pl.when(i == 0)
        def _():
            copies = [
                pltpu.make_async_copy(sources[k].at[:, :, part], ext.at[:, rows, columns], sems.at[j])
                for j, (k, part, rows, columns) in enumerate(pieces)
            ]
            for copy in copies:
                copy.start()
            cover[...] = jnp.zeros_like(cover)
            for copy in copies:
                copy.wait()

        @pl.when(i < info_ref[0])
        def _():
            row_at, col_at, row, col = corner_of(offs, i, full, size)
            total = jnp.zeros((1, size), F32)
            for part in range(2):
                block = shift_in(ext[part, pl.ds(row_at, size + 8), pl.ds(col_at, size + 128)], row, col)
                out[0, part] = block
                total = total + jnp.sum(block * block, axis=0, keepdims=True)
            here = lax.broadcasted_iota(jnp.int32, cover.shape, 0) == i // POS
            cover[...] += jnp.where(here, total, 0.0)

    return call(
        body,
        [offsets, info],
        [tile, *sides],
        [pl.BlockSpec(memory_space=pl.ANY)] * 7,
        [(slots, 2, size, size), (8, size)],
        [per_slot(2, size, size), whole(8, size)],
        slots,
        scratch=[pltpu.VMEM((2, full, full), F32), pltpu.SemaphoreType.DMA((len(pieces),))],
        flops=10**6,
        moved=8 * 10**6,
    )


def place_gradients(offsets, info, patches, after, edge):
    size = patches[0].shape[-1]
    full = edge + 2 * H
    n = len(patches)

    def body(offs, info_ref, *refs):
        patch_refs, (core, upper, lower, left_part, right_part, ext) = refs[:n], refs[n + len(after) :]
        i = pl.program_id(0)

        @pl.when(i == 0)
        def _():
            ext[...] = jnp.zeros_like(ext)

        for batch in range(n):

            @pl.when((i // POS == batch) & (i < info_ref[0]))
            def _():
                row_at, col_at, row, col = corner_of(offs, i, full, size)
                for part in range(2):
                    block = shift_out(patch_refs[batch][0, part], row, col)
                    ext[part, pl.ds(row_at, size + 8), pl.ds(col_at, size + 128)] += block

        @pl.when(i == n * POS - 1)
        def _():
            core[...] = ext[:, H : H + edge, H : H + edge]
            upper[...] = ext[:, :H]
            lower[...] = ext[:, H + edge :]
            left_part[...] = ext[:, H : H + edge, :H]
            right_part[...] = ext[:, H : H + edge, H + edge :]

    def spec(batch):
        return pl.BlockSpec((1, 2, size, size), lambda i, *_: (jnp.clip(i - batch * POS, 0, POS - 1), 0, 0, 0))

    shapes = [(2, edge, edge), (2, H, full), (2, H, full), (2, edge, H), (2, edge, H)]
    return call(
        body,
        [offsets, info],
        [*patches, *after],
        [spec(batch) for batch in range(n)] + [pl.BlockSpec(memory_space=pl.ANY)] * len(after),
        shapes,
        [whole(*shape) for shape in shapes],
        n * POS,
        scratch=[pltpu.VMEM((2, full, full), F32)],
        flops=10**6,
        moved=10**7,
    )


def side_borders(left_part, right_part, from_below, from_above, after):
    edge = left_part.shape[1]
    full = from_below.shape[2]

    def body(left_ref, right_ref, below, above, *rest):
        for ref, out, at in ((left_ref, rest[-2], 0), (right_ref, rest[-1], H + edge)):
            out[...] = ref[...]
            out[:, edge - H :] += below[:, :, at : at + H]
            out[:, :H] += above[:, :, at : at + H]

    return call(
        body,
        [],
        [left_part, right_part, from_below, from_above, *after],
        [whole(2, edge, H)] * 2 + [whole(2, H, full)] * 2 + [pl.BlockSpec(memory_space=pl.ANY)] * len(after),
        [(2, edge, H)] * 2,
        [whole(2, edge, H)] * 2,
        1,
        flops=10**5,
        moved=4 * 10**6,
    )


def call_in_vmem(body, info, operands, out_shapes, scratch=(), after=(), flops=0, moved=0):
    vmem = pl.BlockSpec(memory_space=pltpu.VMEM)
    return pl.pallas_call(
        body,
        out_shape=[pltpu.VMEM(s, F32) for s in out_shapes],
        in_specs=[pl.BlockSpec(memory_space=pltpu.SMEM)]
        + [vmem] * len(operands)
        + [pl.BlockSpec(memory_space=pl.ANY)] * len(after),
        out_specs=[vmem] * len(out_shapes),
        scratch_shapes=list(scratch),
        compiler_params=pltpu.CompilerParams(vmem_limit_bytes=VMEM_KERNEL),
        cost_estimate=pl.CostEstimate(flops=flops, bytes_accessed=moved, transcendentals=0),
    )(info, *[pltpu.with_memory_space_constraint(x, pltpu.VMEM) for x in operands], *after)


def turn_kernel(tables, info, patches, probes, roots, cover, batch):
    size = patches.shape[-1]
    h = size // 2
    rows = 4 * size
    extra = 0 if cover is None else cover.shape[0]

    def body(info_ref, t, patches_ref, roots_ref, *rest):
        p, rest = rest[:8], rest[8:]
        if extra:
            cover_ref, rest = rest[0], rest[1:]
        sent, keeps, gpatches, z, scratch = rest
        sent[:rows] = jnp.zeros((rows, size), F32)
        if extra:
            sent[rows:] = cover_ref[...]
        gpatches[...] = jnp.zeros_like(gpatches)
        for i in range(POS):
            slot = batch * POS + i
            patch, root = patches_ref.at[slot : slot + 1], roots_ref.at[slot : slot + 1]
            keep, gpatch = keeps.at[i : i + 1], gpatches.at[i : i + 1]

            @pl.when(slot < info_ref[0])
            def _():
                bits = [info_ref[2], info_ref[2], info_ref[1], info_ref[1]]
                totals = [0.0, 0.0]
                for m in range(4):
                    pair = illuminated(t, patch, (rows_of(p[2 * m], bits[m]), rows_of(p[2 * m + 1], bits[m])))
                    for e in range(2):
                        if m < 2:
                            z[i, m, e] = pair[e]
                        else:
                            scratch[m - 2, e] = pair[e]
                        totals[e] = totals[e] + power_of(pair[e])
                for e in range(2):
                    keep[0, e] = 1.0 - root[0, e] * lax.rsqrt(totals[e] + 0.1)
                for m in range(2, 4):
                    probe = (rows_of(p[2 * m], bits[m]), rows_of(p[2 * m + 1], bits[m]))
                    spectrum = (scratch[m - 2, 0], scratch[m - 2, 1])
                    gradients(t, patch, probe, spectrum, keep, sent, (m - 2) * 2 * size, bits[m], gpatch)

    return call_in_vmem(
        body,
        info,
        [tables, patches, roots, *probes] + ([cover] if extra else []),
        [(rows + extra, size), (POS, 2, size, h), (POS, 2, size, size), (POS, 2, 2, size, size)],
        scratch=[pltpu.VMEM((2, 2, size, size), F32)],
        flops=POS * 6 * 24 * size**3,
        moved=8 * 10**6,
    )


def back_kernel(tables, info, patches, probe, spectra, keeps, gpatches, batch, mode, after):
    size = patches.shape[-1]

    def body(info_ref, t, patches_ref, z, keeps_ref, g_in, p_re, p_im, *rest):
        pgrad, g_out = rest[len(after) :]
        pgrad[...] = jnp.zeros_like(pgrad)
        g_out[...] = g_in[...]
        for i in range(POS):
            slot = batch * POS + i
            patch, keep, gpatch = patches_ref.at[slot : slot + 1], keeps_ref.at[i : i + 1], g_out.at[i : i + 1]

            @pl.when(slot < info_ref[0])
            def _():
                bit = info_ref[2]
                pair = (rows_of(p_re, bit), rows_of(p_im, bit))
                gradients(t, patch, pair, (z[i, mode, 0], z[i, mode, 1]), keep, pgrad, 0, bit, gpatch)

    return call_in_vmem(
        body,
        info,
        [tables, patches, spectra, keeps, gpatches, *probe],
        [(2 * size, size), (POS, 2, size, size)],
        after=after,
        flops=POS * 24 * size**3,
        moved=4 * 10**6,
    )


def probe_kernel(info, probes):
    size = probes[0].shape[0]

    def body(info_ref, *refs):
        p, (probe_out, top, power) = refs[:8], refs[8:]
        i = pl.program_id(0)
        for m in range(4):

            @pl.when(i == m)
            def _():
                bit = info_ref[2] if m < 2 else info_ref[1]
                re, im = rows_of(p[2 * m], bit), rows_of(p[2 * m + 1], bit)
                probe_out[0, 0], probe_out[0, 1] = re, im
                square = re * re + im * im
                power[...] = square if m == 0 else power[...] + square

        @pl.when(i == 3)
        def _():
            top[...] = jnp.broadcast_to(jnp.max(power[...], keepdims=True), top.shape)

    return call(
        body,
        [info],
        probes,
        [whole(size, size)] * 8,
        [(4, 2, size, size), (8, 128)],
        [pl.BlockSpec((1, 2, size, size), lambda i, info_ref: (info_ref[3 + i], 0, 0, 0)), whole(8, 128)],
        4,
        scratch=[pltpu.VMEM((size, size), F32)],
        flops=10**6,
        moved=4 * 10**6,
    )


def object_kernel(top, field, core, from_right, from_left, from_below, from_above):
    edge = field.shape[1]
    full = from_below.shape[2]
    steps = edge // H

    def body(top_ref, o, g, fr, fl, fb, fa, out):
        i = pl.program_id(0)
        step = (0.5 / top_ref[:1, :1])[None]
        out[...] = o[...] - step * g[...]
        out[:, :, edge - H :] -= step * fr[...]
        out[:, :, :H] -= step * fl[...]

        @pl.when(i == steps - 1)
        def _():
            out[...] -= step * fb[:, :, H : H + edge]

        @pl.when(i == 0)
        def _():
            out[...] -= step * fa[:, :, H : H + edge]

    band = pl.BlockSpec((2, H, edge), lambda i: (0, i, 0))
    side = pl.BlockSpec((2, H, H), lambda i: (0, i, 0))
    return call(
        body,
        [],
        [top, field, core, from_right, from_left, from_below, from_above],
        [whole(8, 128), band, band, side, side, whole(2, H, full), whole(2, H, full)],
        [field.shape],
        [band],
        steps,
        flops=10**6,
        moved=8 * 10**6,
    )[0]


def flips(wide, narrow):
    bits = [(0, 2 << i) for i in range(1, narrow.bit_length() - 2)] + [
        (1 << i, 0) for i in range(1, wide.bit_length() - 1)
    ]

    def exchange(even, odd):
        pairs = []
        for w in range(wide):
            for n in range(narrow):
                dw, dn = odd if n & 1 else even
                pairs.append((w * narrow + n, (w ^ dw) * narrow + (n ^ dn)))
        return functools.partial(lax.ppermute, axis_name=AXES, perm=pairs)

    core = exchange((0, 1), (0, 1))
    first = exchange((0, 2), (1, 0))
    second = exchange((1, 0), (0, 2))
    return core, first, second, [exchange(a, b) for a, b in zip(bits, bits[::-1])]


def shifted(value, axis, steps):
    count = lax.axis_size(axis)
    leading, last = (max(0, -steps), min(count, count - steps))
    return lax.ppermute(value, axis, [(source, source + steps) for source in range(leading, last)])


def local(object_field, probe, patterns, offsets, counts):
    edge = object_field.shape[1]
    size = probe.shape[-1]
    slots = patterns.shape[2]
    h = size // 2
    wide, narrow = lax.axis_size("wide"), lax.axis_size("narrow")
    w, n = lax.axis_index("wide"), lax.axis_index("narrow")
    core, first, second, rest = flips(wide, narrow)
    offs = offsets.reshape(slots * 2)

    left_side = shifted(object_field[:, :, edge - H :], "wide", 1)
    right_side = shifted(object_field[:, :, :H], "wide", -1)
    top_side = shifted(object_field[:, edge - H :], "narrow", 1)
    bottom_side = shifted(object_field[:, :H], "narrow", -1)

    tables = jnp.asarray(dft_tables(size))
    order = np.concatenate([np.arange(0, size, 2), np.arange(1, size, 2)])
    pick = jnp.asarray(np.eye(size, dtype=np.float32)[order])
    roots = jnp.einsum("pj,sjk->spk", pick, jnp.sqrt(patterns[0, 0]), precision=lax.Precision.HIGHEST)
    roots = jnp.einsum("spk,qk->spq", roots, pick, precision=lax.Precision.HIGHEST)
    roots = roots.reshape(slots, size, 2, h).transpose(0, 2, 1, 3)

    c = n % 2
    bit_n, bit_w = (n // 2) % 2, w % 2
    b1 = jnp.where(c == 0, bit_n, bit_w)
    b2 = jnp.where(c == 0, bit_w, bit_n)
    ours, theirs = 2 * c, 2 * (1 - c)
    order_of = [ours + b1, ours + 1 - b1, theirs + b2, theirs + 1 - b2]
    info = jnp.stack([counts[0, 0], b1, b2, *order_of]).astype(jnp.int32)
    split_rows = probe.reshape(4, 2, 2, h, size)
    probes = []
    for m, bit in zip(order_of, (b2, b2, b1, b1)):
        for part in range(2):
            mine = lax.dynamic_slice(split_rows, (m, part, bit, 0, 0), (1, 1, 1, h, size))
            other = lax.dynamic_slice(split_rows, (m, part, 1 - bit, 0, 0), (1, 1, 1, h, size))
            probes.append(jnp.concatenate([mine.reshape(h, size), other.reshape(h, size)], 0))

    leading, last = cut_corners(left_side, right_side, (roots, *probes))
    top_corners = shifted(last, "narrow", 1)
    bottom_corners = shifted(leading, "narrow", -1)
    sides = (left_side, right_side, top_side, bottom_side, top_corners, bottom_corners)
    patches, cover = cut_patches(offs, info, object_field, sides, size, slots)

    patch_gradients = []
    for batch in range(BATCHES):
        extra = cover if batch == 0 else None

        def ride(x):
            return x if extra is None else jnp.concatenate([x, extra], 0)

        sent, keep, gpatch, z = turn_kernel(tables, info, patches, probes, roots, extra, batch)
        got = core(sent)
        g1, gpatch = back_kernel(tables, info, patches, probes[2:4], z, keep, gpatch, batch, 1, ())
        if extra is not None:
            extra = extra + got[4 * size :]
        sent_a = g1[:size] + got[2 * size : 3 * size]
        sent_b = g1[size:] + got[3 * size : 4 * size]
        got_a = first(ride(sent_a))
        got_b = first(sent_b)
        g0, gpatch = back_kernel(tables, info, patches, probes[:2], z, keep, gpatch, batch, 0, (sent_a, sent_b))
        patch_gradients.append(gpatch)
        sent_a = g0[h:size] + got[h:size] + got_a[h:size]
        sent_b = g0[size + h :] + got[size + h : 2 * size] + got_b[h:]
        a = g0[:h] + got[:h] + got_a[:h]
        b = g0[size : size + h] + got[size : size + h] + got_b[:h]
        if extra is not None:
            extra = extra + got_a[size:]
        got_a = second(ride(sent_a))
        got_b = second(sent_b)
        a = a + got_a[:h]
        b = b + got_b
        if extra is not None:
            extra = extra + got_a[h:]
        if batch == BATCHES - 1:
            inside, upper, lower, left_part, right_part = place_gradients(offs, info, patch_gradients, (a, b), edge)
            from_below = shifted(upper, "narrow", -1)
            from_above = shifted(lower, "narrow", 1)
        for exchange in rest:
            got_a = exchange(ride(a))
            got_b = exchange(b)
            a = a + got_a[:h]
            b = b + got_b
            if extra is not None:
                extra = extra + got_a[h:]
        if extra is not None:
            scales = jnp.sum(extra, axis=1) / (size * size)
        a = probes[0][:h] - a / scales[batch]
        b = probes[1][:h] - b / scales[batch]
        a = jnp.concatenate([a, second(a)], 0)
        b = jnp.concatenate([b, second(b)], 0)
        own = [a, b, first(a), first(b)]
        probes = own + [core(x) for x in own]

    to_left, to_right = side_borders(left_part, right_part, from_below, from_above, own[2:])
    from_right = shifted(to_left, "wide", -1)
    from_left = shifted(to_right, "wide", 1)
    probe_new, top = probe_kernel(info, probes)
    object_new = object_kernel(top, object_field, inside, from_right, from_left, from_below, from_above)
    return (object_new, probe_new)


def solution(mesh):
    placed = (
        P(None, "narrow", "wide"),
        P(),
        P("narrow", "wide", None, None, None),
        P("narrow", "wide", None, None),
        P("narrow", "wide"),
    )
    return jax.shard_map(
        local,
        mesh=mesh,
        in_specs=placed,
        out_specs=(P(None, "narrow", "wide"), P()),
        check_vma=False,
    )
```

```python
import functools

import jax
import jax.numpy as jnp
import ml_dtypes
import numpy as np
from jax import lax
from jax.experimental import pallas as pl
from jax.experimental.pallas import tpu as pltpu
from jax.sharding import PartitionSpec as P

H = 128
BATCHES = 3
POS = 2
AXES = ("wide", "narrow")
F32 = jnp.float32
BF16 = jnp.bfloat16
VMEM_LIMIT = 32 * 1024 * 1024
VMEM_KERNEL = 24 * 1024 * 1024


def halves(table):
    high = table.astype(ml_dtypes.bfloat16)
    low = (table - high.astype(np.float64)).astype(ml_dtypes.bfloat16)
    return np.stack([high, low])


def dft_tables(size):
    half = size // 2
    k = np.arange(half)
    out = []
    for odd in range(2):
        phase = ((2 * k[:, None] + odd) * k[None, :]) % size
        angle = -2.0 * np.pi * phase / size
        re, im = np.cos(angle) / np.sqrt(size), np.sin(angle) / np.sqrt(size)
        out.append(np.block([[re, -im], [im, re]]))
    return np.stack([halves(t) for t in (out[0], out[1], out[0].T, out[1].T)])


def split(x):
    high = x.astype(BF16)
    return high, (x - high.astype(F32)).astype(BF16)


def dot(a, b):
    return jnp.dot(a, b, preferred_element_type=F32)


def left(tables, which, x):
    high, low = split(x)
    t_high, t_low = tables[which, 0], tables[which, 1]
    return dot(t_high, high) + dot(t_high, low) + dot(t_low, high)


def right(x, tables, which):
    high, low = split(x)
    t_high, t_low = tables[which, 0], tables[which, 1]
    return dot(high, t_high) + dot(low, t_high) + dot(high, t_low)


def forward(tables, re, im):
    h = re.shape[0] // 2
    u = jnp.concatenate([re[:h] + re[h:], im[:h] + im[h:]], 0)
    v = jnp.concatenate([re[:h] - re[h:], im[:h] - im[h:]], 0)
    even, odd = left(tables, 0, u), left(tables, 1, v)

    def columns(op):
        rows = [jnp.concatenate([op(y[:h, :h], y[:h, h:]), op(y[h:, :h], y[h:, h:])], 1) for y in (even, odd)]
        return jnp.concatenate(rows, 0)

    return (
        right(columns(lambda a, b: a + b), tables, 2),
        right(columns(lambda a, b: a - b), tables, 3),
    )


def inverse(tables, even, odd):
    h = even.shape[0] // 2
    a, b = right(even, tables, 0), right(odd, tables, 1)
    s, d = a + b, a - b

    def rows(lo):
        return jnp.concatenate(
            [
                jnp.concatenate([s[lo : lo + h, :h], d[lo : lo + h, :h]], 1),
                jnp.concatenate([s[lo : lo + h, h:], d[lo : lo + h, h:]], 1),
            ],
            0,
        )

    a, b = left(tables, 2, rows(0)), left(tables, 3, rows(h))
    s, d = a + b, a - b
    return jnp.concatenate([s[:h], d[:h]], 0), jnp.concatenate([s[h:], d[h:]], 0)


def power_of(z):
    h = z.shape[-1] // 2
    return z[:, :h] * z[:, :h] + z[:, h:] * z[:, h:]


def place_of(which, bit, h):
    return pl.multiple_of(jnp.where(bit == which, 0, h), h)


def rows_of(ref, bit):
    h = ref.shape[0] // 2
    return jnp.concatenate([ref[pl.ds(place_of(which, bit, h), h)] for which in range(2)], 0)


def add_rows(ref, base, bit, value):
    h = value.shape[0] // 2
    for which in range(2):
        ref[pl.ds(base + place_of(which, bit, h), h)] += value[which * h : (which + 1) * h]


def illuminated(tables, patch, probe):
    (p_re, p_im), (o_re, o_im) = probe, (patch[0, 0], patch[0, 1])
    return forward(tables, p_re * o_re - p_im * o_im, p_re * o_im + p_im * o_re)


def gradients(tables, patch, probe, spectrum, keep, pgrad, base, bit, gpatch):
    size = patch.shape[-1]
    k_even, k_odd = keep[0, 0], keep[0, 1]
    b_re, b_im = inverse(
        tables,
        spectrum[0] * jnp.concatenate([k_even, k_even], 1),
        spectrum[1] * jnp.concatenate([k_odd, k_odd], 1),
    )
    (p_re, p_im), (o_re, o_im) = probe, (patch[0, 0], patch[0, 1])
    gpatch[0, 0] += p_re * b_re + p_im * b_im
    gpatch[0, 1] += p_re * b_im - p_im * b_re
    add_rows(pgrad, base, bit, o_re * b_re + o_im * b_im)
    add_rows(pgrad, base + size, bit, o_re * b_im - o_im * b_re)


def whole(*shape):
    return pl.BlockSpec(shape, lambda i, *_: (0,) * len(shape))


def per_slot(*shape):
    return pl.BlockSpec((1, *shape), lambda i, *_: (i,) + (0,) * len(shape))


def per_batch_slot(batch, *shape):
    return pl.BlockSpec((1, *shape), lambda i, *_: (batch * POS + i,) + (0,) * len(shape))


def call(body, scalars, operands, in_specs, out_shapes, out_specs, grid, scratch=(), aliases=None, flops=0, moved=0):
    return pl.pallas_call(
        body,
        out_shape=[jax.ShapeDtypeStruct(s, F32) for s in out_shapes],
        grid_spec=pltpu.PrefetchScalarGridSpec(
            num_scalar_prefetch=len(scalars),
            grid=(grid,),
            in_specs=in_specs,
            out_specs=out_specs,
            scratch_shapes=list(scratch),
        ),
        input_output_aliases=aliases or {},
        compiler_params=pltpu.CompilerParams(vmem_limit_bytes=VMEM_LIMIT),
        cost_estimate=pl.CostEstimate(flops=flops, bytes_accessed=moved, transcendentals=0),
    )(*scalars, *operands)


def corner_of(offs, slot, full, size):
    row = offs[2 * slot] + H
    col = offs[2 * slot + 1] + H
    row_at = pl.multiple_of(jnp.minimum(row // 8 * 8, full - size - 8), 8)
    col_at = pl.multiple_of(jnp.minimum(col // 128 * 128, full - size - 128), 128)
    return row_at, col_at, row - row_at, col - col_at


def shift_in(block, row, col):
    rows, columns = block.shape
    turn = lax.rem(128 - col, 128)
    tiles = [pltpu.roll(block[:, at : at + 128], turn, 1) for at in range(0, columns, 128)]
    here = lax.broadcasted_iota(jnp.int32, (rows, 128), 1) < 128 - col
    block = jnp.concatenate([jnp.where(here, a, b) for a, b in zip(tiles, tiles[1:])], 1)
    block = pltpu.roll(block.reshape(rows // 8, 8, columns - 128), lax.rem(8 - row, 8), 1)
    here = lax.broadcasted_iota(jnp.int32, (rows // 8 - 1, 8, columns - 128), 1) < 8 - row
    return jnp.where(here, block[:-1], block[1:]).reshape(rows - 8, columns - 128)


def shift_out(block, row, col):
    rows, columns = block.shape
    block = pltpu.roll(block.reshape(rows // 8, 8, columns), lax.rem(row, 8), 1)
    zero = jnp.zeros((1, 8, columns), F32)
    here = lax.broadcasted_iota(jnp.int32, (rows // 8 + 1, 8, columns), 1) >= row
    block = jnp.where(here, jnp.concatenate([block, zero], 0), jnp.concatenate([zero, block], 0))
    block = block.reshape(rows + 8, columns)
    zero = jnp.zeros((rows + 8, 128), F32)
    tiles = [zero] + [pltpu.roll(block[:, at : at + 128], lax.rem(col, 128), 1) for at in range(0, columns, 128)] + [zero]
    here = lax.broadcasted_iota(jnp.int32, (rows + 8, 128), 1) >= col
    return jnp.concatenate([jnp.where(here, b, a) for a, b in zip(tiles, tiles[1:])], 1)


def cut_corners(left_side, right_side, after):
    edge = left_side.shape[1]
    bands = [pl.BlockSpec((2, H, H), lambda i, at=at: (0, at, 0)) for at in (0, 0, edge // H - 1, edge // H - 1)]

    def body(left_first, right_first, left_last, right_last, *rest):
        for ref, left_ref, right_ref in ((rest[-2], left_first, right_first), (rest[-1], left_last, right_last)):
            ref[:, :, :H] = left_ref[...]
            ref[:, :, H:] = right_ref[...]

    return call(
        body,
        [],
        [left_side, right_side, left_side, right_side, *after],
        bands + [pl.BlockSpec(memory_space=pl.ANY)] * len(after),
        [(2, H, 2 * H)] * 2,
        [whole(2, H, 2 * H)] * 2,
        1,
        flops=10**5,
        moved=2 * 10**6,
    )


def cut_patches(offsets, info, tile, sides, size, slots):
    edge = tile.shape[1]
    full = edge + 2 * H
    low, mid, high = slice(0, H), slice(H, H + edge), slice(H + edge, full)
    first_half, second_half, everything = slice(0, H), slice(H, 2 * H), slice(None)
    pieces = [
        (0, everything, mid, mid),
        (1, everything, mid, low),
        (2, everything, mid, high),
        (3, everything, low, mid),
        (4, everything, high, mid),
        (5, first_half, low, low),
        (5, second_half, low, high),
        (6, first_half, high, low),
        (6, second_half, high, high),
    ]

    def body(offs, info_ref, *refs):
        sources, (out, cover, ext, sems) = refs[:7], refs[7:]
        i = pl.program_id(0)

        @pl.when(i == 0)
        def _():
            copies = [
                pltpu.make_async_copy(sources[k].at[:, :, part], ext.at[:, rows, columns], sems.at[j])
                for j, (k, part, rows, columns) in enumerate(pieces)
            ]
            for copy in copies:
                copy.start()
            cover[...] = jnp.zeros_like(cover)
            for copy in copies:
                copy.wait()

        @pl.when(i < info_ref[0])
        def _():
            row_at, col_at, row, col = corner_of(offs, i, full, size)
            total = jnp.zeros((1, size), F32)
            for part in range(2):
                block = shift_in(ext[part, pl.ds(row_at, size + 8), pl.ds(col_at, size + 128)], row, col)
                out[0, part] = block
                total = total + jnp.sum(block * block, axis=0, keepdims=True)
            here = lax.broadcasted_iota(jnp.int32, cover.shape, 0) == i // POS
            cover[...] += jnp.where(here, total, 0.0)

    return call(
        body,
        [offsets, info],
        [tile, *sides],
        [pl.BlockSpec(memory_space=pl.ANY)] * 7,
        [(slots, 2, size, size), (8, size)],
        [per_slot(2, size, size), whole(8, size)],
        slots,
        scratch=[pltpu.VMEM((2, full, full), F32), pltpu.SemaphoreType.DMA((len(pieces),))],
        flops=10**6,
        moved=8 * 10**6,
    )


def place_gradients(offsets, info, patches, after, edge):
    size = patches[0].shape[-1]
    full = edge + 2 * H
    n = len(patches)

    def body(offs, info_ref, *refs):
        patch_refs, (core, upper, lower, left_part, right_part, ext) = refs[:n], refs[n + len(after) :]
        i = pl.program_id(0)

        @pl.when(i == 0)
        def _():
            ext[...] = jnp.zeros_like(ext)

        for batch in range(n):

            @pl.when((i // POS == batch) & (i < info_ref[0]))
            def _():
                row_at, col_at, row, col = corner_of(offs, i, full, size)
                for part in range(2):
                    block = shift_out(patch_refs[batch][0, part], row, col)
                    ext[part, pl.ds(row_at, size + 8), pl.ds(col_at, size + 128)] += block

        @pl.when(i == n * POS - 1)
        def _():
            core[...] = ext[:, H : H + edge, H : H + edge]
            upper[...] = ext[:, :H]
            lower[...] = ext[:, H + edge :]
            left_part[...] = ext[:, H : H + edge, :H]
            right_part[...] = ext[:, H : H + edge, H + edge :]

    def spec(batch):
        return pl.BlockSpec((1, 2, size, size), lambda i, *_: (jnp.clip(i - batch * POS, 0, POS - 1), 0, 0, 0))

    shapes = [(2, edge, edge), (2, H, full), (2, H, full), (2, edge, H), (2, edge, H)]
    return call(
        body,
        [offsets, info],
        [*patches, *after],
        [spec(batch) for batch in range(n)] + [pl.BlockSpec(memory_space=pl.ANY)] * len(after),
        shapes,
        [whole(*shape) for shape in shapes],
        n * POS,
        scratch=[pltpu.VMEM((2, full, full), F32)],
        flops=10**6,
        moved=10**7,
    )


def side_borders(left_part, right_part, from_below, from_above, after):
    edge = left_part.shape[1]
    full = from_below.shape[2]

    def body(left_ref, right_ref, below, above, *rest):
        for ref, out, at in ((left_ref, rest[-2], 0), (right_ref, rest[-1], H + edge)):
            out[...] = ref[...]
            out[:, edge - H :] += below[:, :, at : at + H]
            out[:, :H] += above[:, :, at : at + H]

    return call(
        body,
        [],
        [left_part, right_part, from_below, from_above, *after],
        [whole(2, edge, H)] * 2 + [whole(2, H, full)] * 2 + [pl.BlockSpec(memory_space=pl.ANY)] * len(after),
        [(2, edge, H)] * 2,
        [whole(2, edge, H)] * 2,
        1,
        flops=10**5,
        moved=4 * 10**6,
    )


def call_in_vmem(body, info, operands, out_shapes, scratch=(), after=(), flops=0, moved=0):
    vmem = pl.BlockSpec(memory_space=pltpu.VMEM)
    return pl.pallas_call(
        body,
        out_shape=[pltpu.VMEM(s, F32) for s in out_shapes],
        in_specs=[pl.BlockSpec(memory_space=pltpu.SMEM)]
        + [vmem] * len(operands)
        + [pl.BlockSpec(memory_space=pl.ANY)] * len(after),
        out_specs=[vmem] * len(out_shapes),
        scratch_shapes=list(scratch),
        compiler_params=pltpu.CompilerParams(vmem_limit_bytes=VMEM_KERNEL),
        cost_estimate=pl.CostEstimate(flops=flops, bytes_accessed=moved, transcendentals=0),
    )(info, *[pltpu.with_memory_space_constraint(x, pltpu.VMEM) for x in operands], *after)


def turn_kernel(tables, info, patches, probes, roots, cover, batch):
    size = patches.shape[-1]
    h = size // 2
    rows = 4 * size
    extra = 0 if cover is None else cover.shape[0]

    def body(info_ref, t, patches_ref, roots_ref, *rest):
        p, rest = rest[:8], rest[8:]
        if extra:
            cover_ref, rest = rest[0], rest[1:]
        sent, keeps, gpatches, z, scratch = rest
        sent[:rows] = jnp.zeros((rows, size), F32)
        if extra:
            sent[rows:] = cover_ref[...]
        gpatches[...] = jnp.zeros_like(gpatches)
        for i in range(POS):
            slot = batch * POS + i
            patch, root = patches_ref.at[slot : slot + 1], roots_ref.at[slot : slot + 1]
            keep, gpatch = keeps.at[i : i + 1], gpatches.at[i : i + 1]

            @pl.when(slot < info_ref[0])
            def _():
                bits = [info_ref[2], info_ref[2], info_ref[1], info_ref[1]]
                totals = [0.0, 0.0]
                for m in range(4):
                    pair = illuminated(t, patch, (rows_of(p[2 * m], bits[m]), rows_of(p[2 * m + 1], bits[m])))
                    for e in range(2):
                        if m < 2:
                            z[i, m, e] = pair[e]
                        else:
                            scratch[m - 2, e] = pair[e]
                        totals[e] = totals[e] + power_of(pair[e])
                for e in range(2):
                    keep[0, e] = 1.0 - root[0, e] * lax.rsqrt(totals[e] + 0.1)
                for m in range(2, 4):
                    probe = (rows_of(p[2 * m], bits[m]), rows_of(p[2 * m + 1], bits[m]))
                    spectrum = (scratch[m - 2, 0], scratch[m - 2, 1])
                    gradients(t, patch, probe, spectrum, keep, sent, (m - 2) * 2 * size, bits[m], gpatch)

    return call_in_vmem(
        body,
        info,
        [tables, patches, roots, *probes] + ([cover] if extra else []),
        [(rows + extra, size), (POS, 2, size, h), (POS, 2, size, size), (POS, 2, 2, size, size)],
        scratch=[pltpu.VMEM((2, 2, size, size), F32)],
        flops=POS * 6 * 24 * size**3,
        moved=8 * 10**6,
    )


def back_kernel(tables, info, patches, probe, spectra, keeps, gpatches, batch, mode, start, after):
    size = patches.shape[-1]
    h = size // 2

    def body(info_ref, t, patches_ref, z, keeps_ref, g_in, p_re, p_im, *rest):
        quarters, g_out, pgrad = rest[-6:-2], rest[-2], rest[-1]
        if start:
            pgrad[...] = rest[0][: 2 * size]
        else:
            pgrad[...] = jnp.zeros_like(pgrad)
        g_out[...] = g_in[...]
        for i in range(POS):
            slot = batch * POS + i
            patch, keep, gpatch = patches_ref.at[slot : slot + 1], keeps_ref.at[i : i + 1], g_out.at[i : i + 1]

            @pl.when(slot < info_ref[0])
            def _():
                bit = info_ref[2]
                pair = (rows_of(p_re, bit), rows_of(p_im, bit))
                gradients(t, patch, pair, (z[i, mode, 0], z[i, mode, 1]), keep, pgrad, 0, bit, gpatch)

        for at, out in enumerate(quarters):
            out[...] = pgrad[at * h : (at + 1) * h]

    return call_in_vmem(
        body,
        info,
        [tables, patches, spectra, keeps, gpatches, *probe, *start],
        [(h, size)] * 4 + [(POS, 2, size, size)],
        scratch=[pltpu.VMEM((2 * size, size), F32)],
        after=after,
        flops=POS * 24 * size**3,
        moved=4 * 10**6,
    )


def probe_kernel(info, probes):
    size = probes[0].shape[0]

    def body(info_ref, *refs):
        p, (probe_out, top, power) = refs[:8], refs[8:]
        i = pl.program_id(0)
        for m in range(4):

            @pl.when(i == m)
            def _():
                bit = info_ref[2] if m < 2 else info_ref[1]
                re, im = rows_of(p[2 * m], bit), rows_of(p[2 * m + 1], bit)
                probe_out[0, 0], probe_out[0, 1] = re, im
                square = re * re + im * im
                power[...] = square if m == 0 else power[...] + square

        @pl.when(i == 3)
        def _():
            top[...] = jnp.broadcast_to(jnp.max(power[...], keepdims=True), top.shape)

    return call(
        body,
        [info],
        probes,
        [whole(size, size)] * 8,
        [(4, 2, size, size), (8, 128)],
        [pl.BlockSpec((1, 2, size, size), lambda i, info_ref: (info_ref[3 + i], 0, 0, 0)), whole(8, 128)],
        4,
        scratch=[pltpu.VMEM((size, size), F32)],
        flops=10**6,
        moved=4 * 10**6,
    )


def object_kernel(top, field, core, from_right, from_left, from_below, from_above):
    edge = field.shape[1]
    full = from_below.shape[2]
    steps = edge // H

    def body(top_ref, o, g, fr, fl, fb, fa, out):
        i = pl.program_id(0)
        step = (0.5 / top_ref[:1, :1])[None]
        out[...] = o[...] - step * g[...]
        out[:, :, edge - H :] -= step * fr[...]
        out[:, :, :H] -= step * fl[...]

        @pl.when(i == steps - 1)
        def _():
            out[...] -= step * fb[:, :, H : H + edge]

        @pl.when(i == 0)
        def _():
            out[...] -= step * fa[:, :, H : H + edge]

    band = pl.BlockSpec((2, H, edge), lambda i: (0, i, 0))
    side = pl.BlockSpec((2, H, H), lambda i: (0, i, 0))
    return call(
        body,
        [],
        [top, field, core, from_right, from_left, from_below, from_above],
        [whole(8, 128), band, band, side, side, whole(2, H, full), whole(2, H, full)],
        [field.shape],
        [band],
        steps,
        flops=10**6,
        moved=8 * 10**6,
    )[0]


def flips(wide, narrow):
    bits = [(0, 2 << i) for i in range(1, narrow.bit_length() - 2)] + [
        (1 << i, 0) for i in range(1, wide.bit_length() - 1)
    ]

    def exchange(even, odd):
        pairs = []
        for w in range(wide):
            for n in range(narrow):
                dw, dn = odd if n & 1 else even
                pairs.append((w * narrow + n, (w ^ dw) * narrow + (n ^ dn)))
        return functools.partial(lax.ppermute, axis_name=AXES, perm=pairs)

    core = exchange((0, 1), (0, 1))
    first = exchange((0, 2), (1, 0))
    second = exchange((1, 0), (0, 2))
    return core, first, second, [exchange(a, b) for a, b in zip(bits, bits[::-1])]


def shifted(value, axis, steps):
    count = lax.axis_size(axis)
    leading, last = (max(0, -steps), min(count, count - steps))
    return lax.ppermute(value, axis, [(source, source + steps) for source in range(leading, last)])


def local(object_field, probe, patterns, offsets, counts):
    edge = object_field.shape[1]
    size = probe.shape[-1]
    slots = patterns.shape[2]
    h = size // 2
    wide, narrow = lax.axis_size("wide"), lax.axis_size("narrow")
    w, n = lax.axis_index("wide"), lax.axis_index("narrow")
    core, first, second, rest = flips(wide, narrow)
    offs = offsets.reshape(slots * 2)

    left_side = shifted(object_field[:, :, edge - H :], "wide", 1)
    right_side = shifted(object_field[:, :, :H], "wide", -1)
    top_side = shifted(object_field[:, edge - H :], "narrow", 1)
    bottom_side = shifted(object_field[:, :H], "narrow", -1)

    tables = jnp.asarray(dft_tables(size))
    order = np.concatenate([np.arange(0, size, 2), np.arange(1, size, 2)])
    pick = jnp.asarray(np.eye(size, dtype=np.float32)[order])
    roots = jnp.einsum("pj,sjk->spk", pick, jnp.sqrt(patterns[0, 0]), precision=lax.Precision.HIGHEST)
    roots = jnp.einsum("spk,qk->spq", roots, pick, precision=lax.Precision.HIGHEST)
    roots = roots.reshape(slots, size, 2, h).transpose(0, 2, 1, 3)

    c = n % 2
    bit_n, bit_w = (n // 2) % 2, w % 2
    b1 = jnp.where(c == 0, bit_n, bit_w)
    b2 = jnp.where(c == 0, bit_w, bit_n)
    ours, theirs = 2 * c, 2 * (1 - c)
    order_of = [ours + b1, ours + 1 - b1, theirs + b2, theirs + 1 - b2]
    info = jnp.stack([counts[0, 0], b1, b2, *order_of]).astype(jnp.int32)
    split_rows = probe.reshape(4, 2, 2, h, size)
    probes = []
    for m, bit in zip(order_of, (b2, b2, b1, b1)):
        for part in range(2):
            mine = lax.dynamic_slice(split_rows, (m, part, bit, 0, 0), (1, 1, 1, h, size))
            other = lax.dynamic_slice(split_rows, (m, part, 1 - bit, 0, 0), (1, 1, 1, h, size))
            probes.append(jnp.concatenate([mine.reshape(h, size), other.reshape(h, size)], 0))

    leading, last = cut_corners(left_side, right_side, (roots, *probes))
    top_corners = shifted(last, "narrow", 1)
    bottom_corners = shifted(leading, "narrow", -1)
    sides = (left_side, right_side, top_side, bottom_side, top_corners, bottom_corners)
    patches, cover = cut_patches(offs, info, object_field, sides, size, slots)

    patch_gradients = []
    for batch in range(BATCHES):
        extra = cover if batch == 0 else None

        def ride(x):
            return x if extra is None else jnp.concatenate([x, extra], 0)

        sent, keep, gpatch, z = turn_kernel(tables, info, patches, probes, roots, extra, batch)
        got = core(sent)
        *q, gpatch = back_kernel(tables, info, patches, probes[2:4], z, keep, gpatch, batch, 1, (), ())
        if extra is not None:
            extra = extra + got[4 * size :]
        sent_a = jnp.concatenate([q[0], q[1]], 0) + got[2 * size : 3 * size]
        sent_b = jnp.concatenate([q[2], q[3]], 0) + got[3 * size : 4 * size]
        got_a = first(ride(sent_a))
        got_b = first(sent_b)
        after = (sent_a, sent_b)
        *q, gpatch = back_kernel(tables, info, patches, probes[:2], z, keep, gpatch, batch, 0, (got,), after)
        patch_gradients.append(gpatch)
        sent_a = q[1] + got_a[h:size]
        sent_b = q[3] + got_b[h:]
        a = q[0] + got_a[:h]
        b = q[2] + got_b[:h]
        if extra is not None:
            extra = extra + got_a[size:]
        got_a = second(ride(sent_a))
        got_b = second(sent_b)
        a = a + got_a[:h]
        b = b + got_b
        if extra is not None:
            extra = extra + got_a[h:]
        if batch == BATCHES - 1:
            inside, upper, lower, left_part, right_part = place_gradients(offs, info, patch_gradients, (a, b), edge)
            from_below = shifted(upper, "narrow", -1)
            from_above = shifted(lower, "narrow", 1)
        for exchange in rest:
            got_a = exchange(ride(a))
            got_b = exchange(b)
            a = a + got_a[:h]
            b = b + got_b
            if extra is not None:
                extra = extra + got_a[h:]
        if extra is not None:
            scales = jnp.sum(extra, axis=1) / (size * size)
        a = probes[0][:h] - a / scales[batch]
        b = probes[1][:h] - b / scales[batch]
        a = jnp.concatenate([a, second(a)], 0)
        b = jnp.concatenate([b, second(b)], 0)
        own = [a, b, first(a), first(b)]
        probes = own + [core(x) for x in own]

    to_left, to_right = side_borders(left_part, right_part, from_below, from_above, own[2:])
    from_right = shifted(to_left, "wide", -1)
    from_left = shifted(to_right, "wide", 1)
    probe_new, top = probe_kernel(info, probes)
    object_new = object_kernel(top, object_field, inside, from_right, from_left, from_below, from_above)
    return (object_new, probe_new)


def solution(mesh):
    placed = (
        P(None, "narrow", "wide"),
        P(),
        P("narrow", "wide", None, None, None),
        P("narrow", "wide", None, None),
        P("narrow", "wide"),
    )
    return jax.shard_map(
        local,
        mesh=mesh,
        in_specs=placed,
        out_specs=(P(None, "narrow", "wide"), P()),
        check_vma=False,
    )
```

```python
import functools

import jax
import jax.numpy as jnp
import ml_dtypes
import numpy as np
from jax import lax
from jax.experimental import pallas as pl
from jax.experimental.pallas import tpu as pltpu
from jax.sharding import PartitionSpec as P

H = 128
BATCHES = 3
POS = 2
AXES = ("wide", "narrow")
F32 = jnp.float32
BF16 = jnp.bfloat16
VMEM_LIMIT = 32 * 1024 * 1024
VMEM_KERNEL = 24 * 1024 * 1024


def halves(table):
    high = table.astype(ml_dtypes.bfloat16)
    low = (table - high.astype(np.float64)).astype(ml_dtypes.bfloat16)
    return np.stack([high, low])


def dft_tables(size):
    half = size // 2
    k = np.arange(half)
    out = []
    for odd in range(2):
        phase = ((2 * k[:, None] + odd) * k[None, :]) % size
        angle = -2.0 * np.pi * phase / size
        re, im = np.cos(angle) / np.sqrt(size), np.sin(angle) / np.sqrt(size)
        out.append(np.block([[re, -im], [im, re]]))
    return np.stack([halves(t) for t in (out[0], out[1], out[0].T, out[1].T)])


def split(x):
    high = x.astype(BF16)
    return high, (x - high.astype(F32)).astype(BF16)


def dot(a, b):
    return jnp.dot(a, b, preferred_element_type=F32)


def left(tables, which, x):
    high, low = split(x)
    t_high, t_low = tables[which, 0], tables[which, 1]
    return dot(t_high, high) + dot(t_high, low) + dot(t_low, high)


def right(x, tables, which):
    high, low = split(x)
    t_high, t_low = tables[which, 0], tables[which, 1]
    return dot(high, t_high) + dot(low, t_high) + dot(high, t_low)


def forward(tables, re, im):
    h = re.shape[0] // 2
    u = jnp.concatenate([re[:h] + re[h:], im[:h] + im[h:]], 0)
    v = jnp.concatenate([re[:h] - re[h:], im[:h] - im[h:]], 0)
    even, odd = left(tables, 0, u), left(tables, 1, v)

    def columns(op):
        rows = [jnp.concatenate([op(y[:h, :h], y[:h, h:]), op(y[h:, :h], y[h:, h:])], 1) for y in (even, odd)]
        return jnp.concatenate(rows, 0)

    return (
        right(columns(lambda a, b: a + b), tables, 2),
        right(columns(lambda a, b: a - b), tables, 3),
    )


def inverse(tables, even, odd):
    h = even.shape[0] // 2
    a, b = right(even, tables, 0), right(odd, tables, 1)
    s, d = a + b, a - b

    def rows(lo):
        return jnp.concatenate(
            [
                jnp.concatenate([s[lo : lo + h, :h], d[lo : lo + h, :h]], 1),
                jnp.concatenate([s[lo : lo + h, h:], d[lo : lo + h, h:]], 1),
            ],
            0,
        )

    a, b = left(tables, 2, rows(0)), left(tables, 3, rows(h))
    s, d = a + b, a - b
    return jnp.concatenate([s[:h], d[:h]], 0), jnp.concatenate([s[h:], d[h:]], 0)


def power_of(z):
    h = z.shape[-1] // 2
    return z[:, :h] * z[:, :h] + z[:, h:] * z[:, h:]


def place_of(which, bit, h):
    return pl.multiple_of(jnp.where(bit == which, 0, h), h)


def rows_of(ref, bit):
    h = ref.shape[0] // 2
    return jnp.concatenate([ref[pl.ds(place_of(which, bit, h), h)] for which in range(2)], 0)


def add_rows(ref, base, bit, value):
    h = value.shape[0] // 2
    for which in range(2):
        ref[pl.ds(base + place_of(which, bit, h), h)] += value[which * h : (which + 1) * h]


def illuminated(tables, patch, probe):
    (p_re, p_im), (o_re, o_im) = probe, (patch[0, 0], patch[0, 1])
    return forward(tables, p_re * o_re - p_im * o_im, p_re * o_im + p_im * o_re)


def gradients(tables, patch, probe, spectrum, keep, pgrad, base, bit, gpatch):
    size = patch.shape[-1]
    k_even, k_odd = keep[0, 0], keep[0, 1]
    b_re, b_im = inverse(
        tables,
        spectrum[0] * jnp.concatenate([k_even, k_even], 1),
        spectrum[1] * jnp.concatenate([k_odd, k_odd], 1),
    )
    (p_re, p_im), (o_re, o_im) = probe, (patch[0, 0], patch[0, 1])
    gpatch[0, 0] += p_re * b_re + p_im * b_im
    gpatch[0, 1] += p_re * b_im - p_im * b_re
    add_rows(pgrad, base, bit, o_re * b_re + o_im * b_im)
    add_rows(pgrad, base + size, bit, o_re * b_im - o_im * b_re)


def whole(*shape):
    return pl.BlockSpec(shape, lambda i, *_: (0,) * len(shape))


def per_slot(*shape):
    return pl.BlockSpec((1, *shape), lambda i, *_: (i,) + (0,) * len(shape))


def per_batch_slot(batch, *shape):
    return pl.BlockSpec((1, *shape), lambda i, *_: (batch * POS + i,) + (0,) * len(shape))


def call(body, scalars, operands, in_specs, out_shapes, out_specs, grid, scratch=(), aliases=None, flops=0, moved=0):
    return pl.pallas_call(
        body,
        out_shape=[jax.ShapeDtypeStruct(s, F32) for s in out_shapes],
        grid_spec=pltpu.PrefetchScalarGridSpec(
            num_scalar_prefetch=len(scalars),
            grid=(grid,),
            in_specs=in_specs,
            out_specs=out_specs,
            scratch_shapes=list(scratch),
        ),
        input_output_aliases=aliases or {},
        compiler_params=pltpu.CompilerParams(vmem_limit_bytes=VMEM_LIMIT),
        cost_estimate=pl.CostEstimate(flops=flops, bytes_accessed=moved, transcendentals=0),
    )(*scalars, *operands)


def corner_of(offs, slot, full, size):
    row = offs[2 * slot] + H
    col = offs[2 * slot + 1] + H
    row_at = pl.multiple_of(jnp.minimum(row // 8 * 8, full - size - 8), 8)
    col_at = pl.multiple_of(jnp.minimum(col // 128 * 128, full - size - 128), 128)
    return row_at, col_at, row - row_at, col - col_at


def shift_in(block, row, col):
    rows, columns = block.shape
    turn = lax.rem(128 - col, 128)
    tiles = [pltpu.roll(block[:, at : at + 128], turn, 1) for at in range(0, columns, 128)]
    here = lax.broadcasted_iota(jnp.int32, (rows, 128), 1) < 128 - col
    block = jnp.concatenate([jnp.where(here, a, b) for a, b in zip(tiles, tiles[1:])], 1)
    block = pltpu.roll(block.reshape(rows // 8, 8, columns - 128), lax.rem(8 - row, 8), 1)
    here = lax.broadcasted_iota(jnp.int32, (rows // 8 - 1, 8, columns - 128), 1) < 8 - row
    return jnp.where(here, block[:-1], block[1:]).reshape(rows - 8, columns - 128)


def shift_out(block, row, col):
    rows, columns = block.shape
    block = pltpu.roll(block.reshape(rows // 8, 8, columns), lax.rem(row, 8), 1)
    zero = jnp.zeros((1, 8, columns), F32)
    here = lax.broadcasted_iota(jnp.int32, (rows // 8 + 1, 8, columns), 1) >= row
    block = jnp.where(here, jnp.concatenate([block, zero], 0), jnp.concatenate([zero, block], 0))
    block = block.reshape(rows + 8, columns)
    zero = jnp.zeros((rows + 8, 128), F32)
    tiles = [zero] + [pltpu.roll(block[:, at : at + 128], lax.rem(col, 128), 1) for at in range(0, columns, 128)] + [zero]
    here = lax.broadcasted_iota(jnp.int32, (rows + 8, 128), 1) >= col
    return jnp.concatenate([jnp.where(here, b, a) for a, b in zip(tiles, tiles[1:])], 1)


def cut_corners(left_side, right_side, after):
    edge = left_side.shape[1]

    def body(left_ref, right_ref, *rest):
        leading, last, sems = rest[-3:]
        copies = [
            pltpu.make_async_copy(ref.at[:, rows], out.at[:, :, columns], sems.at[2 * k + at])
            for k, (out, rows) in enumerate(((leading, slice(0, H)), (last, slice(edge - H, edge))))
            for at, (ref, columns) in enumerate(((left_ref, slice(0, H)), (right_ref, slice(H, 2 * H))))
        ]
        for copy in copies:
            copy.start()
        for copy in copies:
            copy.wait()

    return call(
        body,
        [],
        [left_side, right_side, *after],
        [pl.BlockSpec(memory_space=pl.ANY)] * (2 + len(after)),
        [(2, H, 2 * H)] * 2,
        [whole(2, H, 2 * H)] * 2,
        1,
        scratch=[pltpu.SemaphoreType.DMA((4,))],
        flops=10**5,
        moved=2 * 10**6,
    )


def cut_patches(offsets, info, tile, sides, size, slots):
    edge = tile.shape[1]
    full = edge + 2 * H
    low, mid, high = slice(0, H), slice(H, H + edge), slice(H + edge, full)
    first_half, second_half, everything = slice(0, H), slice(H, 2 * H), slice(None)
    pieces = [
        (0, everything, mid, mid),
        (1, everything, mid, low),
        (2, everything, mid, high),
        (3, everything, low, mid),
        (4, everything, high, mid),
        (5, first_half, low, low),
        (5, second_half, low, high),
        (6, first_half, high, low),
        (6, second_half, high, high),
    ]

    def body(offs, info_ref, *refs):
        sources, (out, cover, ext, sems) = refs[:7], refs[7:]
        i = pl.program_id(0)

        @pl.when(i == 0)
        def _():
            copies = [
                pltpu.make_async_copy(sources[k].at[:, :, part], ext.at[:, rows, columns], sems.at[j])
                for j, (k, part, rows, columns) in enumerate(pieces)
            ]
            for copy in copies:
                copy.start()
            cover[...] = jnp.zeros_like(cover)
            for copy in copies:
                copy.wait()

        @pl.when(i < info_ref[0])
        def _():
            row_at, col_at, row, col = corner_of(offs, i, full, size)
            total = jnp.zeros((1, size), F32)
            for part in range(2):
                block = shift_in(ext[part, pl.ds(row_at, size + 8), pl.ds(col_at, size + 128)], row, col)
                out[0, part] = block
                total = total + jnp.sum(block * block, axis=0, keepdims=True)
            here = lax.broadcasted_iota(jnp.int32, cover.shape, 0) == i // POS
            cover[...] += jnp.where(here, total, 0.0)

    return call(
        body,
        [offsets, info],
        [tile, *sides],
        [pl.BlockSpec(memory_space=pl.ANY)] * 7,
        [(slots, 2, size, size), (8, size)],
        [per_slot(2, size, size), whole(8, size)],
        slots,
        scratch=[pltpu.VMEM((2, full, full), F32), pltpu.SemaphoreType.DMA((len(pieces),))],
        flops=10**6,
        moved=8 * 10**6,
    )


def place_gradients(offsets, info, patches, after, edge):
    size = patches[0].shape[-1]
    full = edge + 2 * H
    n = len(patches)

    def body(offs, info_ref, *refs):
        patch_refs, (core, upper, lower, left_part, right_part, ext) = refs[:n], refs[n + len(after) :]
        i = pl.program_id(0)

        @pl.when(i == 0)
        def _():
            ext[...] = jnp.zeros_like(ext)

        for batch in range(n):

            @pl.when((i // POS == batch) & (i < info_ref[0]))
            def _():
                row_at, col_at, row, col = corner_of(offs, i, full, size)
                for part in range(2):
                    block = shift_out(patch_refs[batch][0, part], row, col)
                    ext[part, pl.ds(row_at, size + 8), pl.ds(col_at, size + 128)] += block

        @pl.when(i == n * POS - 1)
        def _():
            core[...] = ext[:, H : H + edge, H : H + edge]
            upper[...] = ext[:, :H]
            lower[...] = ext[:, H + edge :]
            left_part[...] = ext[:, H : H + edge, :H]
            right_part[...] = ext[:, H : H + edge, H + edge :]

    def spec(batch):
        return pl.BlockSpec((1, 2, size, size), lambda i, *_: (jnp.clip(i - batch * POS, 0, POS - 1), 0, 0, 0))

    shapes = [(2, edge, edge), (2, H, full), (2, H, full), (2, edge, H), (2, edge, H)]
    return call(
        body,
        [offsets, info],
        [*patches, *after],
        [spec(batch) for batch in range(n)] + [pl.BlockSpec(memory_space=pl.ANY)] * len(after),
        shapes,
        [whole(*shape) for shape in shapes],
        n * POS,
        scratch=[pltpu.VMEM((2, full, full), F32)],
        flops=10**6,
        moved=10**7,
    )


def side_borders(left_part, right_part, from_below, from_above, after):
    edge = left_part.shape[1]
    full = from_below.shape[2]

    def body(left_ref, right_ref, below, above, *rest):
        for ref, out, at in ((left_ref, rest[-2], 0), (right_ref, rest[-1], H + edge)):
            out[...] = ref[...]
            out[:, edge - H :] += below[:, :, at : at + H]
            out[:, :H] += above[:, :, at : at + H]

    return call(
        body,
        [],
        [left_part, right_part, from_below, from_above, *after],
        [whole(2, edge, H)] * 2 + [whole(2, H, full)] * 2 + [pl.BlockSpec(memory_space=pl.ANY)] * len(after),
        [(2, edge, H)] * 2,
        [whole(2, edge, H)] * 2,
        1,
        flops=10**5,
        moved=4 * 10**6,
    )


def call_in_vmem(body, info, operands, out_shapes, scratch=(), after=(), flops=0, moved=0):
    vmem = pl.BlockSpec(memory_space=pltpu.VMEM)
    return pl.pallas_call(
        body,
        out_shape=[pltpu.VMEM(s, F32) for s in out_shapes],
        in_specs=[pl.BlockSpec(memory_space=pltpu.SMEM)]
        + [vmem] * len(operands)
        + [pl.BlockSpec(memory_space=pl.ANY)] * len(after),
        out_specs=[vmem] * len(out_shapes),
        scratch_shapes=list(scratch),
        compiler_params=pltpu.CompilerParams(vmem_limit_bytes=VMEM_KERNEL),
        cost_estimate=pl.CostEstimate(flops=flops, bytes_accessed=moved, transcendentals=0),
    )(info, *[pltpu.with_memory_space_constraint(x, pltpu.VMEM) for x in operands], *after)


def turn_kernel(tables, info, patches, probes, roots, cover, batch):
    size = patches.shape[-1]
    h = size // 2
    rows = 4 * size
    extra = 0 if cover is None else cover.shape[0]

    def body(info_ref, t, patches_ref, roots_ref, *rest):
        p, rest = rest[:8], rest[8:]
        if extra:
            cover_ref, rest = rest[0], rest[1:]
        sent, keeps, gpatches, z, scratch = rest
        sent[:rows] = jnp.zeros((rows, size), F32)
        if extra:
            sent[rows:] = cover_ref[...]
        gpatches[...] = jnp.zeros_like(gpatches)
        for i in range(POS):
            slot = batch * POS + i
            patch, root = patches_ref.at[slot : slot + 1], roots_ref.at[slot : slot + 1]
            keep, gpatch = keeps.at[i : i + 1], gpatches.at[i : i + 1]

            @pl.when(slot < info_ref[0])
            def _():
                bits = [info_ref[2], info_ref[2], info_ref[1], info_ref[1]]
                totals = [0.0, 0.0]
                for m in range(4):
                    pair = illuminated(t, patch, (rows_of(p[2 * m], bits[m]), rows_of(p[2 * m + 1], bits[m])))
                    for e in range(2):
                        if m < 2:
                            z[i, m, e] = pair[e]
                        else:
                            scratch[m - 2, e] = pair[e]
                        totals[e] = totals[e] + power_of(pair[e])
                for e in range(2):
                    keep[0, e] = 1.0 - root[0, e] * lax.rsqrt(totals[e] + 0.1)
                for m in range(2, 4):
                    probe = (rows_of(p[2 * m], bits[m]), rows_of(p[2 * m + 1], bits[m]))
                    spectrum = (scratch[m - 2, 0], scratch[m - 2, 1])
                    gradients(t, patch, probe, spectrum, keep, sent, (m - 2) * 2 * size, bits[m], gpatch)

    return call_in_vmem(
        body,
        info,
        [tables, patches, roots, *probes] + ([cover] if extra else []),
        [(rows + extra, size), (POS, 2, size, h), (POS, 2, size, size), (POS, 2, 2, size, size)],
        scratch=[pltpu.VMEM((2, 2, size, size), F32)],
        flops=POS * 6 * 24 * size**3,
        moved=8 * 10**6,
    )


def back_kernel(tables, info, patches, probe, spectra, keeps, gpatches, batch, mode, start, after):
    size = patches.shape[-1]
    h = size // 2

    def body(info_ref, t, patches_ref, z, keeps_ref, g_in, p_re, p_im, *rest):
        quarters, g_out, pgrad = rest[-6:-2], rest[-2], rest[-1]
        if start:
            pgrad[...] = rest[0][: 2 * size]
        else:
            pgrad[...] = jnp.zeros_like(pgrad)
        g_out[...] = g_in[...]
        for i in range(POS):
            slot = batch * POS + i
            patch, keep, gpatch = patches_ref.at[slot : slot + 1], keeps_ref.at[i : i + 1], g_out.at[i : i + 1]

            @pl.when(slot < info_ref[0])
            def _():
                bit = info_ref[2]
                pair = (rows_of(p_re, bit), rows_of(p_im, bit))
                gradients(t, patch, pair, (z[i, mode, 0], z[i, mode, 1]), keep, pgrad, 0, bit, gpatch)

        for at, out in enumerate(quarters):
            out[...] = pgrad[at * h : (at + 1) * h]

    return call_in_vmem(
        body,
        info,
        [tables, patches, spectra, keeps, gpatches, *probe, *start],
        [(h, size)] * 4 + [(POS, 2, size, size)],
        scratch=[pltpu.VMEM((2 * size, size), F32)],
        after=after,
        flops=POS * 24 * size**3,
        moved=4 * 10**6,
    )


def probe_kernel(info, probes):
    size = probes[0].shape[0]

    def body(info_ref, *refs):
        p, (probe_out, top, power) = refs[:8], refs[8:]
        i = pl.program_id(0)
        for m in range(4):

            @pl.when(i == m)
            def _():
                bit = info_ref[2] if m < 2 else info_ref[1]
                re, im = rows_of(p[2 * m], bit), rows_of(p[2 * m + 1], bit)
                probe_out[0, 0], probe_out[0, 1] = re, im
                square = re * re + im * im
                power[...] = square if m == 0 else power[...] + square

        @pl.when(i == 3)
        def _():
            top[...] = jnp.broadcast_to(jnp.max(power[...], keepdims=True), top.shape)

    return call(
        body,
        [info],
        probes,
        [whole(size, size)] * 8,
        [(4, 2, size, size), (8, 128)],
        [pl.BlockSpec((1, 2, size, size), lambda i, info_ref: (info_ref[3 + i], 0, 0, 0)), whole(8, 128)],
        4,
        scratch=[pltpu.VMEM((size, size), F32)],
        flops=10**6,
        moved=4 * 10**6,
    )


def object_kernel(top, field, core, from_below, from_above):
    edge = field.shape[1]
    full = from_below.shape[2]
    steps = edge // H

    def body(top_ref, o, g, fb, fa, out):
        i = pl.program_id(0)
        step = (0.5 / top_ref[:1, :1])[None]
        out[...] = o[...] - step * g[...]

        @pl.when(i == steps - 1)
        def _():
            out[...] -= step * fb[:, :, H : H + edge]

        @pl.when(i == 0)
        def _():
            out[...] -= step * fa[:, :, H : H + edge]

    band = pl.BlockSpec((2, H, edge), lambda i: (0, i, 0))
    return call(
        body,
        [],
        [top, field, core, from_below, from_above],
        [whole(8, 128), band, band, whole(2, H, full), whole(2, H, full)],
        [field.shape],
        [band],
        steps,
        flops=10**6,
        moved=8 * 10**6,
    )[0]


def side_kernel(top, updated, from_right, from_left):
    edge = updated.shape[1]

    def body(top_ref, x, fr, fl, out):
        i = pl.program_id(0)
        step = (0.5 / top_ref[:1, :1])[None]

        @pl.when(i == 0)
        def _():
            out[...] = x[...] - step * fl[...]

        @pl.when(i == 1)
        def _():
            out[...] = x[...] - step * fr[...]

    side = pl.BlockSpec((2, edge, H), lambda i: (0, 0, i * (edge // H - 1)))
    return call(
        body,
        [],
        [top, updated, from_right, from_left],
        [whole(8, 128), side, whole(2, edge, H), whole(2, edge, H)],
        [updated.shape],
        [side],
        2,
        aliases={1: 0},
        flops=10**5,
        moved=4 * 10**6,
    )[0]


def flips(wide, narrow):
    bits = [(0, 2 << i) for i in range(1, narrow.bit_length() - 2)] + [
        (1 << i, 0) for i in range(1, wide.bit_length() - 1)
    ]

    def exchange(even, odd):
        pairs = []
        for w in range(wide):
            for n in range(narrow):
                dw, dn = odd if n & 1 else even
                pairs.append((w * narrow + n, (w ^ dw) * narrow + (n ^ dn)))
        return functools.partial(lax.ppermute, axis_name=AXES, perm=pairs)

    core = exchange((0, 1), (0, 1))
    first = exchange((0, 2), (1, 0))
    second = exchange((1, 0), (0, 2))
    return core, first, second, [exchange(a, b) for a, b in zip(bits, bits[::-1])]


def shifted(value, axis, steps):
    count = lax.axis_size(axis)
    leading, last = (max(0, -steps), min(count, count - steps))
    return lax.ppermute(value, axis, [(source, source + steps) for source in range(leading, last)])


def local(object_field, probe, patterns, offsets, counts):
    edge = object_field.shape[1]
    size = probe.shape[-1]
    slots = patterns.shape[2]
    h = size // 2
    wide, narrow = lax.axis_size("wide"), lax.axis_size("narrow")
    w, n = lax.axis_index("wide"), lax.axis_index("narrow")
    core, first, second, rest = flips(wide, narrow)
    offs = offsets.reshape(slots * 2)

    left_side = shifted(object_field[:, :, edge - H :], "wide", 1)
    right_side = shifted(object_field[:, :, :H], "wide", -1)
    top_side = shifted(object_field[:, edge - H :], "narrow", 1)
    bottom_side = shifted(object_field[:, :H], "narrow", -1)

    tables = jnp.asarray(dft_tables(size))
    order = np.concatenate([np.arange(0, size, 2), np.arange(1, size, 2)])
    pick = jnp.asarray(np.eye(size, dtype=np.float32)[order])
    roots = jnp.einsum("pj,sjk->spk", pick, jnp.sqrt(patterns[0, 0]), precision=lax.Precision.HIGHEST)
    roots = jnp.einsum("spk,qk->spq", roots, pick, precision=lax.Precision.HIGHEST)
    roots = roots.reshape(slots, size, 2, h).transpose(0, 2, 1, 3)

    c = n % 2
    bit_n, bit_w = (n // 2) % 2, w % 2
    b1 = jnp.where(c == 0, bit_n, bit_w)
    b2 = jnp.where(c == 0, bit_w, bit_n)
    ours, theirs = 2 * c, 2 * (1 - c)
    order_of = [ours + b1, ours + 1 - b1, theirs + b2, theirs + 1 - b2]
    info = jnp.stack([counts[0, 0], b1, b2, *order_of]).astype(jnp.int32)
    split_rows = probe.reshape(4, 2, 2, h, size)
    probes = []
    for m, bit in zip(order_of, (b2, b2, b1, b1)):
        for part in range(2):
            mine = lax.dynamic_slice(split_rows, (m, part, bit, 0, 0), (1, 1, 1, h, size))
            other = lax.dynamic_slice(split_rows, (m, part, 1 - bit, 0, 0), (1, 1, 1, h, size))
            probes.append(jnp.concatenate([mine.reshape(h, size), other.reshape(h, size)], 0))

    leading, last = cut_corners(left_side, right_side, (roots, *probes))
    top_corners = shifted(last, "narrow", 1)
    bottom_corners = shifted(leading, "narrow", -1)
    sides = (left_side, right_side, top_side, bottom_side, top_corners, bottom_corners)
    patches, cover = cut_patches(offs, info, object_field, sides, size, slots)

    patch_gradients = []
    for batch in range(BATCHES):
        extra = cover if batch == 0 else None

        def ride(x):
            return x if extra is None else jnp.concatenate([x, extra], 0)

        sent, keep, gpatch, z = turn_kernel(tables, info, patches, probes, roots, extra, batch)
        got = core(sent)
        *q, gpatch = back_kernel(tables, info, patches, probes[2:4], z, keep, gpatch, batch, 1, (), ())
        if extra is not None:
            extra = extra + got[4 * size :]
        sent_a = jnp.concatenate([q[0], q[1]], 0) + got[2 * size : 3 * size]
        sent_b = jnp.concatenate([q[2], q[3]], 0) + got[3 * size : 4 * size]
        got_a = first(ride(sent_a))
        got_b = first(sent_b)
        after = (sent_a, sent_b)
        *q, gpatch = back_kernel(tables, info, patches, probes[:2], z, keep, gpatch, batch, 0, (got,), after)
        patch_gradients.append(gpatch)
        sent_a = q[1] + got_a[h:size]
        sent_b = q[3] + got_b[h:]
        a = q[0] + got_a[:h]
        b = q[2] + got_b[:h]
        if extra is not None:
            extra = extra + got_a[size:]
        got_a = second(ride(sent_a))
        got_b = second(sent_b)
        a = a + got_a[:h]
        b = b + got_b
        if extra is not None:
            extra = extra + got_a[h:]
        if batch == BATCHES - 1:
            inside, upper, lower, left_part, right_part = place_gradients(offs, info, patch_gradients, (a, b), edge)
            from_below = shifted(upper, "narrow", -1)
            from_above = shifted(lower, "narrow", 1)
        for exchange in rest:
            got_a = exchange(ride(a))
            got_b = exchange(b)
            a = a + got_a[:h]
            b = b + got_b
            if extra is not None:
                extra = extra + got_a[h:]
        if extra is not None:
            scales = jnp.sum(extra, axis=1) / (size * size)
        a = probes[0][:h] - a / scales[batch]
        b = probes[1][:h] - b / scales[batch]
        a = jnp.concatenate([a, second(a)], 0)
        b = jnp.concatenate([b, second(b)], 0)
        own = [a, b, first(a), first(b)]
        probes = own + [core(x) for x in own]

    to_left, to_right = side_borders(left_part, right_part, from_below, from_above, own[2:])
    from_right = shifted(to_left, "wide", -1)
    from_left = shifted(to_right, "wide", 1)
    probe_new, top = probe_kernel(info, probes)
    updated = object_kernel(top, object_field, inside, from_below, from_above)
    return (side_kernel(top, updated, from_right, from_left), probe_new)


def solution(mesh):
    placed = (
        P(None, "narrow", "wide"),
        P(),
        P("narrow", "wide", None, None, None),
        P("narrow", "wide", None, None),
        P("narrow", "wide"),
    )
    return jax.shard_map(
        local,
        mesh=mesh,
        in_specs=placed,
        out_specs=(P(None, "narrow", "wide"), P()),
        check_vma=False,
    )
```

```python
import functools

import jax
import jax.numpy as jnp
import ml_dtypes
import numpy as np
from jax import lax
from jax.experimental import pallas as pl
from jax.experimental.pallas import tpu as pltpu
from jax.sharding import PartitionSpec as P

H = 128
BATCHES = 3
POS = 2
AXES = ("wide", "narrow")
F32 = jnp.float32
BF16 = jnp.bfloat16
VMEM_LIMIT = 32 * 1024 * 1024
VMEM_KERNEL = 24 * 1024 * 1024


def halves(table):
    high = table.astype(ml_dtypes.bfloat16)
    low = (table - high.astype(np.float64)).astype(ml_dtypes.bfloat16)
    return np.stack([high, low])


def dft_tables(size):
    half = size // 2
    k = np.arange(half)
    out = []
    for odd in range(2):
        phase = ((2 * k[:, None] + odd) * k[None, :]) % size
        angle = -2.0 * np.pi * phase / size
        re, im = np.cos(angle) / np.sqrt(size), np.sin(angle) / np.sqrt(size)
        out.append(np.block([[re, -im], [im, re]]))
    return np.stack([halves(t) for t in (out[0], out[1], out[0].T, out[1].T)])


def split(x):
    high = x.astype(BF16)
    return high, (x - high.astype(F32)).astype(BF16)


def dot(a, b):
    return jnp.dot(a, b, preferred_element_type=F32)


def left(tables, which, x):
    high, low = split(x)
    t_high, t_low = tables[which, 0], tables[which, 1]
    return dot(t_high, high) + dot(t_high, low) + dot(t_low, high)


def right(x, tables, which):
    high, low = split(x)
    t_high, t_low = tables[which, 0], tables[which, 1]
    return dot(high, t_high) + dot(low, t_high) + dot(high, t_low)


def forward(tables, re, im):
    h = re.shape[0] // 2
    u = jnp.concatenate([re[:h] + re[h:], im[:h] + im[h:]], 0)
    v = jnp.concatenate([re[:h] - re[h:], im[:h] - im[h:]], 0)
    even, odd = left(tables, 0, u), left(tables, 1, v)

    def columns(op):
        rows = [jnp.concatenate([op(y[:h, :h], y[:h, h:]), op(y[h:, :h], y[h:, h:])], 1) for y in (even, odd)]
        return jnp.concatenate(rows, 0)

    return (
        right(columns(lambda a, b: a + b), tables, 2),
        right(columns(lambda a, b: a - b), tables, 3),
    )


def inverse(tables, even, odd):
    h = even.shape[0] // 2
    a, b = right(even, tables, 0), right(odd, tables, 1)
    s, d = a + b, a - b

    def rows(lo):
        return jnp.concatenate(
            [
                jnp.concatenate([s[lo : lo + h, :h], d[lo : lo + h, :h]], 1),
                jnp.concatenate([s[lo : lo + h, h:], d[lo : lo + h, h:]], 1),
            ],
            0,
        )

    a, b = left(tables, 2, rows(0)), left(tables, 3, rows(h))
    s, d = a + b, a - b
    return jnp.concatenate([s[:h], d[:h]], 0), jnp.concatenate([s[h:], d[h:]], 0)


def power_of(z):
    h = z.shape[-1] // 2
    return z[:, :h] * z[:, :h] + z[:, h:] * z[:, h:]


def place_of(which, bit, h):
    return pl.multiple_of(jnp.where(bit == which, 0, h), h)


def rows_of(ref, bit):
    h = ref.shape[0] // 2
    return jnp.concatenate([ref[pl.ds(place_of(which, bit, h), h)] for which in range(2)], 0)


def add_rows(ref, base, bit, value):
    h = value.shape[0] // 2
    for which in range(2):
        ref[pl.ds(base + place_of(which, bit, h), h)] += value[which * h : (which + 1) * h]


def illuminated(tables, patch, probe):
    (p_re, p_im), (o_re, o_im) = probe, (patch[0, 0], patch[0, 1])
    return forward(tables, p_re * o_re - p_im * o_im, p_re * o_im + p_im * o_re)


def gradients(tables, patch, probe, spectrum, keep, pgrad, base, bit, gpatch):
    size = patch.shape[-1]
    k_even, k_odd = keep[0, 0], keep[0, 1]
    b_re, b_im = inverse(
        tables,
        spectrum[0] * jnp.concatenate([k_even, k_even], 1),
        spectrum[1] * jnp.concatenate([k_odd, k_odd], 1),
    )
    (p_re, p_im), (o_re, o_im) = probe, (patch[0, 0], patch[0, 1])
    gpatch[0, 0] += p_re * b_re + p_im * b_im
    gpatch[0, 1] += p_re * b_im - p_im * b_re
    add_rows(pgrad, base, bit, o_re * b_re + o_im * b_im)
    add_rows(pgrad, base + size, bit, o_re * b_im - o_im * b_re)


def whole(*shape):
    return pl.BlockSpec(shape, lambda i, *_: (0,) * len(shape))


def per_slot(*shape):
    return pl.BlockSpec((1, *shape), lambda i, *_: (i,) + (0,) * len(shape))


def per_batch_slot(batch, *shape):
    return pl.BlockSpec((1, *shape), lambda i, *_: (batch * POS + i,) + (0,) * len(shape))


def call(body, scalars, operands, in_specs, out_shapes, out_specs, grid, scratch=(), aliases=None, flops=0, moved=0):
    return pl.pallas_call(
        body,
        out_shape=[jax.ShapeDtypeStruct(s, F32) for s in out_shapes],
        grid_spec=pltpu.PrefetchScalarGridSpec(
            num_scalar_prefetch=len(scalars),
            grid=(grid,),
            in_specs=in_specs,
            out_specs=out_specs,
            scratch_shapes=list(scratch),
        ),
        input_output_aliases=aliases or {},
        compiler_params=pltpu.CompilerParams(vmem_limit_bytes=VMEM_LIMIT),
        cost_estimate=pl.CostEstimate(flops=flops, bytes_accessed=moved, transcendentals=0),
    )(*scalars, *operands)


def corner_of(offs, slot, full, size):
    row = offs[2 * slot] + H
    col = offs[2 * slot + 1] + H
    row_at = pl.multiple_of(jnp.minimum(row // 8 * 8, full - size - 8), 8)
    col_at = pl.multiple_of(jnp.minimum(col // 128 * 128, full - size - 128), 128)
    return row_at, col_at, row - row_at, col - col_at


def shift_in(block, row, col):
    rows, columns = block.shape
    turn = lax.rem(128 - col, 128)
    tiles = [pltpu.roll(block[:, at : at + 128], turn, 1) for at in range(0, columns, 128)]
    here = lax.broadcasted_iota(jnp.int32, (rows, 128), 1) < 128 - col
    block = jnp.concatenate([jnp.where(here, a, b) for a, b in zip(tiles, tiles[1:])], 1)
    block = pltpu.roll(block.reshape(rows // 8, 8, columns - 128), lax.rem(8 - row, 8), 1)
    here = lax.broadcasted_iota(jnp.int32, (rows // 8 - 1, 8, columns - 128), 1) < 8 - row
    return jnp.where(here, block[:-1], block[1:]).reshape(rows - 8, columns - 128)


def shift_out(block, row, col):
    rows, columns = block.shape
    block = pltpu.roll(block.reshape(rows // 8, 8, columns), lax.rem(row, 8), 1)
    zero = jnp.zeros((1, 8, columns), F32)
    here = lax.broadcasted_iota(jnp.int32, (rows // 8 + 1, 8, columns), 1) >= row
    block = jnp.where(here, jnp.concatenate([block, zero], 0), jnp.concatenate([zero, block], 0))
    block = block.reshape(rows + 8, columns)
    zero = jnp.zeros((rows + 8, 128), F32)
    tiles = [zero] + [pltpu.roll(block[:, at : at + 128], lax.rem(col, 128), 1) for at in range(0, columns, 128)] + [zero]
    here = lax.broadcasted_iota(jnp.int32, (rows + 8, 128), 1) >= col
    return jnp.concatenate([jnp.where(here, b, a) for a, b in zip(tiles, tiles[1:])], 1)


def cut_corners(left_side, right_side, after):
    edge = left_side.shape[1]

    def body(left_ref, right_ref, *rest):
        leading, last, sems = rest[-3:]
        copies = [
            pltpu.make_async_copy(ref.at[:, rows], out.at[:, :, columns], sems.at[2 * k + at])
            for k, (out, rows) in enumerate(((leading, slice(0, H)), (last, slice(edge - H, edge))))
            for at, (ref, columns) in enumerate(((left_ref, slice(0, H)), (right_ref, slice(H, 2 * H))))
        ]
        for copy in copies:
            copy.start()
        for copy in copies:
            copy.wait()

    return call(
        body,
        [],
        [left_side, right_side, *after],
        [pl.BlockSpec(memory_space=pl.ANY)] * (2 + len(after)),
        [(2, H, 2 * H)] * 2,
        [whole(2, H, 2 * H)] * 2,
        1,
        scratch=[pltpu.SemaphoreType.DMA((4,))],
        flops=10**5,
        moved=2 * 10**6,
    )


def cut_patches(offsets, info, tile, sides, size, slots):
    edge = tile.shape[1]
    full = edge + 2 * H
    low, mid, high = slice(0, H), slice(H, H + edge), slice(H + edge, full)
    first_half, second_half, everything = slice(0, H), slice(H, 2 * H), slice(None)
    pieces = [
        (0, everything, mid, mid),
        (1, everything, mid, low),
        (2, everything, mid, high),
        (3, everything, low, mid),
        (4, everything, high, mid),
        (5, first_half, low, low),
        (5, second_half, low, high),
        (6, first_half, high, low),
        (6, second_half, high, high),
    ]

    def body(offs, info_ref, *refs):
        sources, (out, cover, ext, sems) = refs[:7], refs[7:]
        i = pl.program_id(0)

        @pl.when(i == 0)
        def _():
            copies = [
                pltpu.make_async_copy(sources[k].at[:, :, part], ext.at[:, rows, columns], sems.at[j])
                for j, (k, part, rows, columns) in enumerate(pieces)
            ]
            for copy in copies:
                copy.start()
            cover[...] = jnp.zeros_like(cover)
            for copy in copies:
                copy.wait()

        @pl.when(i < info_ref[0])
        def _():
            row_at, col_at, row, col = corner_of(offs, i, full, size)
            total = jnp.zeros((1, size), F32)
            for part in range(2):
                block = shift_in(ext[part, pl.ds(row_at, size + 8), pl.ds(col_at, size + 128)], row, col)
                out[0, part] = block
                total = total + jnp.sum(block * block, axis=0, keepdims=True)
            here = lax.broadcasted_iota(jnp.int32, cover.shape, 0) == i // POS
            cover[...] += jnp.where(here, total, 0.0)

    return call(
        body,
        [offsets, info],
        [tile, *sides],
        [pl.BlockSpec(memory_space=pl.ANY)] * 7,
        [(slots, 2, size, size), (8, size)],
        [per_slot(2, size, size), whole(8, size)],
        slots,
        scratch=[pltpu.VMEM((2, full, full), F32), pltpu.SemaphoreType.DMA((len(pieces),))],
        flops=10**6,
        moved=8 * 10**6,
    )


def place_gradients(offsets, info, patches, after, edge):
    size = patches[0].shape[-1]
    full = edge + 2 * H
    n = len(patches)

    def body(offs, info_ref, *refs):
        patch_refs, (core, upper, lower, left_part, right_part, ext) = refs[:n], refs[n + len(after) :]
        i = pl.program_id(0)

        @pl.when(i == 0)
        def _():
            ext[...] = jnp.zeros_like(ext)

        for batch in range(n):

            @pl.when((i // POS == batch) & (i < info_ref[0]))
            def _():
                row_at, col_at, row, col = corner_of(offs, i, full, size)
                for part in range(2):
                    block = shift_out(patch_refs[batch][0, part], row, col)
                    ext[part, pl.ds(row_at, size + 8), pl.ds(col_at, size + 128)] += block

        @pl.when(i == n * POS - 1)
        def _():
            core[...] = ext[:, H : H + edge, H : H + edge]
            upper[...] = ext[:, :H]
            lower[...] = ext[:, H + edge :]
            left_part[...] = ext[:, H : H + edge, :H]
            right_part[...] = ext[:, H : H + edge, H + edge :]

    def spec(batch):
        return pl.BlockSpec((1, 2, size, size), lambda i, *_: (jnp.clip(i - batch * POS, 0, POS - 1), 0, 0, 0))

    shapes = [(2, edge, edge), (2, H, full), (2, H, full), (2, edge, H), (2, edge, H)]
    return call(
        body,
        [offsets, info],
        [*patches, *after],
        [spec(batch) for batch in range(n)] + [pl.BlockSpec(memory_space=pl.ANY)] * len(after),
        shapes,
        [whole(*shape) for shape in shapes],
        n * POS,
        scratch=[pltpu.VMEM((2, full, full), F32)],
        flops=10**6,
        moved=10**7,
    )


def side_borders(left_part, right_part, from_below, from_above, after):
    edge = left_part.shape[1]
    full = from_below.shape[2]

    def body(left_ref, right_ref, below, above, *rest):
        for ref, out, at in ((left_ref, rest[-2], 0), (right_ref, rest[-1], H + edge)):
            out[...] = ref[...]
            out[:, edge - H :] += below[:, :, at : at + H]
            out[:, :H] += above[:, :, at : at + H]

    return call(
        body,
        [],
        [left_part, right_part, from_below, from_above, *after],
        [whole(2, edge, H)] * 2 + [whole(2, H, full)] * 2 + [pl.BlockSpec(memory_space=pl.ANY)] * len(after),
        [(2, edge, H)] * 2,
        [whole(2, edge, H)] * 2,
        1,
        flops=10**5,
        moved=4 * 10**6,
    )


def call_in_vmem(body, info, operands, out_shapes, scratch=(), after=(), flops=0, moved=0):
    vmem = pl.BlockSpec(memory_space=pltpu.VMEM)
    return pl.pallas_call(
        body,
        out_shape=[pltpu.VMEM(s, F32) for s in out_shapes],
        in_specs=[pl.BlockSpec(memory_space=pltpu.SMEM)]
        + [vmem] * len(operands)
        + [pl.BlockSpec(memory_space=pl.ANY)] * len(after),
        out_specs=[vmem] * len(out_shapes),
        scratch_shapes=list(scratch),
        compiler_params=pltpu.CompilerParams(vmem_limit_bytes=VMEM_KERNEL),
        cost_estimate=pl.CostEstimate(flops=flops, bytes_accessed=moved, transcendentals=0),
    )(info, *[pltpu.with_memory_space_constraint(x, pltpu.VMEM) for x in operands], *after)


def turn_kernel(tables, info, patches, probes, roots, cover, batch):
    size = patches.shape[-1]
    h = size // 2
    rows = 4 * size
    extra = 0 if cover is None else cover.shape[0]

    def body(info_ref, t, patches_ref, roots_ref, *rest):
        p, rest = rest[:8], rest[8:]
        if extra:
            cover_ref, rest = rest[0], rest[1:]
        sent, keeps, gpatches, z, scratch = rest
        sent[:rows] = jnp.zeros((rows, size), F32)
        if extra:
            sent[rows:] = cover_ref[...]
        gpatches[...] = jnp.zeros_like(gpatches)
        for i in range(POS):
            slot = batch * POS + i
            patch, root = patches_ref.at[slot : slot + 1], roots_ref.at[slot : slot + 1]
            keep, gpatch = keeps.at[i : i + 1], gpatches.at[i : i + 1]

            @pl.when(slot < info_ref[0])
            def _():
                bits = [info_ref[2], info_ref[2], info_ref[1], info_ref[1]]
                totals = [0.0, 0.0]
                for m in range(4):
                    pair = illuminated(t, patch, (rows_of(p[2 * m], bits[m]), rows_of(p[2 * m + 1], bits[m])))
                    for e in range(2):
                        if m < 2:
                            z[i, m, e] = pair[e]
                        else:
                            scratch[m - 2, e] = pair[e]
                        totals[e] = totals[e] + power_of(pair[e])
                for e in range(2):
                    keep[0, e] = 1.0 - root[0, e] * lax.rsqrt(totals[e] + 0.1)
                for m in range(2, 4):
                    probe = (rows_of(p[2 * m], bits[m]), rows_of(p[2 * m + 1], bits[m]))
                    spectrum = (scratch[m - 2, 0], scratch[m - 2, 1])
                    gradients(t, patch, probe, spectrum, keep, sent, (m - 2) * 2 * size, bits[m], gpatch)

    return call_in_vmem(
        body,
        info,
        [tables, patches, roots, *probes] + ([cover] if extra else []),
        [(rows + extra, size), (POS, 2, size, h), (POS, 2, size, size), (POS, 2, 2, size, size)],
        scratch=[pltpu.VMEM((2, 2, size, size), F32)],
        flops=POS * 6 * 24 * size**3,
        moved=8 * 10**6,
    )


def back_kernel(tables, info, patches, probe, spectra, keeps, gpatches, batch, mode, start, after):
    size = patches.shape[-1]
    h = size // 2

    def body(info_ref, t, patches_ref, z, keeps_ref, g_in, p_re, p_im, *rest):
        quarters, g_out, pgrad = rest[-6:-2], rest[-2], rest[-1]
        if start:
            pgrad[...] = rest[0][: 2 * size]
        else:
            pgrad[...] = jnp.zeros_like(pgrad)
        g_out[...] = g_in[...]
        for i in range(POS):
            slot = batch * POS + i
            patch, keep, gpatch = patches_ref.at[slot : slot + 1], keeps_ref.at[i : i + 1], g_out.at[i : i + 1]

            @pl.when(slot < info_ref[0])
            def _():
                bit = info_ref[2]
                pair = (rows_of(p_re, bit), rows_of(p_im, bit))
                gradients(t, patch, pair, (z[i, mode, 0], z[i, mode, 1]), keep, pgrad, 0, bit, gpatch)

        for at, out in enumerate(quarters):
            out[...] = pgrad[at * h : (at + 1) * h]

    return call_in_vmem(
        body,
        info,
        [tables, patches, spectra, keeps, gpatches, *probe, *start],
        [(h, size)] * 4 + [(POS, 2, size, size)],
        scratch=[pltpu.VMEM((2 * size, size), F32)],
        after=after,
        flops=POS * 24 * size**3,
        moved=4 * 10**6,
    )


def probe_kernel(info, probes):
    size = probes[0].shape[0]

    def body(info_ref, *refs):
        p, (probe_out, top, power) = refs[:8], refs[8:]
        i = pl.program_id(0)
        for m in range(4):

            @pl.when(i == m)
            def _():
                bit = info_ref[2] if m < 2 else info_ref[1]
                re, im = rows_of(p[2 * m], bit), rows_of(p[2 * m + 1], bit)
                probe_out[0, 0], probe_out[0, 1] = re, im
                square = re * re + im * im
                power[...] = square if m == 0 else power[...] + square

        @pl.when(i == 3)
        def _():
            top[...] = jnp.broadcast_to(jnp.max(power[...], keepdims=True), top.shape)

    return call(
        body,
        [info],
        probes,
        [whole(size, size)] * 8,
        [(4, 2, size, size), (8, 128)],
        [pl.BlockSpec((1, 2, size, size), lambda i, info_ref: (info_ref[3 + i], 0, 0, 0)), whole(8, 128)],
        4,
        scratch=[pltpu.VMEM((size, size), F32)],
        flops=10**6,
        moved=4 * 10**6,
    )


def object_kernel(top, field, core, from_below, from_above):
    edge = field.shape[1]
    full = from_below.shape[2]
    steps = edge // H

    def body(top_ref, o, g, fb, fa, out):
        i = pl.program_id(0)
        step = (0.5 / top_ref[:1, :1])[None]
        out[...] = o[...] - step * g[...]

        @pl.when(i == steps - 1)
        def _():
            out[...] -= step * fb[:, :, H : H + edge]

        @pl.when(i == 0)
        def _():
            out[...] -= step * fa[:, :, H : H + edge]

    band = pl.BlockSpec((2, H, edge), lambda i: (0, i, 0))
    return call(
        body,
        [],
        [top, field, core, from_below, from_above],
        [whole(8, 128), band, band, whole(2, H, full), whole(2, H, full)],
        [field.shape],
        [band],
        steps,
        flops=10**6,
        moved=8 * 10**6,
    )[0]


def side_kernel(top, updated, from_right, from_left):
    edge = updated.shape[1]

    def body(top_ref, x, fr, fl, out):
        i = pl.program_id(0)
        step = (0.5 / top_ref[:1, :1])[None]

        @pl.when(i == 0)
        def _():
            out[...] = x[...] - step * fl[...]

        @pl.when(i == 1)
        def _():
            out[...] = x[...] - step * fr[...]

    side = pl.BlockSpec((2, edge, H), lambda i: (0, 0, i * (edge // H - 1)))
    return call(
        body,
        [],
        [top, updated, from_right, from_left],
        [whole(8, 128), side, whole(2, edge, H), whole(2, edge, H)],
        [updated.shape],
        [side],
        2,
        aliases={1: 0},
        flops=10**5,
        moved=4 * 10**6,
    )[0]


def flips(wide, narrow):
    bits = [(0, 2 << i) for i in range(1, narrow.bit_length() - 2)] + [
        (1 << i, 0) for i in range(1, wide.bit_length() - 1)
    ]

    def exchange(even, odd):
        pairs = []
        for w in range(wide):
            for n in range(narrow):
                dw, dn = odd if n & 1 else even
                pairs.append((w * narrow + n, (w ^ dw) * narrow + (n ^ dn)))
        return functools.partial(lax.ppermute, axis_name=AXES, perm=pairs)

    core = exchange((0, 1), (0, 1))
    first = exchange((0, 2), (1, 0))
    second = exchange((1, 0), (0, 2))
    return core, first, second, [exchange(a, b) for a, b in zip(bits, bits[::-1])]


def shifted(value, axis, steps):
    count = lax.axis_size(axis)
    leading, last = (max(0, -steps), min(count, count - steps))
    return lax.ppermute(value, axis, [(source, source + steps) for source in range(leading, last)])


def local(object_field, probe, patterns, offsets, counts):
    edge = object_field.shape[1]
    size = probe.shape[-1]
    slots = patterns.shape[2]
    h = size // 2
    wide, narrow = lax.axis_size("wide"), lax.axis_size("narrow")
    w, n = lax.axis_index("wide"), lax.axis_index("narrow")
    core, first, second, rest = flips(wide, narrow)
    offs = offsets.reshape(slots * 2)

    left_side = shifted(object_field[:, :, edge - H :], "wide", 1)
    right_side = shifted(object_field[:, :, :H], "wide", -1)
    top_side = shifted(object_field[:, edge - H :], "narrow", 1)
    bottom_side = shifted(object_field[:, :H], "narrow", -1)

    tables = jnp.asarray(dft_tables(size))
    order = np.concatenate([np.arange(0, size, 2), np.arange(1, size, 2)])
    pick = jnp.asarray(np.eye(size, dtype=np.float32)[order])
    roots = jnp.einsum("pj,sjk->spk", pick, jnp.sqrt(patterns[0, 0]), precision=lax.Precision.HIGHEST)
    roots = jnp.einsum("spk,qk->spq", roots, pick, precision=lax.Precision.HIGHEST)
    roots = roots.reshape(slots, size, 2, h).transpose(0, 2, 1, 3)

    c = n % 2
    bit_n, bit_w = (n // 2) % 2, w % 2
    b1 = jnp.where(c == 0, bit_n, bit_w)
    b2 = jnp.where(c == 0, bit_w, bit_n)
    ours, theirs = 2 * c, 2 * (1 - c)
    order_of = [ours + b1, ours + 1 - b1, theirs + b2, theirs + 1 - b2]
    info = jnp.stack([counts[0, 0], b1, b2, *order_of]).astype(jnp.int32)
    split_rows = probe.reshape(4, 2, 2, h, size)
    probes = []
    for m, bit in zip(order_of, (b2, b2, b1, b1)):
        for part in range(2):
            mine = lax.dynamic_slice(split_rows, (m, part, bit, 0, 0), (1, 1, 1, h, size))
            other = lax.dynamic_slice(split_rows, (m, part, 1 - bit, 0, 0), (1, 1, 1, h, size))
            probes.append(jnp.concatenate([mine.reshape(h, size), other.reshape(h, size)], 0))

    leading, last = cut_corners(left_side, right_side, (roots, *probes))
    top_corners = shifted(last, "narrow", 1)
    bottom_corners = shifted(leading, "narrow", -1)
    sides = (left_side, right_side, top_side, bottom_side, top_corners, bottom_corners)
    patches, cover = cut_patches(offs, info, object_field, sides, size, slots)

    patch_gradients = []
    for batch in range(BATCHES):
        extra = cover if batch == 0 else None

        def ride(x):
            return x if extra is None else jnp.concatenate([x, extra], 0)

        sent, keep, gpatch, z = turn_kernel(tables, info, patches, probes, roots, extra, batch)
        got = core(sent)
        *q, gpatch = back_kernel(tables, info, patches, probes[2:4], z, keep, gpatch, batch, 1, (), ())
        if extra is not None:
            extra = extra + got[4 * size :]
        sent_a = jnp.concatenate([q[0], q[1]], 0) + got[2 * size : 3 * size]
        sent_b = jnp.concatenate([q[2], q[3]], 0) + got[3 * size : 4 * size]
        got_a = first(ride(sent_a))
        got_b = first(sent_b)
        after = (sent_a, sent_b)
        *q, gpatch = back_kernel(tables, info, patches, probes[:2], z, keep, gpatch, batch, 0, (got,), after)
        patch_gradients.append(gpatch)
        sent_a = q[1] + got_a[h:size]
        sent_b = q[3] + got_b[h:]
        a = q[0] + got_a[:h]
        b = q[2] + got_b[:h]
        if extra is not None:
            extra = extra + got_a[size:]
        got_a = second(ride(sent_a))
        got_b = second(sent_b)
        a = a + got_a[:h]
        b = b + got_b
        if extra is not None:
            extra = extra + got_a[h:]
        if batch == BATCHES - 1:
            inside, upper, lower, left_part, right_part = place_gradients(offs, info, patch_gradients, (a, b), edge)
            from_below = shifted(upper, "narrow", -1)
            from_above = shifted(lower, "narrow", 1)
        for exchange in rest:
            got_a = exchange(ride(a))
            got_b = exchange(b)
            a = a + got_a[:h]
            b = b + got_b
            if extra is not None:
                extra = extra + got_a[h:]
        if extra is not None:
            scales = jnp.sum(extra, axis=1) / (size * size)
        a = probes[0][:h] - a / scales[batch]
        b = probes[1][:h] - b / scales[batch]
        a = jnp.concatenate([a, second(a)], 0)
        b = jnp.concatenate([b, second(b)], 0)
        own = [a, b, first(a), first(b)]
        probes = own + [core(x) for x in own]

    to_left, to_right = side_borders(left_part, right_part, from_below, from_above, own[:2])
    from_right = shifted(to_left, "wide", -1)
    from_left = shifted(to_right, "wide", 1)
    probe_new, top = probe_kernel(info, probes)
    updated = object_kernel(top, object_field, inside, from_below, from_above)
    return (side_kernel(top, updated, from_right, from_left), probe_new)


def solution(mesh):
    placed = (
        P(None, "narrow", "wide"),
        P(),
        P("narrow", "wide", None, None, None),
        P("narrow", "wide", None, None),
        P("narrow", "wide"),
    )
    return jax.shard_map(
        local,
        mesh=mesh,
        in_specs=placed,
        out_specs=(P(None, "narrow", "wide"), P()),
        check_vma=False,
    )
```

```python
import functools

import jax
import jax.numpy as jnp
import ml_dtypes
import numpy as np
from jax import lax
from jax.experimental import pallas as pl
from jax.experimental.pallas import tpu as pltpu
from jax.sharding import PartitionSpec as P

H = 128
BATCHES = 3
POS = 2
AXES = ("wide", "narrow")
F32 = jnp.float32
BF16 = jnp.bfloat16
VMEM_LIMIT = 32 * 1024 * 1024
VMEM_KERNEL = 24 * 1024 * 1024


def halves(table):
    high = table.astype(ml_dtypes.bfloat16)
    low = (table - high.astype(np.float64)).astype(ml_dtypes.bfloat16)
    return np.stack([high, low])


def dft_tables(size):
    half = size // 2
    k = np.arange(half)
    out = []
    for odd in range(2):
        phase = ((2 * k[:, None] + odd) * k[None, :]) % size
        angle = -2.0 * np.pi * phase / size
        re, im = np.cos(angle) / np.sqrt(size), np.sin(angle) / np.sqrt(size)
        out.append(np.block([[re, -im], [im, re]]))
    return np.stack([halves(t) for t in (out[0], out[1], out[0].T, out[1].T)])


def split(x):
    high = x.astype(BF16)
    return high, (x - high.astype(F32)).astype(BF16)


def dot(a, b):
    return jnp.dot(a, b, preferred_element_type=F32)


def left(tables, which, x):
    high, low = split(x)
    t_high, t_low = tables[which, 0], tables[which, 1]
    return dot(t_high, high) + dot(t_high, low) + dot(t_low, high)


def right(x, tables, which):
    high, low = split(x)
    t_high, t_low = tables[which, 0], tables[which, 1]
    return dot(high, t_high) + dot(low, t_high) + dot(high, t_low)


def forward(tables, re, im):
    h = re.shape[0] // 2
    u = jnp.concatenate([re[:h] + re[h:], im[:h] + im[h:]], 0)
    v = jnp.concatenate([re[:h] - re[h:], im[:h] - im[h:]], 0)
    even, odd = left(tables, 0, u), left(tables, 1, v)

    def columns(op):
        rows = [jnp.concatenate([op(y[:h, :h], y[:h, h:]), op(y[h:, :h], y[h:, h:])], 1) for y in (even, odd)]
        return jnp.concatenate(rows, 0)

    return (
        right(columns(lambda a, b: a + b), tables, 2),
        right(columns(lambda a, b: a - b), tables, 3),
    )


def inverse(tables, even, odd):
    h = even.shape[0] // 2
    a, b = right(even, tables, 0), right(odd, tables, 1)
    s, d = a + b, a - b

    def rows(lo):
        return jnp.concatenate(
            [
                jnp.concatenate([s[lo : lo + h, :h], d[lo : lo + h, :h]], 1),
                jnp.concatenate([s[lo : lo + h, h:], d[lo : lo + h, h:]], 1),
            ],
            0,
        )

    a, b = left(tables, 2, rows(0)), left(tables, 3, rows(h))
    s, d = a + b, a - b
    return jnp.concatenate([s[:h], d[:h]], 0), jnp.concatenate([s[h:], d[h:]], 0)


def power_of(z):
    h = z.shape[-1] // 2
    return z[:, :h] * z[:, :h] + z[:, h:] * z[:, h:]


def place_of(which, bit, h):
    return pl.multiple_of(jnp.where(bit == which, 0, h), h)


def rows_of(ref, bit):
    h = ref.shape[0] // 2
    return jnp.concatenate([ref[pl.ds(place_of(which, bit, h), h)] for which in range(2)], 0)


def add_rows(ref, base, bit, value):
    h = value.shape[0] // 2
    for which in range(2):
        ref[pl.ds(base + place_of(which, bit, h), h)] += value[which * h : (which + 1) * h]


def illuminated(tables, patch, probe):
    (p_re, p_im), (o_re, o_im) = probe, (patch[0, 0], patch[0, 1])
    return forward(tables, p_re * o_re - p_im * o_im, p_re * o_im + p_im * o_re)


def gradients(tables, patch, probe, spectrum, keep, pgrad, base, bit, gpatch):
    size = patch.shape[-1]
    k_even, k_odd = keep[0, 0], keep[0, 1]
    b_re, b_im = inverse(
        tables,
        spectrum[0] * jnp.concatenate([k_even, k_even], 1),
        spectrum[1] * jnp.concatenate([k_odd, k_odd], 1),
    )
    (p_re, p_im), (o_re, o_im) = probe, (patch[0, 0], patch[0, 1])
    gpatch[0, 0] += p_re * b_re + p_im * b_im
    gpatch[0, 1] += p_re * b_im - p_im * b_re
    add_rows(pgrad, base, bit, o_re * b_re + o_im * b_im)
    add_rows(pgrad, base + size, bit, o_re * b_im - o_im * b_re)


def whole(*shape):
    return pl.BlockSpec(shape, lambda i, *_: (0,) * len(shape))


def per_slot(*shape):
    return pl.BlockSpec((1, *shape), lambda i, *_: (i,) + (0,) * len(shape))


def per_batch_slot(batch, *shape):
    return pl.BlockSpec((1, *shape), lambda i, *_: (batch * POS + i,) + (0,) * len(shape))


def call(body, scalars, operands, in_specs, out_shapes, out_specs, grid, scratch=(), aliases=None, flops=0, moved=0):
    return pl.pallas_call(
        body,
        out_shape=[jax.ShapeDtypeStruct(s, F32) for s in out_shapes],
        grid_spec=pltpu.PrefetchScalarGridSpec(
            num_scalar_prefetch=len(scalars),
            grid=(grid,),
            in_specs=in_specs,
            out_specs=out_specs,
            scratch_shapes=list(scratch),
        ),
        input_output_aliases=aliases or {},
        compiler_params=pltpu.CompilerParams(vmem_limit_bytes=VMEM_LIMIT),
        cost_estimate=pl.CostEstimate(flops=flops, bytes_accessed=moved, transcendentals=0),
    )(*scalars, *operands)


def corner_of(offs, slot, full, size):
    row = offs[2 * slot] + H
    col = offs[2 * slot + 1] + H
    row_at = pl.multiple_of(jnp.minimum(row // 8 * 8, full - size - 8), 8)
    col_at = pl.multiple_of(jnp.minimum(col // 128 * 128, full - size - 128), 128)
    return row_at, col_at, row - row_at, col - col_at


def shift_in(block, row, col):
    rows, columns = block.shape
    turn = lax.rem(128 - col, 128)
    tiles = [pltpu.roll(block[:, at : at + 128], turn, 1) for at in range(0, columns, 128)]
    here = lax.broadcasted_iota(jnp.int32, (rows, 128), 1) < 128 - col
    block = jnp.concatenate([jnp.where(here, a, b) for a, b in zip(tiles, tiles[1:])], 1)
    block = pltpu.roll(block.reshape(rows // 8, 8, columns - 128), lax.rem(8 - row, 8), 1)
    here = lax.broadcasted_iota(jnp.int32, (rows // 8 - 1, 8, columns - 128), 1) < 8 - row
    return jnp.where(here, block[:-1], block[1:]).reshape(rows - 8, columns - 128)


def shift_out(block, row, col):
    rows, columns = block.shape
    block = pltpu.roll(block.reshape(rows // 8, 8, columns), lax.rem(row, 8), 1)
    zero = jnp.zeros((1, 8, columns), F32)
    here = lax.broadcasted_iota(jnp.int32, (rows // 8 + 1, 8, columns), 1) >= row
    block = jnp.where(here, jnp.concatenate([block, zero], 0), jnp.concatenate([zero, block], 0))
    block = block.reshape(rows + 8, columns)
    zero = jnp.zeros((rows + 8, 128), F32)
    tiles = [zero] + [pltpu.roll(block[:, at : at + 128], lax.rem(col, 128), 1) for at in range(0, columns, 128)] + [zero]
    here = lax.broadcasted_iota(jnp.int32, (rows + 8, 128), 1) >= col
    return jnp.concatenate([jnp.where(here, b, a) for a, b in zip(tiles, tiles[1:])], 1)


def cut_corners(left_side, right_side, after):
    edge = left_side.shape[1]

    def body(left_ref, right_ref, *rest):
        leading, last, sems = rest[-3:]
        copies = [
            pltpu.make_async_copy(ref.at[:, rows], out.at[:, :, columns], sems.at[2 * k + at])
            for k, (out, rows) in enumerate(((leading, slice(0, H)), (last, slice(edge - H, edge))))
            for at, (ref, columns) in enumerate(((left_ref, slice(0, H)), (right_ref, slice(H, 2 * H))))
        ]
        for copy in copies:
            copy.start()
        for copy in copies:
            copy.wait()

    return call(
        body,
        [],
        [left_side, right_side, *after],
        [pl.BlockSpec(memory_space=pl.ANY)] * (2 + len(after)),
        [(2, H, 2 * H)] * 2,
        [whole(2, H, 2 * H)] * 2,
        1,
        scratch=[pltpu.SemaphoreType.DMA((4,))],
        flops=10**5,
        moved=2 * 10**6,
    )


def cut_patches(offsets, info, tile, sides, size, slots):
    edge = tile.shape[1]
    full = edge + 2 * H
    low, mid, high = slice(0, H), slice(H, H + edge), slice(H + edge, full)
    first_half, second_half, everything = slice(0, H), slice(H, 2 * H), slice(None)
    pieces = [
        (0, everything, mid, mid),
        (1, everything, mid, low),
        (2, everything, mid, high),
        (3, everything, low, mid),
        (4, everything, high, mid),
        (5, first_half, low, low),
        (5, second_half, low, high),
        (6, first_half, high, low),
        (6, second_half, high, high),
    ]

    def body(offs, info_ref, *refs):
        sources, (out, cover, ext, sems) = refs[:7], refs[7:]
        i = pl.program_id(0)

        @pl.when(i == 0)
        def _():
            copies = [
                pltpu.make_async_copy(sources[k].at[:, :, part], ext.at[:, rows, columns], sems.at[j])
                for j, (k, part, rows, columns) in enumerate(pieces)
            ]
            for copy in copies:
                copy.start()
            cover[...] = jnp.zeros_like(cover)
            for copy in copies:
                copy.wait()

        @pl.when(i < info_ref[0])
        def _():
            row_at, col_at, row, col = corner_of(offs, i, full, size)
            total = jnp.zeros((1, size), F32)
            for part in range(2):
                block = shift_in(ext[part, pl.ds(row_at, size + 8), pl.ds(col_at, size + 128)], row, col)
                out[0, part] = block
                total = total + jnp.sum(block * block, axis=0, keepdims=True)
            here = lax.broadcasted_iota(jnp.int32, cover.shape, 0) == i // POS
            cover[...] += jnp.where(here, total, 0.0)

    return call(
        body,
        [offsets, info],
        [tile, *sides],
        [pl.BlockSpec(memory_space=pl.ANY)] * 7,
        [(slots, 2, size, size), (8, size)],
        [per_slot(2, size, size), whole(8, size)],
        slots,
        scratch=[pltpu.VMEM((2, full, full), F32), pltpu.SemaphoreType.DMA((len(pieces),))],
        flops=10**6,
        moved=8 * 10**6,
    )


def place_gradients(offsets, info, patches, after, edge):
    size = patches[0].shape[-1]
    full = edge + 2 * H
    n = len(patches)

    def body(offs, info_ref, *refs):
        patch_refs, (core, upper, lower, left_part, right_part, ext) = refs[:n], refs[n + len(after) :]
        i = pl.program_id(0)

        @pl.when(i == 0)
        def _():
            ext[...] = jnp.zeros_like(ext)

        for batch in range(n):

            @pl.when((i // POS == batch) & (i < info_ref[0]))
            def _():
                row_at, col_at, row, col = corner_of(offs, i, full, size)
                for part in range(2):
                    block = shift_out(patch_refs[batch][0, part], row, col)
                    ext[part, pl.ds(row_at, size + 8), pl.ds(col_at, size + 128)] += block

        @pl.when(i == n * POS - 1)
        def _():
            core[...] = ext[:, H : H + edge, H : H + edge]
            upper[...] = ext[:, :H]
            lower[...] = ext[:, H + edge :]
            left_part[...] = ext[:, H : H + edge, :H]
            right_part[...] = ext[:, H : H + edge, H + edge :]

    def spec(batch):
        return pl.BlockSpec((1, 2, size, size), lambda i, *_: (jnp.clip(i - batch * POS, 0, POS - 1), 0, 0, 0))

    shapes = [(2, edge, edge), (2, H, full), (2, H, full), (2, edge, H), (2, edge, H)]
    return call(
        body,
        [offsets, info],
        [*patches, *after],
        [spec(batch) for batch in range(n)] + [pl.BlockSpec(memory_space=pl.ANY)] * len(after),
        shapes,
        [whole(*shape) for shape in shapes],
        n * POS,
        scratch=[pltpu.VMEM((2, full, full), F32)],
        flops=10**6,
        moved=10**7,
    )


def side_borders(left_part, right_part, from_below, from_above, after):
    edge = left_part.shape[1]
    full = from_below.shape[2]

    def body(left_ref, right_ref, below, above, *rest):
        for ref, out, at in ((left_ref, rest[-2], 0), (right_ref, rest[-1], H + edge)):
            out[...] = ref[...]
            out[:, edge - H :] += below[:, :, at : at + H]
            out[:, :H] += above[:, :, at : at + H]

    return call(
        body,
        [],
        [left_part, right_part, from_below, from_above, *after],
        [whole(2, edge, H)] * 2 + [whole(2, H, full)] * 2 + [pl.BlockSpec(memory_space=pl.ANY)] * len(after),
        [(2, edge, H)] * 2,
        [whole(2, edge, H)] * 2,
        1,
        flops=10**5,
        moved=4 * 10**6,
    )


def call_in_vmem(body, info, operands, out_shapes, scratch=(), after=(), flops=0, moved=0):
    vmem = pl.BlockSpec(memory_space=pltpu.VMEM)
    return pl.pallas_call(
        body,
        out_shape=[pltpu.VMEM(s, F32) for s in out_shapes],
        in_specs=[pl.BlockSpec(memory_space=pltpu.SMEM)]
        + [vmem] * len(operands)
        + [pl.BlockSpec(memory_space=pl.ANY)] * len(after),
        out_specs=[vmem] * len(out_shapes),
        scratch_shapes=list(scratch),
        compiler_params=pltpu.CompilerParams(vmem_limit_bytes=VMEM_KERNEL),
        cost_estimate=pl.CostEstimate(flops=flops, bytes_accessed=moved, transcendentals=0),
    )(info, *[pltpu.with_memory_space_constraint(x, pltpu.VMEM) for x in operands], *after)


def turn_kernel(tables, info, patches, probes, roots, cover, batch):
    size = patches.shape[-1]
    h = size // 2
    rows = 4 * size
    extra = 0 if cover is None else cover.shape[0]

    def body(info_ref, t, patches_ref, roots_ref, *rest):
        p, rest = rest[:8], rest[8:]
        if extra:
            cover_ref, rest = rest[0], rest[1:]
        sent, keeps, gpatches, z, scratch = rest
        sent[:rows] = jnp.zeros((rows, size), F32)
        if extra:
            sent[rows:] = cover_ref[...]
        gpatches[...] = jnp.zeros_like(gpatches)
        for i in range(POS):
            slot = batch * POS + i
            patch, root = patches_ref.at[slot : slot + 1], roots_ref.at[slot : slot + 1]
            keep, gpatch = keeps.at[i : i + 1], gpatches.at[i : i + 1]

            @pl.when(slot < info_ref[0])
            def _():
                bits = [info_ref[2], info_ref[2], info_ref[1], info_ref[1]]
                totals = [0.0, 0.0]
                for m in range(4):
                    pair = illuminated(t, patch, (rows_of(p[2 * m], bits[m]), rows_of(p[2 * m + 1], bits[m])))
                    for e in range(2):
                        if m < 2:
                            z[i, m, e] = pair[e]
                        else:
                            scratch[m - 2, e] = pair[e]
                        totals[e] = totals[e] + power_of(pair[e])
                for e in range(2):
                    keep[0, e] = 1.0 - root[0, e] * lax.rsqrt(totals[e] + 0.1)
                for m in range(2, 4):
                    probe = (rows_of(p[2 * m], bits[m]), rows_of(p[2 * m + 1], bits[m]))
                    spectrum = (scratch[m - 2, 0], scratch[m - 2, 1])
                    gradients(t, patch, probe, spectrum, keep, sent, (m - 2) * 2 * size, bits[m], gpatch)

    return call_in_vmem(
        body,
        info,
        [tables, patches, roots, *probes] + ([cover] if extra else []),
        [(rows + extra, size), (POS, 2, size, h), (POS, 2, size, size), (POS, 2, 2, size, size)],
        scratch=[pltpu.VMEM((2, 2, size, size), F32)],
        flops=POS * 6 * 24 * size**3,
        moved=8 * 10**6,
    )


def back_kernel(tables, info, patches, probe, spectra, keeps, gpatches, batch, mode, start, after):
    size = patches.shape[-1]
    h = size // 2

    def body(info_ref, t, patches_ref, z, keeps_ref, g_in, p_re, p_im, *rest):
        quarters, g_out, pgrad = rest[-6:-2], rest[-2], rest[-1]
        if start:
            pgrad[...] = rest[0][: 2 * size]
        else:
            pgrad[...] = jnp.zeros_like(pgrad)
        g_out[...] = g_in[...]
        for i in range(POS):
            slot = batch * POS + i
            patch, keep, gpatch = patches_ref.at[slot : slot + 1], keeps_ref.at[i : i + 1], g_out.at[i : i + 1]

            @pl.when(slot < info_ref[0])
            def _():
                bit = info_ref[2]
                pair = (rows_of(p_re, bit), rows_of(p_im, bit))
                gradients(t, patch, pair, (z[i, mode, 0], z[i, mode, 1]), keep, pgrad, 0, bit, gpatch)

        for at, out in enumerate(quarters):
            out[...] = pgrad[at * h : (at + 1) * h]

    return call_in_vmem(
        body,
        info,
        [tables, patches, spectra, keeps, gpatches, *probe, *start],
        [(h, size)] * 4 + [(POS, 2, size, size)],
        scratch=[pltpu.VMEM((2 * size, size), F32)],
        after=after,
        flops=POS * 24 * size**3,
        moved=4 * 10**6,
    )


def probe_kernel(info, probes):
    size = probes[0].shape[0]

    def body(info_ref, *refs):
        p, (probe_out, top, power) = refs[:8], refs[8:]
        i = pl.program_id(0)
        for m in range(4):

            @pl.when(i == m)
            def _():
                bit = info_ref[2] if m < 2 else info_ref[1]
                re, im = rows_of(p[2 * m], bit), rows_of(p[2 * m + 1], bit)
                probe_out[0, 0], probe_out[0, 1] = re, im
                square = re * re + im * im
                power[...] = square if m == 0 else power[...] + square

        @pl.when(i == 3)
        def _():
            top[...] = jnp.broadcast_to(jnp.max(power[...], keepdims=True), top.shape)

    return call(
        body,
        [info],
        probes,
        [whole(size, size)] * 8,
        [(4, 2, size, size), (8, 128)],
        [pl.BlockSpec((1, 2, size, size), lambda i, info_ref: (info_ref[3 + i], 0, 0, 0)), whole(8, 128)],
        4,
        scratch=[pltpu.VMEM((size, size), F32)],
        flops=10**6,
        moved=4 * 10**6,
    )


def object_kernel(top, field, core, from_below, from_above):
    edge = field.shape[1]
    full = from_below.shape[2]
    steps = edge // H

    def body(top_ref, o, g, fb, fa, out):
        i = pl.program_id(0)
        step = (0.5 / top_ref[:1, :1])[None]
        out[...] = o[...] - step * g[...]

        @pl.when(i == steps - 1)
        def _():
            out[...] -= step * fb[:, :, H : H + edge]

        @pl.when(i == 0)
        def _():
            out[...] -= step * fa[:, :, H : H + edge]

    band = pl.BlockSpec((2, H, edge), lambda i: (0, i, 0))
    return call(
        body,
        [],
        [top, field, core, from_below, from_above],
        [whole(8, 128), band, band, whole(2, H, full), whole(2, H, full)],
        [field.shape],
        [band],
        steps,
        flops=10**6,
        moved=8 * 10**6,
    )[0]


def side_kernel(top, updated, from_right, from_left):
    edge = updated.shape[1]

    def body(top_ref, x, fr, fl, out):
        i = pl.program_id(0)
        step = (0.5 / top_ref[:1, :1])[None]

        @pl.when(i == 0)
        def _():
            out[...] = x[...] - step * fl[...]

        @pl.when(i == 1)
        def _():
            out[...] = x[...] - step * fr[...]

    side = pl.BlockSpec((2, edge, H), lambda i: (0, 0, i * (edge // H - 1)))
    return call(
        body,
        [],
        [top, updated, from_right, from_left],
        [whole(8, 128), side, whole(2, edge, H), whole(2, edge, H)],
        [updated.shape],
        [side],
        2,
        aliases={1: 0},
        flops=10**5,
        moved=4 * 10**6,
    )[0]


def flips(wide, narrow):
    bits = [(0, 2 << i) for i in range(1, narrow.bit_length() - 2)] + [
        (1 << i, 0) for i in range(1, wide.bit_length() - 1)
    ]

    def exchange(even, odd):
        pairs = []
        for w in range(wide):
            for n in range(narrow):
                dw, dn = odd if n & 1 else even
                pairs.append((w * narrow + n, (w ^ dw) * narrow + (n ^ dn)))
        return functools.partial(lax.ppermute, axis_name=AXES, perm=pairs)

    core = exchange((0, 1), (0, 1))
    first = exchange((0, 2), (1, 0))
    second = exchange((1, 0), (0, 2))
    return core, first, second, [exchange(a, b) for a, b in zip(bits, bits[::-1])]


def shifted(value, axis, steps):
    count = lax.axis_size(axis)
    leading, last = (max(0, -steps), min(count, count - steps))
    return lax.ppermute(value, axis, [(source, source + steps) for source in range(leading, last)])


def local(object_field, probe, patterns, offsets, counts):
    edge = object_field.shape[1]
    size = probe.shape[-1]
    slots = patterns.shape[2]
    h = size // 2
    wide, narrow = lax.axis_size("wide"), lax.axis_size("narrow")
    w, n = lax.axis_index("wide"), lax.axis_index("narrow")
    core, first, second, rest = flips(wide, narrow)
    offs = offsets.reshape(slots * 2)

    left_side = shifted(object_field[:, :, edge - H :], "wide", 1)
    right_side = shifted(object_field[:, :, :H], "wide", -1)
    top_side = shifted(object_field[:, edge - H :], "narrow", 1)
    bottom_side = shifted(object_field[:, :H], "narrow", -1)

    tables = jnp.asarray(dft_tables(size))
    order = np.concatenate([np.arange(0, size, 2), np.arange(1, size, 2)])
    pick = jnp.asarray(np.eye(size, dtype=np.float32)[order])
    roots = jnp.einsum("pj,sjk->spk", pick, jnp.sqrt(patterns[0, 0]), precision=lax.Precision.HIGHEST)
    roots = jnp.einsum("spk,qk->spq", roots, pick, precision=lax.Precision.HIGHEST)
    roots = roots.reshape(slots, size, 2, h).transpose(0, 2, 1, 3)

    c = n % 2
    bit_n, bit_w = (n // 2) % 2, w % 2
    b1 = jnp.where(c == 0, bit_n, bit_w)
    b2 = jnp.where(c == 0, bit_w, bit_n)
    ours, theirs = 2 * c, 2 * (1 - c)
    order_of = [ours + b1, ours + 1 - b1, theirs + b2, theirs + 1 - b2]
    info = jnp.stack([counts[0, 0], b1, b2, *order_of]).astype(jnp.int32)
    split_rows = probe.reshape(4, 2, 2, h, size)
    probes = []
    for m, bit in zip(order_of, (b2, b2, b1, b1)):
        for part in range(2):
            mine = lax.dynamic_slice(split_rows, (m, part, bit, 0, 0), (1, 1, 1, h, size))
            other = lax.dynamic_slice(split_rows, (m, part, 1 - bit, 0, 0), (1, 1, 1, h, size))
            probes.append(jnp.concatenate([mine.reshape(h, size), other.reshape(h, size)], 0))

    leading, last = cut_corners(left_side, right_side, (roots, *probes))
    top_corners = shifted(last, "narrow", 1)
    bottom_corners = shifted(leading, "narrow", -1)
    sides = (left_side, right_side, top_side, bottom_side, top_corners, bottom_corners)
    patches, cover = cut_patches(offs, info, object_field, sides, size, slots)

    patch_gradients = []
    for batch in range(BATCHES):
        extra = cover if batch == 0 else None

        def ride(x):
            return x if extra is None else jnp.concatenate([x, extra], 0)

        sent, keep, gpatch, z = turn_kernel(tables, info, patches, probes, roots, extra, batch)
        got = core(sent)
        *q, gpatch = back_kernel(tables, info, patches, probes[2:4], z, keep, gpatch, batch, 1, (), ())
        if extra is not None:
            extra = extra + got[4 * size :]
        sent_a = jnp.concatenate([q[0], q[1]], 0) + got[2 * size : 3 * size]
        sent_b = jnp.concatenate([q[2], q[3]], 0) + got[3 * size : 4 * size]
        got_a = first(ride(sent_a))
        got_b = first(sent_b)
        after = (sent_a, sent_b)
        *q, gpatch = back_kernel(tables, info, patches, probes[:2], z, keep, gpatch, batch, 0, (got,), after)
        patch_gradients.append(gpatch)
        sent_a = q[1] + got_a[h:size]
        sent_b = q[3] + got_b[h:]
        a = q[0] + got_a[:h]
        b = q[2] + got_b[:h]
        if extra is not None:
            extra = extra + got_a[size:]
        got_a = second(ride(sent_a))
        got_b = second(sent_b)
        a = a + got_a[:h]
        b = b + got_b
        if extra is not None:
            extra = extra + got_a[h:]
        if batch == BATCHES - 1:
            inside, upper, lower, left_part, right_part = place_gradients(offs, info, patch_gradients, (a, b), edge)
            from_below = shifted(upper, "narrow", -1)
            from_above = shifted(lower, "narrow", 1)
        for exchange in rest:
            got_a = exchange(ride(a))
            got_b = exchange(b)
            a = a + got_a[:h]
            b = b + got_b
            if extra is not None:
                extra = extra + got_a[h:]
        if extra is not None:
            scales = jnp.sum(extra, axis=1) / (size * size)
        a = probes[0][:h] - a / scales[batch]
        b = probes[1][:h] - b / scales[batch]
        shards = [a, b]
        a = jnp.concatenate([a, second(a)], 0)
        b = jnp.concatenate([b, second(b)], 0)
        own = [a, b, first(a), first(b)]
        probes = own + [core(x) for x in own]

    to_left, to_right = side_borders(left_part, right_part, from_below, from_above, shards)
    from_right = shifted(to_left, "wide", -1)
    from_left = shifted(to_right, "wide", 1)
    probe_new, top = probe_kernel(info, probes)
    updated = object_kernel(top, object_field, inside, from_below, from_above)
    return (side_kernel(top, updated, from_right, from_left), probe_new)


def solution(mesh):
    placed = (
        P(None, "narrow", "wide"),
        P(),
        P("narrow", "wide", None, None, None),
        P("narrow", "wide", None, None),
        P("narrow", "wide"),
    )
    return jax.shard_map(
        local,
        mesh=mesh,
        in_specs=placed,
        out_specs=(P(None, "narrow", "wide"), P()),
        check_vma=False,
    )
```

```python
import functools

import jax
import jax.numpy as jnp
import ml_dtypes
import numpy as np
from jax import lax
from jax.experimental import pallas as pl
from jax.experimental.pallas import tpu as pltpu
from jax.sharding import PartitionSpec as P

H = 128
BATCHES = 3
POS = 2
AXES = ("wide", "narrow")
F32 = jnp.float32
BF16 = jnp.bfloat16
VMEM_LIMIT = 32 * 1024 * 1024
VMEM_KERNEL = 24 * 1024 * 1024


def halves(table):
    high = table.astype(ml_dtypes.bfloat16)
    low = (table - high.astype(np.float64)).astype(ml_dtypes.bfloat16)
    return np.stack([high, low])


def dft_tables(size):
    half = size // 2
    k = np.arange(half)
    out = []
    for odd in range(2):
        phase = ((2 * k[:, None] + odd) * k[None, :]) % size
        angle = -2.0 * np.pi * phase / size
        re, im = np.cos(angle) / np.sqrt(size), np.sin(angle) / np.sqrt(size)
        out.append(np.block([[re, -im], [im, re]]))
    return np.stack([halves(t) for t in (out[0], out[1], out[0].T, out[1].T)])


def split(x):
    high = x.astype(BF16)
    return high, (x - high.astype(F32)).astype(BF16)


def dot(a, b):
    return jnp.dot(a, b, preferred_element_type=F32)


def left(tables, which, x):
    high, low = split(x)
    t_high, t_low = tables[which, 0], tables[which, 1]
    return dot(t_high, high) + dot(t_high, low) + dot(t_low, high)


def right(x, tables, which):
    high, low = split(x)
    t_high, t_low = tables[which, 0], tables[which, 1]
    return dot(high, t_high) + dot(low, t_high) + dot(high, t_low)


def forward(tables, re, im):
    h = re.shape[0] // 2
    u = jnp.concatenate([re[:h] + re[h:], im[:h] + im[h:]], 0)
    v = jnp.concatenate([re[:h] - re[h:], im[:h] - im[h:]], 0)
    even, odd = left(tables, 0, u), left(tables, 1, v)

    def columns(op):
        rows = [jnp.concatenate([op(y[:h, :h], y[:h, h:]), op(y[h:, :h], y[h:, h:])], 1) for y in (even, odd)]
        return jnp.concatenate(rows, 0)

    return (
        right(columns(lambda a, b: a + b), tables, 2),
        right(columns(lambda a, b: a - b), tables, 3),
    )


def inverse(tables, even, odd):
    h = even.shape[0] // 2
    a, b = right(even, tables, 0), right(odd, tables, 1)
    s, d = a + b, a - b

    def rows(lo):
        return jnp.concatenate(
            [
                jnp.concatenate([s[lo : lo + h, :h], d[lo : lo + h, :h]], 1),
                jnp.concatenate([s[lo : lo + h, h:], d[lo : lo + h, h:]], 1),
            ],
            0,
        )

    a, b = left(tables, 2, rows(0)), left(tables, 3, rows(h))
    s, d = a + b, a - b
    return jnp.concatenate([s[:h], d[:h]], 0), jnp.concatenate([s[h:], d[h:]], 0)


def power_of(z):
    h = z.shape[-1] // 2
    return z[:, :h] * z[:, :h] + z[:, h:] * z[:, h:]


def place_of(which, bit, h):
    return pl.multiple_of(jnp.where(bit == which, 0, h), h)


def rows_of(ref, bit):
    h = ref.shape[0] // 2
    return jnp.concatenate([ref[pl.ds(place_of(which, bit, h), h)] for which in range(2)], 0)


def add_rows(ref, base, bit, value):
    h = value.shape[0] // 2
    for which in range(2):
        ref[pl.ds(base + place_of(which, bit, h), h)] += value[which * h : (which + 1) * h]


def illuminated(tables, patch, probe):
    (p_re, p_im), (o_re, o_im) = probe, (patch[0, 0], patch[0, 1])
    return forward(tables, p_re * o_re - p_im * o_im, p_re * o_im + p_im * o_re)


def gradients(tables, patch, probe, spectrum, keep, pgrad, base, bit, gpatch):
    size = patch.shape[-1]
    k_even, k_odd = keep[0, 0], keep[0, 1]
    b_re, b_im = inverse(
        tables,
        spectrum[0] * jnp.concatenate([k_even, k_even], 1),
        spectrum[1] * jnp.concatenate([k_odd, k_odd], 1),
    )
    (p_re, p_im), (o_re, o_im) = probe, (patch[0, 0], patch[0, 1])
    gpatch[0, 0] += p_re * b_re + p_im * b_im
    gpatch[0, 1] += p_re * b_im - p_im * b_re
    add_rows(pgrad, base, bit, o_re * b_re + o_im * b_im)
    add_rows(pgrad, base + size, bit, o_re * b_im - o_im * b_re)


def whole(*shape):
    return pl.BlockSpec(shape, lambda i, *_: (0,) * len(shape))


def per_slot(*shape):
    return pl.BlockSpec((1, *shape), lambda i, *_: (i,) + (0,) * len(shape))


def per_batch_slot(batch, *shape):
    return pl.BlockSpec((1, *shape), lambda i, *_: (batch * POS + i,) + (0,) * len(shape))


def call(body, scalars, operands, in_specs, out_shapes, out_specs, grid, scratch=(), aliases=None, flops=0, moved=0):
    return pl.pallas_call(
        body,
        out_shape=[jax.ShapeDtypeStruct(s, F32) for s in out_shapes],
        grid_spec=pltpu.PrefetchScalarGridSpec(
            num_scalar_prefetch=len(scalars),
            grid=(grid,),
            in_specs=in_specs,
            out_specs=out_specs,
            scratch_shapes=list(scratch),
        ),
        input_output_aliases=aliases or {},
        compiler_params=pltpu.CompilerParams(vmem_limit_bytes=VMEM_LIMIT),
        cost_estimate=pl.CostEstimate(flops=flops, bytes_accessed=moved, transcendentals=0),
    )(*scalars, *operands)


def corner_of(offs, slot, full, size):
    row = offs[2 * slot] + H
    col = offs[2 * slot + 1] + H
    row_at = pl.multiple_of(jnp.minimum(row // 8 * 8, full - size - 8), 8)
    col_at = pl.multiple_of(jnp.minimum(col // 128 * 128, full - size - 128), 128)
    return row_at, col_at, row - row_at, col - col_at


def shift_in(block, row, col):
    rows, columns = block.shape
    turn = lax.rem(128 - col, 128)
    tiles = [pltpu.roll(block[:, at : at + 128], turn, 1) for at in range(0, columns, 128)]
    here = lax.broadcasted_iota(jnp.int32, (rows, 128), 1) < 128 - col
    block = jnp.concatenate([jnp.where(here, a, b) for a, b in zip(tiles, tiles[1:])], 1)
    block = pltpu.roll(block.reshape(rows // 8, 8, columns - 128), lax.rem(8 - row, 8), 1)
    here = lax.broadcasted_iota(jnp.int32, (rows // 8 - 1, 8, columns - 128), 1) < 8 - row
    return jnp.where(here, block[:-1], block[1:]).reshape(rows - 8, columns - 128)


def shift_out(block, row, col):
    rows, columns = block.shape
    block = pltpu.roll(block.reshape(rows // 8, 8, columns), lax.rem(row, 8), 1)
    zero = jnp.zeros((1, 8, columns), F32)
    here = lax.broadcasted_iota(jnp.int32, (rows // 8 + 1, 8, columns), 1) >= row
    block = jnp.where(here, jnp.concatenate([block, zero], 0), jnp.concatenate([zero, block], 0))
    block = block.reshape(rows + 8, columns)
    zero = jnp.zeros((rows + 8, 128), F32)
    tiles = [zero] + [pltpu.roll(block[:, at : at + 128], lax.rem(col, 128), 1) for at in range(0, columns, 128)] + [zero]
    here = lax.broadcasted_iota(jnp.int32, (rows + 8, 128), 1) >= col
    return jnp.concatenate([jnp.where(here, b, a) for a, b in zip(tiles, tiles[1:])], 1)


def cut_corners(left_side, right_side, after):
    edge = left_side.shape[1]

    def body(left_ref, right_ref, *rest):
        leading, last, sems = rest[-3:]
        copies = [
            pltpu.make_async_copy(ref.at[:, rows], out.at[:, :, columns], sems.at[2 * k + at])
            for k, (out, rows) in enumerate(((leading, slice(0, H)), (last, slice(edge - H, edge))))
            for at, (ref, columns) in enumerate(((left_ref, slice(0, H)), (right_ref, slice(H, 2 * H))))
        ]
        for copy in copies:
            copy.start()
        for copy in copies:
            copy.wait()

    return call(
        body,
        [],
        [left_side, right_side, *after],
        [pl.BlockSpec(memory_space=pl.ANY)] * (2 + len(after)),
        [(2, H, 2 * H)] * 2,
        [whole(2, H, 2 * H)] * 2,
        1,
        scratch=[pltpu.SemaphoreType.DMA((4,))],
        flops=10**5,
        moved=2 * 10**6,
    )


def cut_patches(offsets, info, tile, sides, size, slots):
    edge = tile.shape[1]
    full = edge + 2 * H
    low, mid, high = slice(0, H), slice(H, H + edge), slice(H + edge, full)
    first_half, second_half, everything = slice(0, H), slice(H, 2 * H), slice(None)
    pieces = [
        (0, everything, mid, mid),
        (1, everything, mid, low),
        (2, everything, mid, high),
        (3, everything, low, mid),
        (4, everything, high, mid),
        (5, first_half, low, low),
        (5, second_half, low, high),
        (6, first_half, high, low),
        (6, second_half, high, high),
    ]

    def body(offs, info_ref, *refs):
        sources, (out, cover, ext, sems) = refs[:7], refs[7:]
        i = pl.program_id(0)

        @pl.when(i == 0)
        def _():
            copies = [
                pltpu.make_async_copy(sources[k].at[:, :, part], ext.at[:, rows, columns], sems.at[j])
                for j, (k, part, rows, columns) in enumerate(pieces)
            ]
            for copy in copies:
                copy.start()
            cover[...] = jnp.zeros_like(cover)
            for copy in copies:
                copy.wait()

        @pl.when(i < info_ref[0])
        def _():
            row_at, col_at, row, col = corner_of(offs, i, full, size)
            total = jnp.zeros((1, size), F32)
            for part in range(2):
                block = shift_in(ext[part, pl.ds(row_at, size + 8), pl.ds(col_at, size + 128)], row, col)
                out[0, part] = block
                total = total + jnp.sum(block * block, axis=0, keepdims=True)
            here = lax.broadcasted_iota(jnp.int32, cover.shape, 0) == i // POS
            cover[...] += jnp.where(here, total, 0.0)

    return call(
        body,
        [offsets, info],
        [tile, *sides],
        [pl.BlockSpec(memory_space=pl.ANY)] * 7,
        [(slots, 2, size, size), (8, size)],
        [per_slot(2, size, size), whole(8, size)],
        slots,
        scratch=[pltpu.VMEM((2, full, full), F32), pltpu.SemaphoreType.DMA((len(pieces),))],
        flops=10**6,
        moved=8 * 10**6,
    )


def place_gradients(offsets, info, patches, after, edge):
    size = patches[0].shape[-1]
    full = edge + 2 * H
    n = len(patches)

    def body(offs, info_ref, *refs):
        patch_refs, (core, upper, lower, left_part, right_part, ext) = refs[:n], refs[n + len(after) :]
        i = pl.program_id(0)

        @pl.when(i == 0)
        def _():
            ext[...] = jnp.zeros_like(ext)

        for batch in range(n):

            @pl.when((i // POS == batch) & (i < info_ref[0]))
            def _():
                row_at, col_at, row, col = corner_of(offs, i, full, size)
                for part in range(2):
                    block = shift_out(patch_refs[batch][0, part], row, col)
                    ext[part, pl.ds(row_at, size + 8), pl.ds(col_at, size + 128)] += block

        @pl.when(i == n * POS - 1)
        def _():
            core[...] = ext[:, H : H + edge, H : H + edge]
            upper[...] = ext[:, :H]
            lower[...] = ext[:, H + edge :]
            left_part[...] = ext[:, H : H + edge, :H]
            right_part[...] = ext[:, H : H + edge, H + edge :]

    def spec(batch):
        return pl.BlockSpec((1, 2, size, size), lambda i, *_: (jnp.clip(i - batch * POS, 0, POS - 1), 0, 0, 0))

    shapes = [(2, edge, edge), (2, H, full), (2, H, full), (2, edge, H), (2, edge, H)]
    return call(
        body,
        [offsets, info],
        [*patches, *after],
        [spec(batch) for batch in range(n)] + [pl.BlockSpec(memory_space=pl.ANY)] * len(after),
        shapes,
        [whole(*shape) for shape in shapes],
        n * POS,
        scratch=[pltpu.VMEM((2, full, full), F32)],
        flops=10**6,
        moved=10**7,
    )


def side_borders(left_part, right_part, from_below, from_above, after):
    edge = left_part.shape[1]
    full = from_below.shape[2]

    def body(left_ref, right_ref, below, above, *rest):
        for ref, out, at in ((left_ref, rest[-2], 0), (right_ref, rest[-1], H + edge)):
            out[...] = ref[...]
            out[:, edge - H :] += below[:, :, at : at + H]
            out[:, :H] += above[:, :, at : at + H]

    return call(
        body,
        [],
        [left_part, right_part, from_below, from_above, *after],
        [whole(2, edge, H)] * 2 + [whole(2, H, full)] * 2 + [pl.BlockSpec(memory_space=pl.ANY)] * len(after),
        [(2, edge, H)] * 2,
        [whole(2, edge, H)] * 2,
        1,
        flops=10**5,
        moved=4 * 10**6,
    )


def call_in_vmem(body, info, operands, out_shapes, scratch=(), after=(), flops=0, moved=0):
    vmem = pl.BlockSpec(memory_space=pltpu.VMEM)
    return pl.pallas_call(
        body,
        out_shape=[pltpu.VMEM(s, F32) for s in out_shapes],
        in_specs=[pl.BlockSpec(memory_space=pltpu.SMEM)]
        + [vmem] * len(operands)
        + [pl.BlockSpec(memory_space=pl.ANY)] * len(after),
        out_specs=[vmem] * len(out_shapes),
        scratch_shapes=list(scratch),
        compiler_params=pltpu.CompilerParams(vmem_limit_bytes=VMEM_KERNEL),
        cost_estimate=pl.CostEstimate(flops=flops, bytes_accessed=moved, transcendentals=0),
    )(info, *[pltpu.with_memory_space_constraint(x, pltpu.VMEM) for x in operands], *after)


def turn_kernel(tables, info, patches, probes, roots, cover, batch):
    size = patches.shape[-1]
    h = size // 2
    rows = 4 * size
    extra = 0 if cover is None else cover.shape[0]

    def body(info_ref, t, patches_ref, roots_ref, *rest):
        p, rest = rest[:8], rest[8:]
        if extra:
            cover_ref, rest = rest[0], rest[1:]
        sent, keeps, gpatches, z, scratch = rest
        sent[:rows] = jnp.zeros((rows, size), F32)
        if extra:
            sent[rows:] = cover_ref[...]
        gpatches[...] = jnp.zeros_like(gpatches)
        for i in range(POS):
            slot = batch * POS + i
            patch, root = patches_ref.at[slot : slot + 1], roots_ref.at[slot : slot + 1]
            keep, gpatch = keeps.at[i : i + 1], gpatches.at[i : i + 1]

            @pl.when(slot < info_ref[0])
            def _():
                bits = [info_ref[2], info_ref[2], info_ref[1], info_ref[1]]
                totals = [0.0, 0.0]
                for m in range(4):
                    pair = illuminated(t, patch, (rows_of(p[2 * m], bits[m]), rows_of(p[2 * m + 1], bits[m])))
                    for e in range(2):
                        if m < 2:
                            z[i, m, e] = pair[e]
                        else:
                            scratch[m - 2, e] = pair[e]
                        totals[e] = totals[e] + power_of(pair[e])
                for e in range(2):
                    keep[0, e] = 1.0 - root[0, e] * lax.rsqrt(totals[e] + 0.1)
                for m in range(2, 4):
                    probe = (rows_of(p[2 * m], bits[m]), rows_of(p[2 * m + 1], bits[m]))
                    spectrum = (scratch[m - 2, 0], scratch[m - 2, 1])
                    gradients(t, patch, probe, spectrum, keep, sent, (m - 2) * 2 * size, bits[m], gpatch)

    return call_in_vmem(
        body,
        info,
        [tables, patches, roots, *probes] + ([cover] if extra else []),
        [(rows + extra, size), (POS, 2, size, h), (POS, 2, size, size), (POS, 2, 2, size, size)],
        scratch=[pltpu.VMEM((2, 2, size, size), F32)],
        flops=POS * 6 * 24 * size**3,
        moved=8 * 10**6,
    )


def back_kernel(tables, info, patches, probe, spectra, keeps, gpatches, batch, mode, start, after):
    size = patches.shape[-1]
    h = size // 2

    def body(info_ref, t, patches_ref, z, keeps_ref, g_in, p_re, p_im, *rest):
        quarters, g_out, pgrad = rest[-6:-2], rest[-2], rest[-1]
        if start:
            pgrad[...] = rest[0][: 2 * size]
        else:
            pgrad[...] = jnp.zeros_like(pgrad)
        g_out[...] = g_in[...]
        for i in range(POS):
            slot = batch * POS + i
            patch, keep, gpatch = patches_ref.at[slot : slot + 1], keeps_ref.at[i : i + 1], g_out.at[i : i + 1]

            @pl.when(slot < info_ref[0])
            def _():
                bit = info_ref[2]
                pair = (rows_of(p_re, bit), rows_of(p_im, bit))
                gradients(t, patch, pair, (z[i, mode, 0], z[i, mode, 1]), keep, pgrad, 0, bit, gpatch)

        for at, out in enumerate(quarters):
            out[...] = pgrad[at * h : (at + 1) * h]

    return call_in_vmem(
        body,
        info,
        [tables, patches, spectra, keeps, gpatches, *probe, *start],
        [(h, size)] * 4 + [(POS, 2, size, size)],
        scratch=[pltpu.VMEM((2 * size, size), F32)],
        after=after,
        flops=POS * 24 * size**3,
        moved=4 * 10**6,
    )


def probe_kernel(info, probes):
    size = probes[0].shape[0]

    def body(info_ref, *refs):
        p, (probe_out, top, power) = refs[:8], refs[8:]
        i = pl.program_id(0)
        for m in range(4):

            @pl.when(i == m)
            def _():
                bit = info_ref[2] if m < 2 else info_ref[1]
                re, im = rows_of(p[2 * m], bit), rows_of(p[2 * m + 1], bit)
                probe_out[0, 0], probe_out[0, 1] = re, im
                square = re * re + im * im
                power[...] = square if m == 0 else power[...] + square

        @pl.when(i == 3)
        def _():
            top[...] = jnp.broadcast_to(jnp.max(power[...], keepdims=True), top.shape)

    return call(
        body,
        [info],
        probes,
        [whole(size, size)] * 8,
        [(4, 2, size, size), (8, 128)],
        [pl.BlockSpec((1, 2, size, size), lambda i, info_ref: (info_ref[3 + i], 0, 0, 0)), whole(8, 128)],
        4,
        scratch=[pltpu.VMEM((size, size), F32)],
        flops=10**6,
        moved=4 * 10**6,
    )


def object_kernel(top, field, core, from_below, from_above):
    edge = field.shape[1]
    full = from_below.shape[2]
    steps = edge // H

    def body(top_ref, o, g, fb, fa, out):
        i = pl.program_id(0)
        step = (0.5 / top_ref[:1, :1])[None]
        out[...] = o[...] - step * g[...]

        @pl.when(i == steps - 1)
        def _():
            out[...] -= step * fb[:, :, H : H + edge]

        @pl.when(i == 0)
        def _():
            out[...] -= step * fa[:, :, H : H + edge]

    band = pl.BlockSpec((2, H, edge), lambda i: (0, i, 0))
    return call(
        body,
        [],
        [top, field, core, from_below, from_above],
        [whole(8, 128), band, band, whole(2, H, full), whole(2, H, full)],
        [field.shape],
        [band],
        steps,
        flops=10**6,
        moved=8 * 10**6,
    )[0]


def side_kernel(top, updated, from_right, from_left):
    edge = updated.shape[1]

    def body(top_ref, x, fr, fl, out):
        i = pl.program_id(0)
        step = (0.5 / top_ref[:1, :1])[None]

        @pl.when(i == 0)
        def _():
            out[...] = x[...] - step * fl[...]

        @pl.when(i == 1)
        def _():
            out[...] = x[...] - step * fr[...]

    side = pl.BlockSpec((2, edge, H), lambda i: (0, 0, i * (edge // H - 1)))
    return call(
        body,
        [],
        [top, updated, from_right, from_left],
        [whole(8, 128), side, whole(2, edge, H), whole(2, edge, H)],
        [updated.shape],
        [side],
        2,
        aliases={1: 0},
        flops=10**5,
        moved=4 * 10**6,
    )[0]


def flips(wide, narrow):
    bits = [(0, 2 << i) for i in range(1, narrow.bit_length() - 2)] + [
        (1 << i, 0) for i in range(1, wide.bit_length() - 1)
    ]

    def exchange(even, odd):
        pairs = []
        for w in range(wide):
            for n in range(narrow):
                dw, dn = odd if n & 1 else even
                pairs.append((w * narrow + n, (w ^ dw) * narrow + (n ^ dn)))
        return functools.partial(lax.ppermute, axis_name=AXES, perm=pairs)

    core = exchange((0, 1), (0, 1))
    first = exchange((0, 2), (1, 0))
    second = exchange((1, 0), (0, 2))
    return core, first, second, [exchange(a, b) for a, b in zip(bits, bits[::-1])]


def shifted(value, axis, steps):
    count = lax.axis_size(axis)
    leading, last = (max(0, -steps), min(count, count - steps))
    return lax.ppermute(value, axis, [(source, source + steps) for source in range(leading, last)])


def local(object_field, probe, patterns, offsets, counts):
    edge = object_field.shape[1]
    size = probe.shape[-1]
    slots = patterns.shape[2]
    h = size // 2
    wide, narrow = lax.axis_size("wide"), lax.axis_size("narrow")
    w, n = lax.axis_index("wide"), lax.axis_index("narrow")
    core, first, second, rest = flips(wide, narrow)
    offs = offsets.reshape(slots * 2)

    left_side = shifted(object_field[:, :, edge - H :], "wide", 1)
    right_side = shifted(object_field[:, :, :H], "wide", -1)
    top_side = shifted(object_field[:, edge - H :], "narrow", 1)
    bottom_side = shifted(object_field[:, :H], "narrow", -1)

    tables = jnp.asarray(dft_tables(size))
    order = np.concatenate([np.arange(0, size, 2), np.arange(1, size, 2)])
    pick = jnp.asarray(np.eye(size, dtype=np.float32)[order])
    roots = jnp.einsum("pj,sjk->spk", pick, jnp.sqrt(patterns[0, 0]), precision=lax.Precision.HIGHEST)
    roots = jnp.einsum("spk,qk->spq", roots, pick, precision=lax.Precision.HIGHEST)
    roots = roots.reshape(slots, size, 2, h).transpose(0, 2, 1, 3)

    c = n % 2
    bit_n, bit_w = (n // 2) % 2, w % 2
    b1 = jnp.where(c == 0, bit_n, bit_w)
    b2 = jnp.where(c == 0, bit_w, bit_n)
    ours, theirs = 2 * c, 2 * (1 - c)
    order_of = [ours + b1, ours + 1 - b1, theirs + b2, theirs + 1 - b2]
    info = jnp.stack([counts[0, 0], b1, b2, *order_of]).astype(jnp.int32)
    split_rows = probe.reshape(4, 2, 2, h, size)
    probes = []
    for m, bit in zip(order_of, (b2, b2, b1, b1)):
        for part in range(2):
            mine = lax.dynamic_slice(split_rows, (m, part, bit, 0, 0), (1, 1, 1, h, size))
            other = lax.dynamic_slice(split_rows, (m, part, 1 - bit, 0, 0), (1, 1, 1, h, size))
            probes.append(jnp.concatenate([mine.reshape(h, size), other.reshape(h, size)], 0))

    leading, last = cut_corners(left_side, right_side, (roots, *probes))
    top_corners = shifted(last, "narrow", 1)
    bottom_corners = shifted(leading, "narrow", -1)
    sides = (left_side, right_side, top_side, bottom_side, top_corners, bottom_corners)
    patches, cover = cut_patches(offs, info, object_field, sides, size, slots)

    patch_gradients = []
    for batch in range(BATCHES):
        extra = cover if batch == 0 else None

        def ride(x):
            return x if extra is None else jnp.concatenate([x, extra], 0)

        sent, keep, gpatch, z = turn_kernel(tables, info, patches, probes, roots, extra, batch)
        got = core(sent)
        *q, gpatch = back_kernel(tables, info, patches, probes[2:4], z, keep, gpatch, batch, 1, (), ())
        if extra is not None:
            extra = extra + got[4 * size :]
        sent_a = jnp.concatenate([q[0], q[1]], 0) + got[2 * size : 3 * size]
        sent_b = jnp.concatenate([q[2], q[3]], 0) + got[3 * size : 4 * size]
        got_a = first(ride(sent_a))
        got_b = first(sent_b)
        after = (sent_a, sent_b)
        *q, gpatch = back_kernel(tables, info, patches, probes[:2], z, keep, gpatch, batch, 0, (got,), after)
        patch_gradients.append(gpatch)
        sent_a = q[1] + got_a[h:size]
        sent_b = q[3] + got_b[h:]
        a = q[0] + got_a[:h]
        b = q[2] + got_b[:h]
        if extra is not None:
            extra = extra + got_a[size:]
        got_a = second(ride(sent_a))
        got_b = second(sent_b)
        a = a + got_a[:h]
        b = b + got_b
        if extra is not None:
            extra = extra + got_a[h:]
        if batch == BATCHES - 1:
            inside, upper, lower, left_part, right_part = place_gradients(offs, info, patch_gradients, (sent_a, sent_b), edge)
            from_below = shifted(upper, "narrow", -1)
            from_above = shifted(lower, "narrow", 1)
        for exchange in rest:
            got_a = exchange(ride(a))
            got_b = exchange(b)
            a = a + got_a[:h]
            b = b + got_b
            if extra is not None:
                extra = extra + got_a[h:]
        if extra is not None:
            scales = jnp.sum(extra, axis=1) / (size * size)
        a = probes[0][:h] - a / scales[batch]
        b = probes[1][:h] - b / scales[batch]
        shards = [a, b]
        a = jnp.concatenate([a, second(a)], 0)
        b = jnp.concatenate([b, second(b)], 0)
        own = [a, b, first(a), first(b)]
        probes = own + [core(x) for x in own]

    to_left, to_right = side_borders(left_part, right_part, from_below, from_above, shards)
    from_right = shifted(to_left, "wide", -1)
    from_left = shifted(to_right, "wide", 1)
    probe_new, top = probe_kernel(info, probes)
    updated = object_kernel(top, object_field, inside, from_below, from_above)
    return (side_kernel(top, updated, from_right, from_left), probe_new)


def solution(mesh):
    placed = (
        P(None, "narrow", "wide"),
        P(),
        P("narrow", "wide", None, None, None),
        P("narrow", "wide", None, None),
        P("narrow", "wide"),
    )
    return jax.shard_map(
        local,
        mesh=mesh,
        in_specs=placed,
        out_specs=(P(None, "narrow", "wide"), P()),
        check_vma=False,
    )
```
